256 devices in a mesh: zg: 4 (over x), gy: 64 (over y, z, core).
Axes of the slice: x: 4, y: 4, z: 8, core: 2. Of those that a mesh axis runs over, the one named last changes fastest.
Arguments:
- initial_heat_state: float32 [256, 256, 128], P('gy', 'zg'), may hold values from -3 to 3
- thermal_conductance_grid: float32 [256, 256, 128], P('gy', 'zg'), may hold values from 1 to 30
Outputs:
- advanced: float32 [256, 256, 128], P('gy', 'zg')
The draws below stay inside these ranges and needn't reach their ends.
All inputs are finite; a program needn't handle non-finite values.
Results may differ from the reference program's by a relative error of at most 0.004.
Values sent between devices are 32-bit elements; how exact they have to be, the bound alone decides.
No kernel may reach another device: no remote copies, remote signals or barrier semaphores. Data moves between devices by JAX's collectives and lax.ppermute only.
A program may use at most 64 MiB of HBM per device.

```python
import math
import jax
import jax.numpy as jnp
from jax import lax

NX = 128
NY = 256
NZ = 256


def draw_initial_heat_state(key, part):
    values = jnp.clip(jax.random.normal(key, (NY, NZ, NX), jnp.float32), -3.0, 3.0)
    return values


def block_scale(rng, extent, split, smallest, top_value):
    loudness = 1.0
    for position, blocks in split:
        heights = jax.random.uniform(jax.random.fold_in(jax.random.fold_in(rng, 6), position), (blocks,), jnp.float32, smallest / len(split), top_value / len(split))
        loudness = loudness * jnp.repeat(jnp.exp(heights), extent[position] // blocks).reshape((-1,) + (1,) * (len(extent) - 1 - position))
    return loudness


def setup_inputs(seed: int = 0) -> dict:
    key_list = jax.random.split(jax.random.key(seed), 3)
    initial_heat_state = draw_initial_heat_state(jax.random.fold_in(key_list[2], 71), 0)
    thermal_conductance_grid = jnp.clip(jnp.exp(math.log(30.0) - 3.4011974 * jax.random.uniform(key_list[1], (NY, NZ, NX), jnp.float32) ** block_scale(key_list[1], (NY, NZ, NX), ((0, 64), (1, 4)), -0.2, 0.2)), 1.0, 30.0)
    return dict(initial_heat_state=initial_heat_state, thermal_conductance_grid=thermal_conductance_grid)


mesh_courant_number = 300.0


def harmonic(left_side, right_side):
    return 2.0 * left_side * right_side / (left_side + right_side)


def face_pair(conduct):
    inner = harmonic(conduct[1:], conduct[:-1])
    border = jnp.zeros_like(conduct[:1])
    return jnp.concatenate([border, inner], 0), jnp.concatenate([inner, border], 0)


def add_interface_current(field, low_face, high_face):
    border = jnp.zeros_like(field[:1])
    before = jnp.concatenate([border, field[:-1]], 0)
    after = jnp.concatenate([field[1:], border], 0)
    return high_face * (after - field) - low_face * (field - before)


def thomas(below_band, middle, above_band, source):
    def forward(state_pair, entries):
        prev_upper, prev_value = state_pair
        low_entry, mid_entry, up_entry, src_entry = entries
        pivot_value = mid_entry - low_entry * prev_upper
        new_upper = up_entry / pivot_value
        new_value = (src_entry - low_entry * prev_value) / pivot_value
        return (new_upper, new_value), (new_upper, new_value)

    start_state = (jnp.zeros_like(middle[0]), jnp.zeros_like(middle[0]))
    ignored, (uppers, values) = lax.scan(forward, start_state, (below_band, middle, above_band, source))

    def backward(following, entries):
        upper_entry, value_entry = entries
        current = value_entry - upper_entry * following
        return current, current

    ignored_too, result = lax.scan(backward, jnp.zeros_like(middle[0]), (uppers, values), reverse=True)
    return result


def implicit_solve(source, low_face, high_face):
    return thomas(-mesh_courant_number * low_face, 1.0 + mesh_courant_number * (low_face + high_face),
                  -mesh_courant_number * high_face, source)


def reference(initial_heat_state, thermal_conductance_grid):
    south_interface, north_interface = face_pair(thermal_conductance_grid)
    second_difference_north = add_interface_current(initial_heat_state, south_interface, north_interface)
    cond_z = jnp.moveaxis(thermal_conductance_grid, 1, 0)
    bottom_interface, top_interface = face_pair(cond_z)
    second_difference_vertical = jnp.moveaxis(add_interface_current(jnp.moveaxis(initial_heat_state, 1, 0), bottom_interface, top_interface), 0, 1)
    first_axis_forcing = initial_heat_state + mesh_courant_number * second_difference_north + mesh_courant_number * second_difference_vertical
    low_x, high_x = face_pair(jnp.moveaxis(thermal_conductance_grid, 2, 0))
    first_pass = jnp.moveaxis(implicit_solve(jnp.moveaxis(first_axis_forcing, 2, 0), low_x, high_x), 0, 2)
    second_pass = implicit_solve(first_pass - mesh_courant_number * second_difference_north, south_interface, north_interface)
    source_z = jnp.moveaxis(second_pass - mesh_courant_number * second_difference_vertical, 1, 0)
    return jnp.moveaxis(implicit_solve(source_z, bottom_interface, top_interface), 0, 1)
```

```python
import jax
import jax.numpy as jnp
from jax import lax
from jax.experimental import pallas as pl
from jax.experimental.pallas import tpu as pltpu
from jax.sharding import PartitionSpec as P

mesh_courant_number = 300.0

NB, NZB, NX = 4, 64, 128
NGY, NZG = 64, 4
X_STRIDES = (1, 2, 4, 8, 16, 32, 64)
Z_STRIDES = (1, 2, 4, 8, 16, 32)
VALUES = 5


def face(k, q):
    return (2.0 * mesh_courant_number) * k * q / (k + q)


def shift(v, by, axis):
    return pltpu.roll(v, by % v.shape[axis], axis)


def rows_of(shape, axis):
    return lax.broadcasted_iota(jnp.int32, shape, axis)


def reduction_factors(leak, low, high, strides, axis, put):
    for j, s in enumerate(strides):
        inverse = 1.0 / (leak + low + high)
        from_low = low * shift(inverse, s, axis)
        from_high = high * shift(inverse, -s, axis)
        put(2 * j, from_low)
        put(2 * j + 1, from_high)
        leak = leak + from_low * shift(leak, s, axis) + from_high * shift(leak, -s, axis)
        low = from_low * shift(low, s, axis)
        high = from_high * shift(high, -s, axis)
    put(2 * len(strides), 1.0 / (leak + low + high))


def reduced_source(b, strides, axis, get):
    for j, s in enumerate(strides):
        b = b + get(2 * j) * shift(b, s, axis) + get(2 * j + 1) * shift(b, -s, axis)
    return b * get(2 * len(strides))


def inner_kernel(t_ref, k_ref, factors_ref, inner_ref, faces_ref):
    lane = rows_of((NZB, NX), 1)
    row = rows_of((NZB, NX), 0)
    flux_y = None
    for y in range(NB):
        k = k_ref[y]
        t = t_ref[y]
        low = jnp.where(lane > 0, face(k, shift(k, 1, 1)), 0.0)
        high = shift(low, -1, 1)
        flux = low * (t - shift(t, 1, 1))
        total = shift(flux, -1, 1) - flux
        face_z = jnp.where(row > 0, face(k, shift(k, 1, 0)), 0.0)
        flux = face_z * (t - shift(t, 1, 0))
        total = total + (shift(flux, -1, 0) - flux)
        if y > 0:
            total = total - flux_y
        if y < NB - 1:
            next_face = face(k_ref[y + 1], k)
            faces_ref[y] = next_face
            flux_y = next_face * (t_ref[y + 1] - t)
            total = total + flux_y
        inner_ref[y] = total
    half = NZB // 2
    for y in range(NB):
        for part in range(2):
            at = pl.ds(part * half, half)
            k = k_ref[y, at, :]
            low = jnp.where(rows_of((half, NX), 1) > 0, face(k, shift(k, 1, 1)), 0.0)
            high = shift(low, -1, 1)

            def put(j, v):
                factors_ref[j, y, at, :] = v

            reduction_factors(jnp.ones_like(k), low, high, X_STRIDES, 1, put)


def first_kernel(t_ref, k_ref, factors_ref, inner_ref, faces_ref, yp_ref, yn_ref, zp_ref, zn_ref,
                 bundle_ref, back_ref):
    gy = lax.axis_index("gy")
    zg = lax.axis_index("zg")
    has_south = jnp.where(gy > 0, 1.0, 0.0)
    has_north = jnp.where(gy < NGY - 1, 1.0, 0.0)
    has_below = jnp.where(zg > 0, 1.0, 0.0)
    has_above = jnp.where(zg < NZG - 1, 1.0, 0.0)
    row = rows_of((NZB, NX), 0)
    solved = []
    g4 = None
    for y in range(NB):
        b = inner_ref[y]
        t = t_ref[y]
        k = k_ref[y]
        if y == 0:
            b = b + face(k, yp_ref[1] * has_south) * (yp_ref[0] - t)
        if y == NB - 1:
            g4 = face(k, yn_ref[1] * has_north)
            b = b + g4 * (yn_ref[0] - t)
        below = face(k[:1], zp_ref[1, y:y + 1] * has_below) * (zp_ref[0, y:y + 1] - t[:1])
        above = face(k[NZB - 1:], zn_ref[1, y:y + 1] * has_above) * (zn_ref[0, y:y + 1] - t[NZB - 1:])
        b = b + jnp.where(row == 0, below, 0.0) + jnp.where(row == NZB - 1, above, 0.0)
        solved.append(reduced_source(b, X_STRIDES, 1, lambda j: factors_ref[j, y]))
    b0, b1, b2, b3 = solved
    g1, g2, g3 = faces_ref[0], faces_ref[1], faces_ref[2]
    i1 = 1.0 / (1.0 + g1 + g2)
    left, right = g1 * i1, g2 * i1
    source = b0 + left * b1
    b2 = b2 + right * b1
    leak = 1.0 + left
    m2 = 1.0 + right
    a2 = g1 * right
    i2 = 1.0 / (m2 + a2 + g3)
    left, right = a2 * i2, g3 * i2
    source = source + left * b2
    b3 = b3 + right * b2
    leak = leak + left * m2
    m3 = 1.0 + right * m2
    a3 = a2 * right
    i3 = 1.0 / (m3 + a3 + g4)
    left, right = a3 * i3, g4 * i3
    put = lambda v, x: pltpu.store(bundle_ref.at[pl.ds(v, NZB, stride=VALUES), :], x)
    put(0, leak + left * m3)
    put(1, right * m3)
    put(2, a3 * right)
    put(3, source + left * b3)
    put(4, right * b3)
    beta, lam, rho = b3 * i3, left, right
    back_ref[0, 2], back_ref[1, 2], back_ref[2, 2] = beta, lam, rho
    beta, lam, rho = (b2 + g3 * beta) * i2, (a2 + g3 * lam) * i2, g3 * rho * i2
    back_ref[0, 1], back_ref[1, 1], back_ref[2, 1] = beta, lam, rho
    beta, lam, rho = (b1 + g2 * beta) * i1, (g1 + g2 * lam) * i1, g2 * rho * i1
    back_ref[0, 0], back_ref[1, 0], back_ref[2, 0] = beta, lam, rho


def column_kernel(bundle_ref, out_ref):
    get = lambda v: bundle_ref[pl.ds(v, NGY, stride=VALUES), :]
    leak = get(0) + shift(get(1), 1, 0)
    high = get(2)
    low = shift(high, 1, 0)
    b = get(3) + shift(get(4), 1, 0)
    for s in (1, 2, 4, 8, 16, 32):
        inverse = 1.0 / (leak + low + high)
        from_low = low * shift(inverse, s, 0)
        from_high = high * shift(inverse, -s, 0)
        leak = leak + from_low * shift(leak, s, 0) + from_high * shift(leak, -s, 0)
        b = b + from_low * shift(b, s, 0) + from_high * shift(b, -s, 0)
        low = from_low * shift(low, s, 0)
        high = from_high * shift(high, -s, 0)
    own = b / (leak + low + high)
    out_ref[pl.ds(0, NGY, stride=2), :] = own
    out_ref[pl.ds(1, NGY, stride=2), :] = shift(own, -1, 0)


def z_kernel(k_ref, zn_ref, factors_ref, spikes_ref, coeffs_ref):
    zg = lax.axis_index("zg")
    has_above = jnp.where(zg < NZG - 1, 1.0, 0.0)
    row = rows_of((NZB, NX), 0)
    for y in range(NB):
        k = k_ref[y]
        g = face(k, shift(k, 1, 0))
        top = face(k[NZB - 1:], zn_ref[1, y:y + 1] * has_above)
        low = jnp.where(row > 1, g, 0.0)
        high = shift(low, -1, 0)
        at_first = jnp.where(row == 1, g, 0.0)
        at_last = jnp.where(row == NZB - 1, top, 0.0)

        def put(j, v):
            factors_ref[j, y] = v

        reduction_factors(1.0 + at_first + at_last, low, high, Z_STRIDES, 0, put)
        get = lambda j: factors_ref[j, y]
        lam = reduced_source(at_first, Z_STRIDES, 0, get)
        lam = jnp.where(row == 0, 1.0, lam)
        rho = reduced_source(at_last, Z_STRIDES, 0, get)
        spikes_ref[0, y] = lam
        spikes_ref[1, y] = rho
        coeffs_ref[0, y:y + 1] = jnp.sum(lam, axis=0, keepdims=True)
        coeffs_ref[1, y:y + 1] = jnp.sum(rho, axis=0, keepdims=True)
        coeffs_ref[2, y:y + 1] = lam[NZB - 1:] * top


def second_kernel(ends_ref, back_ref, spikes_ref, second_ref, sums_ref):
    own = ends_ref[pl.ds(0, NZB, stride=2), :]
    following = ends_ref[pl.ds(1, NZB, stride=2), :]
    for y in range(NB):
        if y == 0:
            u = own
        else:
            u = back_ref[0, y - 1] + back_ref[1, y - 1] * own + back_ref[2, y - 1] * following
        second_ref[y] = u
        sums_ref[0, y:y + 1] = jnp.sum(spikes_ref[0, y] * u, axis=0, keepdims=True)
        sums_ref[1, y:y + 1] = jnp.sum(spikes_ref[1, y] * u, axis=0, keepdims=True)


def local_z_kernel(second_ref, factors_ref, t_ref, out_ref):
    row = rows_of((NZB, NX), 0)
    for y in range(NB):
        b = jnp.where(row == 0, 0.0, second_ref[y])
        out_ref[y] = t_ref[y] + reduced_source(b, Z_STRIDES, 0, lambda j: factors_ref[j, y])


def last_kernel(local_ref, spikes_ref, c0_ref, c1_ref, c2_ref, c3_ref, s0_ref, s1_ref, s2_ref, s3_ref,
                out_ref, coeffs, sums, ends):
    zg = lax.axis_index("zg")
    for j, (c_ref, s_ref) in enumerate(((c0_ref, s0_ref), (c1_ref, s1_ref), (c2_ref, s2_ref), (c3_ref, s3_ref))):
        at = lax.rem(zg + (NZG - j), NZG)
        coeffs[at] = c_ref[...]
        sums[at] = s_ref[...]
    inverses, sources = [], []
    leak, source = coeffs[0, 0], sums[0, 0]
    for d in range(NZG):
        couple = coeffs[d, 2]
        inverse = 1.0 / (leak + couple)
        inverses.append(inverse)
        sources.append(source)
        if d + 1 < NZG:
            passed = couple * inverse
            leak = coeffs[d + 1, 0] + coeffs[d, 1] + passed * leak
            source = sums[d + 1, 0] + sums[d, 1] + passed * source
    value = jnp.zeros_like(source)
    ends[NZG] = value
    for d in reversed(range(NZG)):
        value = (sources[d] + coeffs[d, 2] * value) * inverses[d]
        ends[d] = value
    own = ends[zg]
    following = ends[zg + 1]
    for y in range(NB):
        out_ref[y] = (local_ref[y] + spikes_ref[0, y] * own[y:y + 1] + spikes_ref[1, y] * following[y:y + 1])


def call(kernel, name, outs, args, scratch=(), cost=2000000):
    shapes = [jax.ShapeDtypeStruct(o, jnp.float32) for o in outs]
    vmem = pl.BlockSpec(memory_space=pltpu.VMEM)
    return pl.pallas_call(
        kernel,
        name=name,
        out_shape=shapes,
        in_specs=[vmem] * len(args),
        out_specs=[vmem] * len(outs),
        scratch_shapes=[pltpu.VMEM(s, jnp.float32) for s in scratch],
        cost_estimate=pl.CostEstimate(flops=cost, bytes_accessed=cost, transcendentals=0),
        compiler_params=pltpu.CompilerParams(vmem_limit_bytes=24 * 1024 * 1024),
    )(*args)


def around(x, axis, by):
    count = lax.axis_size(axis)
    return lax.ppermute(x, axis, [(i, (i + by) % count) for i in range(count)])


def shards(t, k):
    joined = jnp.stack([t, k])
    yp = around(joined[:, NB - 1], "gy", 1)
    yn = around(joined[:, 0], "gy", -1)
    zp = around(joined[:, :, NZB - 1], "zg", 1)
    zn = around(joined[:, :, 0], "zg", -1)
    block = (NB, NZB, NX)
    factors, inner, faces = call(
        inner_kernel, "inner", [(2 * len(X_STRIDES) + 1,) + block, block, (NB - 1, NZB, NX)], [t, k])
    bundle, back = call(
        first_kernel, "first", [(NZB * VALUES, NX), (3, NB - 1, NZB, NX)],
        [t, k, factors, inner, faces, yp, yn, zp, zn])
    columns = lax.all_to_all(bundle, "gy", split_axis=0, concat_axis=0, tiled=True)
    z_factors, spikes, coeffs = call(
        z_kernel, "z", [(2 * len(Z_STRIDES) + 1,) + block, (2,) + block, (3, NB, NX)], [k, zn])
    coeffs = [coeffs] + [around(coeffs, "zg", j) for j in range(1, NZG)]
    (ends,) = call(column_kernel, "column", [(2 * NGY, NX)], [columns])
    ends = lax.all_to_all(ends, "gy", split_axis=0, concat_axis=0, tiled=True)
    second, sums = call(second_kernel, "second", [block, (2, NB, NX)], [ends, back, spikes])
    sums = [sums] + [around(sums, "zg", j) for j in range(1, NZG)]
    (local,) = call(local_z_kernel, "local_z", [block], [second, z_factors, t])
    (out,) = call(last_kernel, "last", [block], [local, spikes] + coeffs + sums,
                  scratch=((NZG, 3, NB, NX), (NZG, 2, NB, NX), (NZG + 1, NB, NX)))
    return out


def solution(mesh):
    return jax.shard_map(
        shards,
        mesh=mesh,
        in_specs=(P("gy", "zg", None), P("gy", "zg", None)),
        out_specs=P("gy", "zg", None),
        check_vma=False,
    )
```

```python
import jax
import jax.numpy as jnp
from jax import lax
from jax.experimental import pallas as pl
from jax.experimental.pallas import tpu as pltpu
from jax.sharding import PartitionSpec as P

mesh_courant_number = 300.0

NB, NZB, NX = 4, 64, 128
NGY, NZG = 64, 4
X_STRIDES = (1, 2, 4, 8, 16, 32, 64)
Z_STRIDES = (1, 2, 4, 8, 16, 32)
VALUES = 5


def face(k, q):
    return (2.0 * mesh_courant_number) * k * q / (k + q)


def shift(v, by, axis):
    return pltpu.roll(v, by % v.shape[axis], axis)


def rows_of(shape, axis):
    return lax.broadcasted_iota(jnp.int32, shape, axis)


def reduction_factors(leak, low, high, strides, axis, put):
    for j, s in enumerate(strides):
        inverse = 1.0 / (leak + low + high)
        from_low = low * shift(inverse, s, axis)
        from_high = high * shift(inverse, -s, axis)
        put(2 * j, from_low)
        put(2 * j + 1, from_high)
        leak = leak + from_low * shift(leak, s, axis) + from_high * shift(leak, -s, axis)
        low = from_low * shift(low, s, axis)
        high = from_high * shift(high, -s, axis)
    put(2 * len(strides), 1.0 / (leak + low + high))


def reduced_source(b, strides, axis, get):
    for j, s in enumerate(strides):
        b = b + get(2 * j) * shift(b, s, axis) + get(2 * j + 1) * shift(b, -s, axis)
    return b * get(2 * len(strides))


def load_kernel(t_hbm, k_hbm, t_ref, k_ref, yp_ref, yn_ref, zp_ref, zn_ref, sems):
    copies = [pltpu.make_async_copy(t_hbm, t_ref, sems.at[0]), pltpu.make_async_copy(k_hbm, k_ref, sems.at[1])]
    for copy in copies:
        copy.start()
    for j, (copy, ref) in enumerate(zip(copies, (t_ref, k_ref))):
        copy.wait()
        yp_ref[j] = ref[NB - 1]
        yn_ref[j] = ref[0]
        for y in range(NB):
            zp_ref[j, y:y + 1] = ref[y, NZB - 1:]
            zn_ref[j, y:y + 1] = ref[y, :1]


def pair(ref, h):
    return ref[2 * h:2 * h + 2].reshape(2 * NZB, NX).T


def inner_kernel(t_ref, k_ref, factors_ref, inner_ref, faces_ref):
    lane = rows_of((NZB, NX), 1)
    row = rows_of((NZB, NX), 0)
    flux_y = None
    for y in range(NB):
        k = k_ref[y]
        t = t_ref[y]
        low = jnp.where(lane > 0, face(k, shift(k, 1, 1)), 0.0)
        flux = low * (t - shift(t, 1, 1))
        total = shift(flux, -1, 1) - flux
        face_z = jnp.where(row > 0, face(k, shift(k, 1, 0)), 0.0)
        flux = face_z * (t - shift(t, 1, 0))
        total = total + (shift(flux, -1, 0) - flux)
        if y > 0:
            total = total - flux_y
        if y < NB - 1:
            next_face = face(k_ref[y + 1], k)
            faces_ref[y] = next_face
            flux_y = next_face * (t_ref[y + 1] - t)
            total = total + flux_y
        inner_ref[y] = total
    for h in range(NB // 2):
        k = pair(k_ref, h)
        low = jnp.where(rows_of(k.shape, 0) > 0, face(k, shift(k, 1, 0)), 0.0)

        def put(j, v):
            factors_ref[j, h] = v

        reduction_factors(jnp.ones_like(k), low, shift(low, -1, 0), X_STRIDES, 0, put)


def first_kernel(t_ref, k_ref, factors_ref, inner_ref, faces_ref, yp_ref, yn_ref, zp_ref, zn_ref,
                 bundle_ref, back_ref):
    gy = lax.axis_index("gy")
    zg = lax.axis_index("zg")
    has_south = jnp.where(gy > 0, 1.0, 0.0)
    has_north = jnp.where(gy < NGY - 1, 1.0, 0.0)
    has_below = jnp.where(zg > 0, 1.0, 0.0)
    has_above = jnp.where(zg < NZG - 1, 1.0, 0.0)
    row = rows_of((NZB, NX), 0)
    sources = []
    g4 = None
    for y in range(NB):
        b = inner_ref[y]
        t = t_ref[y]
        k = k_ref[y]
        if y == 0:
            b = b + face(k, yp_ref[1] * has_south) * (yp_ref[0] - t)
        if y == NB - 1:
            g4 = face(k, yn_ref[1] * has_north)
            b = b + g4 * (yn_ref[0] - t)
        below = face(k[:1], zp_ref[1, y:y + 1] * has_below) * (zp_ref[0, y:y + 1] - t[:1])
        above = face(k[NZB - 1:], zn_ref[1, y:y + 1] * has_above) * (zn_ref[0, y:y + 1] - t[NZB - 1:])
        b = b + jnp.where(row == 0, below, 0.0) + jnp.where(row == NZB - 1, above, 0.0)
        sources.append(b)
    solved = []
    for h in range(NB // 2):
        b = jnp.concatenate(sources[2 * h:2 * h + 2], axis=0).T
        b = reduced_source(b, X_STRIDES, 0, lambda j: factors_ref[j, h]).T
        solved += [b[:NZB], b[NZB:]]
    b0, b1, b2, b3 = solved
    g1, g2, g3 = faces_ref[0], faces_ref[1], faces_ref[2]
    i1 = 1.0 / (1.0 + g1 + g2)
    left, right = g1 * i1, g2 * i1
    source = b0 + left * b1
    b2 = b2 + right * b1
    leak = 1.0 + left
    m2 = 1.0 + right
    a2 = g1 * right
    i2 = 1.0 / (m2 + a2 + g3)
    left, right = a2 * i2, g3 * i2
    source = source + left * b2
    b3 = b3 + right * b2
    leak = leak + left * m2
    m3 = 1.0 + right * m2
    a3 = a2 * right
    i3 = 1.0 / (m3 + a3 + g4)
    left, right = a3 * i3, g4 * i3
    put = lambda v, x: pltpu.store(bundle_ref.at[pl.ds(v, NZB, stride=VALUES), :], x)
    put(0, leak + left * m3)
    put(1, right * m3)
    put(2, a3 * right)
    put(3, source + left * b3)
    put(4, right * b3)
    beta, lam, rho = b3 * i3, left, right
    back_ref[0, 2], back_ref[1, 2], back_ref[2, 2] = beta, lam, rho
    beta, lam, rho = (b2 + g3 * beta) * i2, (a2 + g3 * lam) * i2, g3 * rho * i2
    back_ref[0, 1], back_ref[1, 1], back_ref[2, 1] = beta, lam, rho
    beta, lam, rho = (b1 + g2 * beta) * i1, (g1 + g2 * lam) * i1, g2 * rho * i1
    back_ref[0, 0], back_ref[1, 0], back_ref[2, 0] = beta, lam, rho


def column_kernel(bundle_ref, out_ref):
    get = lambda v: bundle_ref[pl.ds(v, NGY, stride=VALUES), :]
    leak = get(0) + shift(get(1), 1, 0)
    high = get(2)
    low = shift(high, 1, 0)
    b = get(3) + shift(get(4), 1, 0)
    for s in (1, 2, 4, 8, 16, 32):
        inverse = 1.0 / (leak + low + high)
        from_low = low * shift(inverse, s, 0)
        from_high = high * shift(inverse, -s, 0)
        leak = leak + from_low * shift(leak, s, 0) + from_high * shift(leak, -s, 0)
        b = b + from_low * shift(b, s, 0) + from_high * shift(b, -s, 0)
        low = from_low * shift(low, s, 0)
        high = from_high * shift(high, -s, 0)
    own = b / (leak + low + high)
    out_ref[pl.ds(0, NGY, stride=2), :] = own
    out_ref[pl.ds(1, NGY, stride=2), :] = shift(own, -1, 0)


def z_kernel(k_ref, zn_ref, factors_ref, spikes_ref, coeffs_ref):
    zg = lax.axis_index("zg")
    has_above = jnp.where(zg < NZG - 1, 1.0, 0.0)
    row = rows_of((NZB, NX), 0)
    for y in range(NB):
        k = k_ref[y]
        g = face(k, shift(k, 1, 0))
        top = face(k[NZB - 1:], zn_ref[1, y:y + 1] * has_above)
        low = jnp.where(row > 1, g, 0.0)
        high = shift(low, -1, 0)
        at_first = jnp.where(row == 1, g, 0.0)
        at_last = jnp.where(row == NZB - 1, top, 0.0)

        def put(j, v):
            factors_ref[j, y] = v

        reduction_factors(1.0 + at_first + at_last, low, high, Z_STRIDES, 0, put)
        get = lambda j: factors_ref[j, y]
        lam = reduced_source(at_first, Z_STRIDES, 0, get)
        lam = jnp.where(row == 0, 1.0, lam)
        rho = reduced_source(at_last, Z_STRIDES, 0, get)
        spikes_ref[0, y] = lam
        spikes_ref[1, y] = rho
        coeffs_ref[0, y:y + 1] = jnp.sum(lam, axis=0, keepdims=True)
        coeffs_ref[1, y:y + 1] = jnp.sum(rho, axis=0, keepdims=True)
        coeffs_ref[2, y:y + 1] = lam[NZB - 1:] * top


def second_kernel(ends_ref, back_ref, spikes_ref, coeffs_ref, second_ref, sums_ref):
    own = ends_ref[pl.ds(0, NZB, stride=2), :]
    following = ends_ref[pl.ds(1, NZB, stride=2), :]
    sums_ref[:3] = coeffs_ref[...]
    for y in range(NB):
        if y == 0:
            u = own
        else:
            u = back_ref[0, y - 1] + back_ref[1, y - 1] * own + back_ref[2, y - 1] * following
        second_ref[y] = u
        sums_ref[3, y:y + 1] = jnp.sum(spikes_ref[0, y] * u, axis=0, keepdims=True)
        sums_ref[4, y:y + 1] = jnp.sum(spikes_ref[1, y] * u, axis=0, keepdims=True)


def local_z_kernel(second_ref, factors_ref, t_ref, out_ref):
    row = rows_of((NZB, NX), 0)
    for y in range(NB):
        b = jnp.where(row == 0, 0.0, second_ref[y])
        out_ref[y] = t_ref[y] + reduced_source(b, Z_STRIDES, 0, lambda j: factors_ref[j, y])


def last_kernel(local_ref, spikes_ref, e0_ref, e1_ref, e2_ref, e3_ref, out_ref, line, ends):
    zg = lax.axis_index("zg")
    for j, e_ref in enumerate((e0_ref, e1_ref, e2_ref, e3_ref)):
        line[lax.rem(zg + (NZG - j), NZG)] = e_ref[...]
    inverses, sources = [], []
    leak, source = line[0, 0], line[0, 3]
    for d in range(NZG):
        couple = line[d, 2]
        inverse = 1.0 / (leak + couple)
        inverses.append(inverse)
        sources.append(source)
        if d + 1 < NZG:
            passed = couple * inverse
            leak = line[d + 1, 0] + line[d, 1] + passed * leak
            source = line[d + 1, 3] + line[d, 4] + passed * source
    value = jnp.zeros_like(source)
    ends[NZG] = value
    for d in reversed(range(NZG)):
        value = (sources[d] + line[d, 2] * value) * inverses[d]
        ends[d] = value
    own = ends[zg]
    following = ends[zg + 1]
    for y in range(NB):
        out_ref[y] = local_ref[y] + spikes_ref[0, y] * own[y:y + 1] + spikes_ref[1, y] * following[y:y + 1]


def call(kernel, name, outs, args, scratch=(), cost=2000000, whole=False):
    shapes = [jax.ShapeDtypeStruct(o, jnp.float32) for o in outs]
    vmem = pl.BlockSpec(memory_space=pltpu.VMEM)
    return pl.pallas_call(
        kernel,
        name=name,
        out_shape=shapes,
        in_specs=[pl.BlockSpec(memory_space=pltpu.HBM)] * len(args) if whole else [vmem] * len(args),
        out_specs=[vmem] * len(outs),
        scratch_shapes=scratch,
        cost_estimate=pl.CostEstimate(flops=cost, bytes_accessed=cost, transcendentals=0),
        compiler_params=pltpu.CompilerParams(vmem_limit_bytes=(54816 if whole else 24576) * 1024),
    )(*args)


def around(x, axis, by):
    count = lax.axis_size(axis)
    return lax.ppermute(x, axis, [(i, (i + by) % count) for i in range(count)])


def shards(t, k):
    block = (NB, NZB, NX)
    t, k, yp, yn, zp, zn = call(
        load_kernel, "load", [block, block, (2, NZB, NX), (2, NZB, NX), (2, NB, NX), (2, NB, NX)], [t, k],
        scratch=[pltpu.SemaphoreType.DMA((2,))], whole=True)
    yp = around(yp, "gy", 1)
    yn = around(yn, "gy", -1)
    zp = around(zp, "zg", 1)
    zn = around(zn, "zg", -1)
    factors, inner, faces = call(
        inner_kernel, "inner",
        [(2 * len(X_STRIDES) + 1, NB // 2, NX, 2 * NZB), block, (NB - 1, NZB, NX)], [t, k])
    bundle, back = call(
        first_kernel, "first", [(NZB * VALUES, NX), (3, NB - 1, NZB, NX)],
        [t, k, factors, inner, faces, yp, yn, zp, zn])
    columns = lax.all_to_all(bundle.reshape(NZB * VALUES, 1, NX), "gy", split_axis=0, concat_axis=0, tiled=True)
    z_factors, spikes, coeffs = call(
        z_kernel, "z", [(2 * len(Z_STRIDES) + 1,) + block, (2,) + block, (3, NB, NX)], [k, zn])
    (ends,) = call(column_kernel, "column", [(2 * NGY, NX)], [columns.reshape(NGY * VALUES, NX)])
    ends = lax.all_to_all(ends, "gy", split_axis=0, concat_axis=0, tiled=True)
    second, sums = call(second_kernel, "second", [block, (5, NB, NX)], [ends, back, spikes, coeffs])
    sums = [sums] + [around(sums, "zg", j) for j in range(1, NZG)]
    (local,) = call(local_z_kernel, "local_z", [block], [second, z_factors, t])
    (out,) = call(last_kernel, "last", [block], [local, spikes] + sums,
                  scratch=[pltpu.VMEM((NZG, 5, NB, NX), jnp.float32), pltpu.VMEM((NZG + 1, NB, NX), jnp.float32)])
    return out


def solution(mesh):
    return jax.shard_map(
        shards,
        mesh=mesh,
        in_specs=(P("gy", "zg", None), P("gy", "zg", None)),
        out_specs=P("gy", "zg", None),
        check_vma=False,
    )
```

```python
import jax
import jax.numpy as jnp
from jax import lax
from jax.experimental import pallas as pl
from jax.experimental.pallas import tpu as pltpu
from jax.sharding import PartitionSpec as P

mesh_courant_number = 300.0

NB, NZB, NX = 4, 64, 128
NGY, NZG = 64, 4
X_STRIDES = (1, 2, 4, 8, 16, 32, 64)
Z_STRIDES = (1, 2, 4, 8, 16, 32)
VALUES = 5


def face(k, q):
    return (2.0 * mesh_courant_number) * k * q / (k + q)


def shift(v, by, axis):
    return pltpu.roll(v, by % v.shape[axis], axis)


def rows_of(shape, axis):
    return lax.broadcasted_iota(jnp.int32, shape, axis)


def reduction_factors(leak, low, high, strides, axis, put):
    for j, s in enumerate(strides):
        inverse = 1.0 / (leak + low + high)
        from_low = low * shift(inverse, s, axis)
        from_high = high * shift(inverse, -s, axis)
        put(2 * j, from_low)
        put(2 * j + 1, from_high)
        leak = leak + from_low * shift(leak, s, axis) + from_high * shift(leak, -s, axis)
        low = from_low * shift(low, s, axis)
        high = from_high * shift(high, -s, axis)
    put(2 * len(strides), 1.0 / (leak + low + high))


def reduced_source(b, strides, axis, get):
    for j, s in enumerate(strides):
        b = b + get(2 * j) * shift(b, s, axis) + get(2 * j + 1) * shift(b, -s, axis)
    return b * get(2 * len(strides))


def load_kernel(t_hbm, k_hbm, t_ref, k_ref, yp_ref, yn_ref, zp_ref, zn_ref, sems):
    copies = [pltpu.make_async_copy(t_hbm, t_ref, sems.at[0]), pltpu.make_async_copy(k_hbm, k_ref, sems.at[1])]
    for copy in copies:
        copy.start()
    for j, (copy, ref) in enumerate(zip(copies, (t_ref, k_ref))):
        copy.wait()
        yp_ref[j] = ref[NB - 1]
        yn_ref[j] = ref[0]
        for y in range(NB):
            zp_ref[j, y:y + 1] = ref[y, NZB - 1:]
            zn_ref[j, y:y + 1] = ref[y, :1]


def pair(ref, h):
    return ref[2 * h:2 * h + 2].reshape(2 * NZB, NX).T


def z_part(k_ref, factors_ref, spikes_ref, coeffs_ref):
    row = rows_of((NZB, NX), 0)
    for y in range(NB):
        k = k_ref[y]
        g = face(k, shift(k, 1, 0))
        low = jnp.where((row > 1) & (row < NZB - 1), g, 0.0)
        at_first = jnp.where(row == 1, g, 0.0)
        at_last = jnp.where(row == NZB - 2, shift(g, -1, 0), 0.0)

        def put(j, v):
            factors_ref[j, y] = v

        reduction_factors(1.0 + at_first + at_last, low, shift(low, -1, 0), Z_STRIDES, 0, put)
        get = lambda j: factors_ref[j, y]
        lam = reduced_source(at_first, Z_STRIDES, 0, get)
        rho = reduced_source(at_last, Z_STRIDES, 0, get)
        coeffs_ref[2, y:y + 1] = g[NZB - 1:] * lam[NZB - 2:NZB - 1]
        lam = jnp.where(row == 0, 1.0, lam)
        rho = jnp.where(row == NZB - 1, 1.0, rho)
        spikes_ref[0, y] = lam
        spikes_ref[1, y] = rho
        coeffs_ref[0, y:y + 1] = jnp.sum(lam, axis=0, keepdims=True)
        coeffs_ref[1, y:y + 1] = jnp.sum(rho, axis=0, keepdims=True)


def inner_kernel(t_ref, k_ref, factors_ref, inner_ref, faces_ref, z_factors_ref, spikes_ref, coeffs_ref):
    lane = rows_of((NZB, NX), 1)
    row = rows_of((NZB, NX), 0)
    flux_y = None
    for y in range(NB):
        k = k_ref[y]
        t = t_ref[y]
        low = jnp.where(lane > 0, face(k, shift(k, 1, 1)), 0.0)
        flux = low * (t - shift(t, 1, 1))
        total = shift(flux, -1, 1) - flux
        face_z = jnp.where(row > 0, face(k, shift(k, 1, 0)), 0.0)
        flux = face_z * (t - shift(t, 1, 0))
        total = total + (shift(flux, -1, 0) - flux)
        if y > 0:
            total = total - flux_y
        if y < NB - 1:
            next_face = face(k_ref[y + 1], k)
            faces_ref[y] = next_face
            flux_y = next_face * (t_ref[y + 1] - t)
            total = total + flux_y
        inner_ref[y] = total
    for h in range(NB // 2):
        k = pair(k_ref, h)
        low = jnp.where(rows_of(k.shape, 0) > 0, face(k, shift(k, 1, 0)), 0.0)

        def put(j, v):
            factors_ref[j, h] = v

        reduction_factors(jnp.ones_like(k), low, shift(low, -1, 0), X_STRIDES, 0, put)
    z_part(k_ref, z_factors_ref, spikes_ref, coeffs_ref)


def first_kernel(t_ref, k_ref, factors_ref, inner_ref, faces_ref, yp_ref, yn_ref, zp_ref, zn_ref,
                 bundle_ref, back_ref, top_ref):
    gy = lax.axis_index("gy")
    zg = lax.axis_index("zg")
    has_south = jnp.where(gy > 0, 1.0, 0.0)
    has_north = jnp.where(gy < NGY - 1, 1.0, 0.0)
    has_below = jnp.where(zg > 0, 1.0, 0.0)
    has_above = jnp.where(zg < NZG - 1, 1.0, 0.0)
    row = rows_of((NZB, NX), 0)
    sources = []
    g4 = None
    for y in range(NB):
        b = inner_ref[y]
        t = t_ref[y]
        k = k_ref[y]
        if y == 0:
            b = b + face(k, yp_ref[1] * has_south) * (yp_ref[0] - t)
        if y == NB - 1:
            g4 = face(k, yn_ref[1] * has_north)
            b = b + g4 * (yn_ref[0] - t)
        below = face(k[:1], zp_ref[1, y:y + 1] * has_below) * (zp_ref[0, y:y + 1] - t[:1])
        top = face(k[NZB - 1:], zn_ref[1, y:y + 1] * has_above)
        top_ref[y:y + 1] = top
        above = top * (zn_ref[0, y:y + 1] - t[NZB - 1:])
        b = b + jnp.where(row == 0, below, 0.0) + jnp.where(row == NZB - 1, above, 0.0)
        sources.append(b)
    solved = []
    for h in range(NB // 2):
        b = jnp.concatenate(sources[2 * h:2 * h + 2], axis=0).T
        b = reduced_source(b, X_STRIDES, 0, lambda j: factors_ref[j, h]).T
        solved += [b[:NZB], b[NZB:]]
    b0, b1, b2, b3 = solved
    g1, g2, g3 = faces_ref[0], faces_ref[1], faces_ref[2]
    i1 = 1.0 / (1.0 + g1 + g2)
    left, right = g1 * i1, g2 * i1
    source = b0 + left * b1
    b2 = b2 + right * b1
    leak = 1.0 + left
    m2 = 1.0 + right
    a2 = g1 * right
    i2 = 1.0 / (m2 + a2 + g3)
    left, right = a2 * i2, g3 * i2
    source = source + left * b2
    b3 = b3 + right * b2
    leak = leak + left * m2
    m3 = 1.0 + right * m2
    a3 = a2 * right
    i3 = 1.0 / (m3 + a3 + g4)
    left, right = a3 * i3, g4 * i3
    put = lambda v, x: pltpu.store(bundle_ref.at[pl.ds(v, NZB, stride=VALUES), :], x)
    put(0, leak + left * m3)
    put(1, right * m3)
    put(2, a3 * right)
    put(3, source + left * b3)
    put(4, right * b3)
    beta, lam, rho = b3 * i3, left, right
    back_ref[0, 2], back_ref[1, 2], back_ref[2, 2] = beta, lam, rho
    beta, lam, rho = (b2 + g3 * beta) * i2, (a2 + g3 * lam) * i2, g3 * rho * i2
    back_ref[0, 1], back_ref[1, 1], back_ref[2, 1] = beta, lam, rho
    beta, lam, rho = (b1 + g2 * beta) * i1, (g1 + g2 * lam) * i1, g2 * rho * i1
    back_ref[0, 0], back_ref[1, 0], back_ref[2, 0] = beta, lam, rho


def column_kernel(bundle_ref, out_ref):
    get = lambda v: bundle_ref[pl.ds(v, NGY, stride=VALUES), :]
    leak = get(0) + shift(get(1), 1, 0)
    high = get(2)
    low = shift(high, 1, 0)
    b = get(3) + shift(get(4), 1, 0)
    for s in (1, 2, 4, 8, 16, 32):
        inverse = 1.0 / (leak + low + high)
        from_low = low * shift(inverse, s, 0)
        from_high = high * shift(inverse, -s, 0)
        leak = leak + from_low * shift(leak, s, 0) + from_high * shift(leak, -s, 0)
        b = b + from_low * shift(b, s, 0) + from_high * shift(b, -s, 0)
        low = from_low * shift(low, s, 0)
        high = from_high * shift(high, -s, 0)
    own = b / (leak + low + high)
    out_ref[pl.ds(0, NGY, stride=2), :] = own
    out_ref[pl.ds(1, NGY, stride=2), :] = shift(own, -1, 0)


def second_kernel(ends_ref, back_ref, spikes_ref, coeffs_ref, top_ref, second_ref, sums_ref, last_row_ref):
    own = ends_ref[pl.ds(0, NZB, stride=2), :]
    following = ends_ref[pl.ds(1, NZB, stride=2), :]
    firsts, lasts = [], []
    for y in range(NB):
        if y == 0:
            u = own
        else:
            u = back_ref[0, y - 1] + back_ref[1, y - 1] * own + back_ref[2, y - 1] * following
        second_ref[y] = u
        firsts.append(jnp.sum(spikes_ref[0, y] * u, axis=0, keepdims=True))
        lasts.append(jnp.sum(spikes_ref[1, y] * u, axis=0, keepdims=True))
    first, last = jnp.concatenate(firsts, axis=0), jnp.concatenate(lasts, axis=0)
    leak, couple, top = coeffs_ref[1], coeffs_ref[2], top_ref[...]
    inverse = 1.0 / (leak + couple + top)
    left, right = couple * inverse, top * inverse
    sums_ref[0] = coeffs_ref[0] + left * leak
    sums_ref[1] = right * leak
    sums_ref[2] = left * top
    sums_ref[3] = first + left * last
    sums_ref[4] = right * last
    last_row_ref[0] = last * inverse
    last_row_ref[1] = left
    last_row_ref[2] = right


def local_z_kernel(second_ref, factors_ref, t_ref, out_ref):
    row = rows_of((NZB, NX), 0)
    for y in range(NB):
        b = jnp.where((row == 0) | (row == NZB - 1), 0.0, second_ref[y])
        out_ref[y] = t_ref[y] + reduced_source(b, Z_STRIDES, 0, lambda j: factors_ref[j, y])


def last_kernel(local_ref, spikes_ref, last_row_ref, e0_ref, e1_ref, e2_ref, e3_ref, out_ref, line, ends):
    zg = lax.axis_index("zg")
    for j, e_ref in enumerate((e0_ref, e1_ref, e2_ref, e3_ref)):
        line[lax.rem(zg + (NZG - j), NZG)] = e_ref[...]
    inverses, sources = [], []
    leak, source = line[0, 0], line[0, 3]
    for d in range(NZG):
        couple = line[d, 2]
        inverse = 1.0 / (leak + couple)
        inverses.append(inverse)
        sources.append(source)
        if d + 1 < NZG:
            passed = couple * inverse
            leak = line[d + 1, 0] + line[d, 1] + passed * leak
            source = line[d + 1, 3] + line[d, 4] + passed * source
    value = jnp.zeros_like(source)
    ends[NZG] = value
    for d in reversed(range(NZG)):
        value = (sources[d] + line[d, 2] * value) * inverses[d]
        ends[d] = value
    own = ends[zg]
    following = last_row_ref[0] + last_row_ref[1] * own + last_row_ref[2] * ends[zg + 1]
    for y in range(NB):
        out_ref[y] = local_ref[y] + spikes_ref[0, y] * own[y:y + 1] + spikes_ref[1, y] * following[y:y + 1]


def call(kernel, name, outs, args, scratch=(), cost=2000000, whole=False):
    shapes = [jax.ShapeDtypeStruct(o, jnp.float32) for o in outs]
    vmem = pl.BlockSpec(memory_space=pltpu.VMEM)
    return pl.pallas_call(
        kernel,
        name=name,
        out_shape=shapes,
        in_specs=[pl.BlockSpec(memory_space=pltpu.HBM)] * len(args) if whole else [vmem] * len(args),
        out_specs=[vmem] * len(outs),
        scratch_shapes=scratch,
        cost_estimate=pl.CostEstimate(flops=cost, bytes_accessed=cost, transcendentals=0),
        compiler_params=pltpu.CompilerParams(vmem_limit_bytes=(54816 if whole else 24576) * 1024),
    )(*args)


def around(x, axis, by):
    count = lax.axis_size(axis)
    return lax.ppermute(x, axis, [(i, (i + by) % count) for i in range(count)])


def shards(t, k):
    block = (NB, NZB, NX)
    t, k, yp, yn, zp, zn = call(
        load_kernel, "load", [block, block, (2, NZB, NX), (2, NZB, NX), (2, NB, NX), (2, NB, NX)], [t, k],
        scratch=[pltpu.SemaphoreType.DMA((2,))], whole=True)
    yp = around(yp, "gy", 1)
    yn = around(yn, "gy", -1)
    zp = around(zp, "zg", 1)
    zn = around(zn, "zg", -1)
    factors, inner, faces, z_factors, spikes, coeffs = call(
        inner_kernel, "inner",
        [(2 * len(X_STRIDES) + 1, NB // 2, NX, 2 * NZB), block, (NB - 1, NZB, NX),
         (2 * len(Z_STRIDES) + 1,) + block, (2,) + block, (3, NB, NX)], [t, k])
    bundle, back, top = call(
        first_kernel, "first", [(NZB * VALUES, NX), (3, NB - 1, NZB, NX), (NB, NX)],
        [t, k, factors, inner, faces, yp, yn, zp, zn])
    columns = lax.all_to_all(bundle.reshape(NZB * VALUES, 1, NX), "gy", split_axis=0, concat_axis=0, tiled=True)
    (ends,) = call(column_kernel, "column", [(2 * NGY, NX)], [columns.reshape(NGY * VALUES, NX)])
    ends = lax.all_to_all(ends, "gy", split_axis=0, concat_axis=0, tiled=True)
    second, sums, last_row = call(
        second_kernel, "second", [block, (5, NB, NX), (3, NB, NX)], [ends, back, spikes, coeffs, top])
    sums = [sums] + [around(sums, "zg", j) for j in range(1, NZG)]
    (local,) = call(local_z_kernel, "local_z", [block], [second, z_factors, t])
    (out,) = call(last_kernel, "last", [block], [local, spikes, last_row] + sums,
                  scratch=[pltpu.VMEM((NZG, 5, NB, NX), jnp.float32), pltpu.VMEM((NZG + 1, NB, NX), jnp.float32)])
    return out


def solution(mesh):
    return jax.shard_map(
        shards,
        mesh=mesh,
        in_specs=(P("gy", "zg", None), P("gy", "zg", None)),
        out_specs=P("gy", "zg", None),
        check_vma=False,
    )
```

```python
import jax
import jax.numpy as jnp
from jax import lax
from jax.experimental import pallas as pl
from jax.experimental.pallas import tpu as pltpu
from jax.sharding import PartitionSpec as P

mesh_courant_number = 300.0

NB, NZB, NX = 4, 64, 128
NGY, NZG = 64, 4
X_STRIDES = (1, 2, 4, 8, 16, 32, 64)
Z_STRIDES = (1, 2, 4, 8, 16, 32)
VALUES = 5

HALO_GRANT, STAGE_GRANT = 55000, 54940


def face(k, q):
    return (2.0 * mesh_courant_number) * k * q / (k + q)


def shift(v, by, axis):
    return pltpu.roll(v, by % v.shape[axis], axis)


def rows_of(shape, axis):
    return lax.broadcasted_iota(jnp.int32, shape, axis)


def reduction_factors(leak, low, high, strides, axis, put):
    for j, s in enumerate(strides):
        inverse = 1.0 / (leak + low + high)
        from_low = low * shift(inverse, s, axis)
        from_high = high * shift(inverse, -s, axis)
        put(2 * j, from_low)
        put(2 * j + 1, from_high)
        leak = leak + from_low * shift(leak, s, axis) + from_high * shift(leak, -s, axis)
        low = from_low * shift(low, s, axis)
        high = from_high * shift(high, -s, axis)
    put(2 * len(strides), 1.0 / (leak + low + high))


def reduced_source(b, strides, axis, get):
    for j, s in enumerate(strides):
        b = b + get(2 * j) * shift(b, s, axis) + get(2 * j + 1) * shift(b, -s, axis)
    return b * get(2 * len(strides))


def halo_kernel(t_hbm, k_hbm, across_ref, inside_ref, zp_ref, zn_ref, edges, sems):
    odd = lax.rem(lax.axis_index("gy"), 2)
    copies = []
    for j, array in enumerate((t_hbm, k_hbm)):
        moves = (
            (array.at[odd * (NB - 1)], across_ref.at[j]),
            (array.at[(1 - odd) * (NB - 1)], inside_ref.at[j]),
            (array.at[:, pl.ds(NZB - 8, 8)], edges.at[j, 0]),
            (array.at[:, pl.ds(0, 8)], edges.at[j, 1]),
        )
        for n, (source, target) in enumerate(moves):
            copies.append(pltpu.make_async_copy(source, target, sems.at[j, n]))
            copies[-1].start()
    for copy in copies:
        copy.wait()
    for j in range(2):
        for y in range(NB):
            zp_ref[j, y:y + 1] = edges[j, 0, y, 7:]
            zn_ref[j, y:y + 1] = edges[j, 1, y, :1]


def pair(ref, h):
    return ref[2 * h:2 * h + 2].reshape(2 * NZB, NX).T


def z_part(k_ref, factors_ref, spikes_ref, coeffs_ref):
    row = rows_of((NZB, NX), 0)
    for y in range(NB):
        k = k_ref[y]
        g = face(k, shift(k, 1, 0))
        low = jnp.where((row > 1) & (row < NZB - 1), g, 0.0)
        at_first = jnp.where(row == 1, g, 0.0)
        at_last = jnp.where(row == NZB - 2, shift(g, -1, 0), 0.0)

        def put(j, v):
            factors_ref[j, y] = v

        reduction_factors(1.0 + at_first + at_last, low, shift(low, -1, 0), Z_STRIDES, 0, put)
        get = lambda j: factors_ref[j, y]
        lam = reduced_source(at_first, Z_STRIDES, 0, get)
        rho = reduced_source(at_last, Z_STRIDES, 0, get)
        coeffs_ref[2, y:y + 1] = g[NZB - 1:] * lam[NZB - 2:NZB - 1]
        lam = jnp.where(row == 0, 1.0, lam)
        rho = jnp.where(row == NZB - 1, 1.0, rho)
        spikes_ref[0, y] = lam
        spikes_ref[1, y] = rho
        coeffs_ref[0, y:y + 1] = jnp.sum(lam, axis=0, keepdims=True)
        coeffs_ref[1, y:y + 1] = jnp.sum(rho, axis=0, keepdims=True)


def stage_kernel(t_hbm, k_hbm, t_ref, k_ref, sems):
    copies = [pltpu.make_async_copy(t_hbm, t_ref, sems.at[0]), pltpu.make_async_copy(k_hbm, k_ref, sems.at[1])]
    for copy in copies:
        copy.start()
    for copy in copies:
        copy.wait()


def inner_kernel(t_ref, k_ref, factors_ref, inner_ref, faces_ref, z_factors_ref, spikes_ref, coeffs_ref):
    lane = rows_of((NZB, NX), 1)
    row = rows_of((NZB, NX), 0)
    flux_y = None
    for y in range(NB):
        k = k_ref[y]
        t = t_ref[y]
        low = jnp.where(lane > 0, face(k, shift(k, 1, 1)), 0.0)
        flux = low * (t - shift(t, 1, 1))
        total = shift(flux, -1, 1) - flux
        face_z = jnp.where(row > 0, face(k, shift(k, 1, 0)), 0.0)
        flux = face_z * (t - shift(t, 1, 0))
        total = total + (shift(flux, -1, 0) - flux)
        if y > 0:
            total = total - flux_y
        if y < NB - 1:
            next_face = face(k_ref[y + 1], k)
            faces_ref[y] = next_face
            flux_y = next_face * (t_ref[y + 1] - t)
            total = total + flux_y
        inner_ref[y] = total
    for h in range(NB // 2):
        k = pair(k_ref, h)
        low = jnp.where(rows_of(k.shape, 0) > 0, face(k, shift(k, 1, 0)), 0.0)

        def put(j, v):
            factors_ref[j, h] = v

        reduction_factors(jnp.ones_like(k), low, shift(low, -1, 0), X_STRIDES, 0, put)
    z_part(k_ref, z_factors_ref, spikes_ref, coeffs_ref)


def first_kernel(t_ref, k_ref, factors_ref, inner_ref, faces_ref, across_ref, inside_ref, zp_ref, zn_ref,
                 bundle_ref, back_ref, top_ref):
    gy = lax.axis_index("gy")
    zg = lax.axis_index("zg")
    odd = lax.rem(gy, 2) == 1
    yp = [jnp.where(odd, inside_ref[j], across_ref[j]) for j in range(2)]
    yn = [jnp.where(odd, across_ref[j], inside_ref[j]) for j in range(2)]
    has_south = jnp.where(gy > 0, 1.0, 0.0)
    has_north = jnp.where(gy < NGY - 1, 1.0, 0.0)
    has_below = jnp.where(zg > 0, 1.0, 0.0)
    has_above = jnp.where(zg < NZG - 1, 1.0, 0.0)
    row = rows_of((NZB, NX), 0)
    sources = []
    g4 = None
    for y in range(NB):
        b = inner_ref[y]
        t = t_ref[y]
        k = k_ref[y]
        if y == 0:
            b = b + face(k, yp[1] * has_south) * (yp[0] - t)
        if y == NB - 1:
            g4 = face(k, yn[1] * has_north)
            b = b + g4 * (yn[0] - t)
        below = face(k[:1], zp_ref[1, y:y + 1] * has_below) * (zp_ref[0, y:y + 1] - t[:1])
        top = face(k[NZB - 1:], zn_ref[1, y:y + 1] * has_above)
        top_ref[y:y + 1] = top
        above = top * (zn_ref[0, y:y + 1] - t[NZB - 1:])
        b = b + jnp.where(row == 0, below, 0.0) + jnp.where(row == NZB - 1, above, 0.0)
        sources.append(b)
    solved = []
    for h in range(NB // 2):
        b = jnp.concatenate(sources[2 * h:2 * h + 2], axis=0).T
        b = reduced_source(b, X_STRIDES, 0, lambda j: factors_ref[j, h]).T
        solved += [b[:NZB], b[NZB:]]
    b0, b1, b2, b3 = solved
    g1, g2, g3 = faces_ref[0], faces_ref[1], faces_ref[2]
    i1 = 1.0 / (1.0 + g1 + g2)
    left, right = g1 * i1, g2 * i1
    source = b0 + left * b1
    b2 = b2 + right * b1
    leak = 1.0 + left
    m2 = 1.0 + right
    a2 = g1 * right
    i2 = 1.0 / (m2 + a2 + g3)
    left, right = a2 * i2, g3 * i2
    source = source + left * b2
    b3 = b3 + right * b2
    leak = leak + left * m2
    m3 = 1.0 + right * m2
    a3 = a2 * right
    i3 = 1.0 / (m3 + a3 + g4)
    left, right = a3 * i3, g4 * i3
    put = lambda v, x: pltpu.store(bundle_ref.at[pl.ds(v, NZB, stride=VALUES), :], x)
    put(0, leak + left * m3)
    put(1, right * m3)
    put(2, a3 * right)
    put(3, source + left * b3)
    put(4, right * b3)
    beta, lam, rho = b3 * i3, left, right
    back_ref[0, 2], back_ref[1, 2], back_ref[2, 2] = beta, lam, rho
    beta, lam, rho = (b2 + g3 * beta) * i2, (a2 + g3 * lam) * i2, g3 * rho * i2
    back_ref[0, 1], back_ref[1, 1], back_ref[2, 1] = beta, lam, rho
    beta, lam, rho = (b1 + g2 * beta) * i1, (g1 + g2 * lam) * i1, g2 * rho * i1
    back_ref[0, 0], back_ref[1, 0], back_ref[2, 0] = beta, lam, rho


def column_kernel(bundle_ref, out_ref):
    get = lambda v: bundle_ref[pl.ds(v, NGY, stride=VALUES), :]
    leak = get(0) + shift(get(1), 1, 0)
    high = get(2)
    low = shift(high, 1, 0)
    b = get(3) + shift(get(4), 1, 0)
    for s in (1, 2, 4, 8, 16, 32):
        inverse = 1.0 / (leak + low + high)
        from_low = low * shift(inverse, s, 0)
        from_high = high * shift(inverse, -s, 0)
        leak = leak + from_low * shift(leak, s, 0) + from_high * shift(leak, -s, 0)
        b = b + from_low * shift(b, s, 0) + from_high * shift(b, -s, 0)
        low = from_low * shift(low, s, 0)
        high = from_high * shift(high, -s, 0)
    own = b / (leak + low + high)
    out_ref[pl.ds(0, NGY, stride=2), :] = own
    out_ref[pl.ds(1, NGY, stride=2), :] = shift(own, -1, 0)


def second_kernel(ends_ref, back_ref, spikes_ref, coeffs_ref, top_ref, second_ref, sums_ref, last_row_ref):
    own = ends_ref[pl.ds(0, NZB, stride=2), :]
    following = ends_ref[pl.ds(1, NZB, stride=2), :]
    firsts, lasts = [], []
    for y in range(NB):
        if y == 0:
            u = own
        else:
            u = back_ref[0, y - 1] + back_ref[1, y - 1] * own + back_ref[2, y - 1] * following
        second_ref[y] = u
        firsts.append(jnp.sum(spikes_ref[0, y] * u, axis=0, keepdims=True))
        lasts.append(jnp.sum(spikes_ref[1, y] * u, axis=0, keepdims=True))
    first, last = jnp.concatenate(firsts, axis=0), jnp.concatenate(lasts, axis=0)
    leak, couple, top = coeffs_ref[1], coeffs_ref[2], top_ref[...]
    inverse = 1.0 / (leak + couple + top)
    left, right = couple * inverse, top * inverse
    sums_ref[0] = coeffs_ref[0] + left * leak
    sums_ref[1] = right * leak
    sums_ref[2] = left * top
    sums_ref[3] = first + left * last
    sums_ref[4] = right * last
    last_row_ref[0] = last * inverse
    last_row_ref[1] = left
    last_row_ref[2] = right


def local_z_kernel(second_ref, factors_ref, t_ref, out_ref):
    row = rows_of((NZB, NX), 0)
    for y in range(NB):
        b = jnp.where((row == 0) | (row == NZB - 1), 0.0, second_ref[y])
        out_ref[y] = t_ref[y] + reduced_source(b, Z_STRIDES, 0, lambda j: factors_ref[j, y])


def last_kernel(local_ref, spikes_ref, last_row_ref, e0_ref, e1_ref, e2_ref, e3_ref, out_ref, line, ends):
    zg = lax.axis_index("zg")
    for j, e_ref in enumerate((e0_ref, e1_ref, e2_ref, e3_ref)):
        line[lax.rem(zg + (NZG - j), NZG)] = e_ref[...]
    inverses, sources = [], []
    leak, source = line[0, 0], line[0, 3]
    for d in range(NZG):
        couple = line[d, 2]
        inverse = 1.0 / (leak + couple)
        inverses.append(inverse)
        sources.append(source)
        if d + 1 < NZG:
            passed = couple * inverse
            leak = line[d + 1, 0] + line[d, 1] + passed * leak
            source = line[d + 1, 3] + line[d, 4] + passed * source
    value = jnp.zeros_like(source)
    ends[NZG] = value
    for d in reversed(range(NZG)):
        value = (sources[d] + line[d, 2] * value) * inverses[d]
        ends[d] = value
    own = ends[zg]
    following = last_row_ref[0] + last_row_ref[1] * own + last_row_ref[2] * ends[zg + 1]
    for y in range(NB):
        out_ref[y] = local_ref[y] + spikes_ref[0, y] * own[y:y + 1] + spikes_ref[1, y] * following[y:y + 1]


def call(kernel, name, outs, args, scratch=(), cost=2000000, granted=0):
    shapes = [jax.ShapeDtypeStruct(o, jnp.float32) for o in outs]
    vmem = pl.BlockSpec(memory_space=pltpu.VMEM)
    return pl.pallas_call(
        kernel,
        name=name,
        out_shape=shapes,
        in_specs=[pl.BlockSpec(memory_space=pltpu.HBM)] * len(args) if granted else [vmem] * len(args),
        out_specs=[vmem] * len(outs),
        scratch_shapes=scratch,
        cost_estimate=pl.CostEstimate(flops=cost, bytes_accessed=cost, transcendentals=0),
        compiler_params=pltpu.CompilerParams(vmem_limit_bytes=(granted or 24576) * 1024),
    )(*args)


def around(x, axis, by):
    count = lax.axis_size(axis)
    return lax.ppermute(x, axis, [(i, (i + by) % count) for i in range(count)])


def swapped(x, axis, first):
    count = lax.axis_size(axis)
    return lax.ppermute(x, axis, [(i, (((i - first) ^ 1) + first) % count) for i in range(count)])


def shards(t, k):
    block = (NB, NZB, NX)
    across, inside, zp, zn = call(
        halo_kernel, "halo", [(2, NZB, NX), (2, NZB, NX), (2, NB, NX), (2, NB, NX)], [t, k],
        scratch=[pltpu.VMEM((2, 2, NB, 8, NX), jnp.float32), pltpu.SemaphoreType.DMA((2, 4))], granted=HALO_GRANT)
    across = swapped(across, "gy", 1)
    zp = around(zp, "zg", 1)
    zn = around(zn, "zg", -1)
    inside = swapped(inside, "gy", 0)
    t, k = call(stage_kernel, "stage", [block, block], [t, k],
                scratch=[pltpu.SemaphoreType.DMA((2,))], granted=STAGE_GRANT)
    factors, inner, faces, z_factors, spikes, coeffs = call(
        inner_kernel, "inner",
        [(2 * len(X_STRIDES) + 1, NB // 2, NX, 2 * NZB), block, (NB - 1, NZB, NX),
         (2 * len(Z_STRIDES) + 1,) + block, (2,) + block, (3, NB, NX)], [t, k])
    bundle, back, top = call(
        first_kernel, "first", [(NZB * VALUES, NX), (3, NB - 1, NZB, NX), (NB, NX)],
        [t, k, factors, inner, faces, across, inside, zp, zn])
    columns = lax.all_to_all(bundle.reshape(NZB * VALUES, 1, NX), "gy", split_axis=0, concat_axis=0, tiled=True)
    (ends,) = call(column_kernel, "column", [(2 * NGY, NX)], [columns.reshape(NGY * VALUES, NX)])
    ends = lax.all_to_all(ends, "gy", split_axis=0, concat_axis=0, tiled=True)
    second, sums, last_row = call(
        second_kernel, "second", [block, (5, NB, NX), (3, NB, NX)], [ends, back, spikes, coeffs, top])
    sums = [sums] + [around(sums, "zg", j) for j in range(1, NZG)]
    (local,) = call(local_z_kernel, "local_z", [block], [second, z_factors, t])
    (out,) = call(last_kernel, "last", [block], [local, spikes, last_row] + sums,
                  scratch=[pltpu.VMEM((NZG, 5, NB, NX), jnp.float32), pltpu.VMEM((NZG + 1, NB, NX), jnp.float32)])
    return out


def solution(mesh):
    return jax.shard_map(
        shards,
        mesh=mesh,
        in_specs=(P("gy", "zg", None), P("gy", "zg", None)),
        out_specs=P("gy", "zg", None),
        check_vma=False,
    )
```

```python
import jax
import jax.numpy as jnp
from jax import lax
from jax.experimental import pallas as pl
from jax.experimental.pallas import tpu as pltpu
from jax.sharding import PartitionSpec as P

mesh_courant_number = 300.0

NB, NZB, NX = 4, 64, 128
NGY, NZG = 64, 4
LANES = 8
XC, ZC, YC = NX // LANES, NZB // LANES, NGY // LANES
STRIDES = (1, 2, 4)
VALUES = 5

LOAD_GRANT = 54816


def face(k, q):
    return (2.0 * mesh_courant_number) * k * q / (k + q)


def shift(v, by, axis):
    return pltpu.roll(v, by % v.shape[axis], axis)


def rows_of(shape, axis):
    return lax.broadcasted_iota(jnp.int32, shape, axis)


def chunked(load, count):
    return jnp.concatenate([load(pl.ds(a, LANES, stride=count)) for a in range(count)], axis=0)


def split(v):
    return [v[LANES * a:LANES * (a + 1)] for a in range(v.shape[0] // LANES)]


def before(v):
    last = v.shape[0] - LANES
    return jnp.concatenate([shift(v[last:], 1, 0), v[:last]], axis=0)


def after(v):
    return jnp.concatenate([v[LANES:], shift(v[:LANES], -1, 0)], axis=0)


def order(count):
    step = 1
    while step < count:
        for a in range(step, count, 2 * step):
            yield a, step
        step *= 2


def fold(leaks, couples, closed=None):
    leaks, couples, plan, over = list(leaks), list(couples), [], 0.0
    count = len(leaks)
    for a, step in order(count):
        low, high = couples[a - step], couples[a]
        inverse = 1.0 / (leaks[a] + low + high)
        left, right = low * inverse, high * inverse
        if closed is not None and a == count - 1:
            inverse = jnp.where(closed, 0.0, inverse)
            left = jnp.where(closed, 0.0, left)
            right = jnp.where(closed, 1.0, right)
        plan.append((inverse, left, right))
        leaks[a - step] = leaks[a - step] + left * leaks[a]
        if a + step < count:
            leaks[a + step] = leaks[a + step] + right * leaks[a]
        else:
            over = over + right * leaks[a]
        couples[a - step] = low * right
    return plan, leaks[0], over, couples[0]


def fold_sources(plan, sources):
    sources, over = list(sources), 0.0
    count = len(sources)
    for (a, step), (_, left, right) in zip(order(count), plan):
        sources[a - step] = sources[a - step] + left * sources[a]
        if a + step < count:
            sources[a + step] = sources[a + step] + right * sources[a]
        else:
            over = over + right * sources[a]
    return sources, over


def unfold(plan, sources, head, following):
    count = len(plan) + 1
    x = [head] + [None] * (count - 1) + [following]
    for (a, step), (inverse, left, right) in reversed(list(zip(order(count), plan))):
        x[a] = left * x[a - step] + right * x[min(a + step, count)]
        if sources is not None:
            x[a] = x[a] + inverse * sources[a]
    return x[:count]


def put_plan(ref, at, plan):
    for i, entries in enumerate(plan):
        for j, entry in enumerate(entries):
            ref[at + (i, j)] = entry


def get_plan(ref, at, count):
    return [tuple(ref[at + (i, j)] for j in range(3)) for i in range(count - 1)]


def separator_factors(leak, low, high):
    factors = []
    for s in STRIDES:
        inverse = 1.0 / (leak + low + high)
        from_low = low * shift(inverse, s, 0)
        from_high = high * shift(inverse, -s, 0)
        factors += [from_low, from_high]
        leak = leak + from_low * shift(leak, s, 0) + from_high * shift(leak, -s, 0)
        low = from_low * shift(low, s, 0)
        high = from_high * shift(high, -s, 0)
    return factors + [1.0 / (leak + low + high)]


def separator_solve(factors, b):
    for j, s in enumerate(STRIDES):
        b = b + factors[2 * j] * shift(b, s, 0) + factors[2 * j + 1] * shift(b, -s, 0)
    return b * factors[2 * len(STRIDES)]


def load_kernel(t_hbm, k_hbm, t_ref, k_ref, across_ref, inside_ref, zp_ref, zn_ref, sems):
    odd = lax.rem(lax.axis_index("gy"), 2)
    copies = [pltpu.make_async_copy(t_hbm, t_ref, sems.at[0]), pltpu.make_async_copy(k_hbm, k_ref, sems.at[1])]
    for copy in copies:
        copy.start()
    for j, (copy, ref) in enumerate(zip(copies, (t_ref, k_ref))):
        copy.wait()
        across_ref[j] = ref[odd * (NB - 1)]
        inside_ref[j] = ref[(1 - odd) * (NB - 1)]
        for y in range(NB):
            zp_ref[j, y:y + 1] = ref[y, NZB - 1:]
            zn_ref[j, y:y + 1] = ref[y, :1]


def block_row(ref, *at):
    return chunked(lambda rows: ref[at + (rows, slice(None))], ZC)


def inner_kernel(t_ref, k_ref, inner_ref, faces_ref, x_plan_ref, x_ends_ref, z_plan_ref, z_ends_ref, spikes_ref,
                 coeffs_ref, turned):
    lane = rows_of((NZB, NX), 1)
    row = rows_of((NZB, NX), 0)
    chunk = rows_of((LANES, NX), 0)
    ts = [block_row(t_ref, y) for y in range(NB)]
    ks = [block_row(k_ref, y) for y in range(NB)]
    flux_y = None
    for y in range(NB):
        k, t = ks[y], ts[y]
        low = jnp.where(lane > 0, face(k, shift(k, 1, 1)), 0.0)
        flux = low * (t - shift(t, 1, 1))
        total = shift(flux, -1, 1) - flux
        face_z = jnp.where(row > 0, face(k, before(k)), 0.0)
        flux = face_z * (t - before(t))
        total = total + (after(flux) - flux)
        if y > 0:
            total = total - flux_y
        if y < NB - 1:
            next_face = face(ks[y + 1], k)
            faces_ref[y] = next_face
            flux_y = next_face * (ts[y + 1] - t)
            total = total + flux_y
        inner_ref[y] = total

        ones = [jnp.ones((LANES, NX), jnp.float32)] * ZC
        plan, leak, over, couple = fold(ones, split(after(face_z)), chunk == LANES - 1)
        put_plan(z_plan_ref, (y,), plan)
        over = shift(over, 1, 0)
        leak_end = over[:1]
        leak = leak + jnp.where(chunk > 0, over, 0.0)
        low = shift(couple, 1, 0)
        at_first = jnp.where(chunk == 1, low, 0.0)
        at_last = jnp.where(chunk == LANES - 1, couple, 0.0)
        factors = separator_factors(leak + at_first + at_last, jnp.where(chunk > 1, low, 0.0),
                                    jnp.where((chunk > 0) & (chunk < LANES - 1), couple, 0.0))
        for j, factor in enumerate(factors):
            z_ends_ref[y, j] = factor
        lam = jnp.where(chunk == 0, 1.0, separator_solve(factors, at_first))
        rho = separator_solve(factors, at_last)
        coeffs_ref[0, y:y + 1] = jnp.sum(lam * leak, axis=0, keepdims=True)
        coeffs_ref[1, y:y + 1] = jnp.sum(rho * leak, axis=0, keepdims=True) + leak_end
        coeffs_ref[2, y:y + 1] = couple[LANES - 1:] * lam[LANES - 1:]
        following = jnp.where(chunk == LANES - 1, 0.0, shift(lam, -1, 0))
        spikes_ref[0, y] = jnp.concatenate(unfold(plan, None, lam, following), axis=0)
        following = jnp.where(chunk == LANES - 1, 1.0, shift(rho, -1, 0))
        spikes_ref[1, y] = jnp.concatenate(unfold(plan, None, rho, following), axis=0)

    for h in range(NB // 2):
        turned[h] = jnp.concatenate(ks[2 * h:2 * h + 2], axis=0).T
        k = block_line(turned, h)
        couples = face(k, after(k))
        couples = jnp.where((rows_of(couples.shape, 0) == NX - 1), 0.0, couples)
        ones = [jnp.ones((LANES, 2 * NZB), jnp.float32)] * XC
        plan, leak, over, couple = fold(ones, split(couples))
        put_plan(x_plan_ref, (h,), plan)
        factors = separator_factors(leak + shift(over, 1, 0), shift(couple, 1, 0), couple)
        for j, factor in enumerate(factors):
            x_ends_ref[h, j] = factor


def block_line(ref, h):
    return chunked(lambda rows: ref[h, rows, :], XC)


def first_kernel(t_ref, k_ref, inner_ref, faces_ref, x_plan_ref, x_ends_ref, across_ref, inside_ref, zp_ref, zn_ref,
                 bundle_ref, back_ref, top_ref, turned):
    gy = lax.axis_index("gy")
    zg = lax.axis_index("zg")
    odd = lax.rem(gy, 2) == 1
    across = [block_row(across_ref, j) for j in range(2)]
    inside = [block_row(inside_ref, j) for j in range(2)]
    yp = [jnp.where(odd, b, a) for a, b in zip(across, inside)]
    yn = [jnp.where(odd, a, b) for a, b in zip(across, inside)]
    has_south = jnp.where(gy > 0, 1.0, 0.0)
    has_north = jnp.where(gy < NGY - 1, 1.0, 0.0)
    has_below = jnp.where(zg > 0, 1.0, 0.0)
    has_above = jnp.where(zg < NZG - 1, 1.0, 0.0)
    row = rows_of((NZB, NX), 0)
    sources = []
    g4 = None
    for y in range(NB):
        b = inner_ref[y]
        if y == 0:
            b = b + face(block_row(k_ref, y), yp[1] * has_south) * (yp[0] - block_row(t_ref, y))
        if y == NB - 1:
            g4 = face(block_row(k_ref, y), yn[1] * has_north)
            b = b + g4 * (yn[0] - block_row(t_ref, y))
        k_low, k_high = k_ref[y, :1], k_ref[y, NZB - 1:]
        below = face(k_low, zp_ref[1, y:y + 1] * has_below) * (zp_ref[0, y:y + 1] - t_ref[y, :1])
        top = face(k_high, zn_ref[1, y:y + 1] * has_above)
        top_ref[y:y + 1] = top
        above = top * (zn_ref[0, y:y + 1] - t_ref[y, NZB - 1:])
        b = b + jnp.where(row == 0, below, 0.0) + jnp.where(row == NZB - 1, above, 0.0)
        sources.append(b)
    solved = []
    for h in range(NB // 2):
        turned[h] = jnp.concatenate(sources[2 * h:2 * h + 2], axis=0).T
        plan = get_plan(x_plan_ref, (h,), XC)
        b, over = fold_sources(plan, split(block_line(turned, h)))
        head = separator_solve([x_ends_ref[h, j] for j in range(2 * len(STRIDES) + 1)], b[0] + shift(over, 1, 0))
        for a, x in enumerate(unfold(plan, b, head, shift(head, -1, 0))):
            turned[h, pl.ds(a, LANES, stride=XC), :] = x
        b = turned[h].T
        solved += [b[:NZB], b[NZB:]]
    b0, b1, b2, b3 = solved
    g1, g2, g3 = faces_ref[0], faces_ref[1], faces_ref[2]
    i1 = 1.0 / (1.0 + g1 + g2)
    left, right = g1 * i1, g2 * i1
    source = b0 + left * b1
    b2 = b2 + right * b1
    leak = 1.0 + left
    m2 = 1.0 + right
    a2 = g1 * right
    i2 = 1.0 / (m2 + a2 + g3)
    left, right = a2 * i2, g3 * i2
    source = source + left * b2
    b3 = b3 + right * b2
    leak = leak + left * m2
    m3 = 1.0 + right * m2
    a3 = a2 * right
    i3 = 1.0 / (m3 + a3 + g4)
    left, right = a3 * i3, g4 * i3

    def put(v, x):
        for a, part in enumerate(split(x)):
            bundle_ref[pl.ds(VALUES * a + v, LANES, stride=VALUES * ZC), :] = part

    put(0, leak + left * m3)
    put(1, right * m3)
    put(2, a3 * right)
    put(3, source + left * b3)
    put(4, right * b3)
    beta, lam, rho = b3 * i3, left, right
    back_ref[0, 2], back_ref[1, 2], back_ref[2, 2] = beta, lam, rho
    beta, lam, rho = (b2 + g3 * beta) * i2, (a2 + g3 * lam) * i2, g3 * rho * i2
    back_ref[0, 1], back_ref[1, 1], back_ref[2, 1] = beta, lam, rho
    beta, lam, rho = (b1 + g2 * beta) * i1, (g1 + g2 * lam) * i1, g2 * rho * i1
    back_ref[0, 0], back_ref[1, 0], back_ref[2, 0] = beta, lam, rho


def column_kernel(bundle_ref, out_ref):
    get = lambda v: [bundle_ref[pl.ds(VALUES * a + v, LANES, stride=VALUES * YC), :] for a in range(YC)]
    joined = lambda own, pushed: split(jnp.concatenate(own, axis=0) + before(jnp.concatenate(pushed, axis=0)))
    plan, leak, over, couple = fold(joined(get(0), get(1)), get(2))
    b, over_source = fold_sources(plan, joined(get(3), get(4)))
    factors = separator_factors(leak + shift(over, 1, 0), shift(couple, 1, 0), couple)
    head = separator_solve(factors, b[0] + shift(over_source, 1, 0))
    following = shift(head, -1, 0)
    x = unfold(plan, b, head, following) + [following]
    for a in range(YC):
        out_ref[pl.ds(2 * a, LANES, stride=2 * YC), :] = x[a]
        out_ref[pl.ds(2 * a + 1, LANES, stride=2 * YC), :] = x[a + 1]


def second_kernel(ends_ref, back_ref, spikes_ref, coeffs_ref, top_ref, second_ref, sums_ref, last_row_ref):
    get = lambda v: jnp.concatenate(
        [ends_ref[pl.ds(2 * a + v, LANES, stride=2 * ZC), :] for a in range(ZC)], axis=0)
    own, following = get(0), get(1)
    firsts, lasts = [], []
    for y in range(NB):
        if y == 0:
            u = own
        else:
            u = back_ref[0, y - 1] + back_ref[1, y - 1] * own + back_ref[2, y - 1] * following
        second_ref[y] = u
        firsts.append(jnp.sum(spikes_ref[0, y] * u, axis=0, keepdims=True))
        lasts.append(jnp.sum(spikes_ref[1, y] * u, axis=0, keepdims=True))
    first, last = jnp.concatenate(firsts, axis=0), jnp.concatenate(lasts, axis=0)
    leak, couple, top = coeffs_ref[1], coeffs_ref[2], top_ref[...]
    inverse = 1.0 / (leak + couple + top)
    left, right = couple * inverse, top * inverse
    sums_ref[0] = coeffs_ref[0] + left * leak
    sums_ref[1] = right * leak
    sums_ref[2] = left * top
    sums_ref[3] = first + left * last
    sums_ref[4] = right * last
    last_row_ref[0] = last * inverse
    last_row_ref[1] = left
    last_row_ref[2] = right


def local_z_kernel(second_ref, z_plan_ref, z_ends_ref, t_ref, out_ref):
    chunk = rows_of((LANES, NX), 0)
    for y in range(NB):
        plan = get_plan(z_plan_ref, (y,), ZC)
        b, over = fold_sources(plan, split(second_ref[y]))
        b0 = jnp.where(chunk > 0, b[0] + shift(over, 1, 0), 0.0)
        head = separator_solve([z_ends_ref[y, j] for j in range(2 * len(STRIDES) + 1)], b0)
        following = jnp.where(chunk == LANES - 1, 0.0, shift(head, -1, 0))
        x = jnp.concatenate(unfold(plan, b, head, following), axis=0)
        out_ref[y] = block_row(t_ref, y) + x


def last_kernel(local_ref, spikes_ref, last_row_ref, e0_ref, e1_ref, e2_ref, e3_ref, out_ref, line, ends):
    zg = lax.axis_index("zg")
    for j, e_ref in enumerate((e0_ref, e1_ref, e2_ref, e3_ref)):
        line[lax.rem(zg + (NZG - j), NZG)] = e_ref[...]
    inverses, sources = [], []
    leak, source = line[0, 0], line[0, 3]
    for d in range(NZG):
        couple = line[d, 2]
        inverse = 1.0 / (leak + couple)
        inverses.append(inverse)
        sources.append(source)
        if d + 1 < NZG:
            passed = couple * inverse
            leak = line[d + 1, 0] + line[d, 1] + passed * leak
            source = line[d + 1, 3] + line[d, 4] + passed * source
    value = jnp.zeros_like(source)
    ends[NZG] = value
    for d in reversed(range(NZG)):
        value = (sources[d] + line[d, 2] * value) * inverses[d]
        ends[d] = value
    own = ends[zg]
    following = last_row_ref[0] + last_row_ref[1] * own + last_row_ref[2] * ends[zg + 1]
    for y in range(NB):
        x = local_ref[y] + spikes_ref[0, y] * own[y:y + 1] + spikes_ref[1, y] * following[y:y + 1]
        for a, part in enumerate(split(x)):
            out_ref[y, pl.ds(a, LANES, stride=ZC), :] = part


def call(kernel, name, outs, args, scratch=(), cost=2000000, granted=0):
    shapes = [jax.ShapeDtypeStruct(o, jnp.float32) for o in outs]
    vmem = pl.BlockSpec(memory_space=pltpu.VMEM)
    return pl.pallas_call(
        kernel,
        name=name,
        out_shape=shapes,
        in_specs=[pl.BlockSpec(memory_space=pltpu.HBM)] * len(args) if granted else [vmem] * len(args),
        out_specs=[vmem] * len(outs),
        scratch_shapes=scratch,
        cost_estimate=pl.CostEstimate(flops=cost, bytes_accessed=cost, transcendentals=0),
        compiler_params=pltpu.CompilerParams(vmem_limit_bytes=(granted or 24576) * 1024),
    )(*args)


def around(x, axis, by):
    count = lax.axis_size(axis)
    return lax.ppermute(x, axis, [(i, (i + by) % count) for i in range(count)])


def swapped(x, axis, first):
    count = lax.axis_size(axis)
    return lax.ppermute(x, axis, [(i, (((i - first) ^ 1) + first) % count) for i in range(count)])


def shards(t, k):
    block = (NB, NZB, NX)
    t, k, across, inside, zp, zn = call(
        load_kernel, "load", [block, block, (2, NZB, NX), (2, NZB, NX), (2, NB, NX), (2, NB, NX)], [t, k],
        scratch=[pltpu.SemaphoreType.DMA((2,))], granted=LOAD_GRANT)
    across = swapped(across, "gy", 1)
    zp = around(zp, "zg", 1)
    zn = around(zn, "zg", -1)
    inside = swapped(inside, "gy", 0)
    turned = pltpu.VMEM((NB // 2, NX, 2 * NZB), jnp.float32)
    ends = (2 * len(STRIDES) + 1, LANES, NX)
    inner, faces, x_plan, x_ends, z_plan, z_ends, spikes, coeffs = call(
        inner_kernel, "inner",
        [block, (NB - 1, NZB, NX), (NB // 2, XC - 1, 3, LANES, 2 * NZB), (NB // 2,) + ends,
         (NB, ZC - 1, 3, LANES, NX), (NB,) + ends, (2,) + block, (3, NB, NX)], [t, k], scratch=[turned])
    bundle, back, top = call(
        first_kernel, "first", [(NZB * VALUES, NX), (3, NB - 1, NZB, NX), (NB, NX)],
        [t, k, inner, faces, x_plan, x_ends, across, inside, zp, zn], scratch=[turned])
    columns = lax.all_to_all(bundle.reshape(NZB * VALUES, 1, NX), "gy", split_axis=0, concat_axis=0, tiled=True)
    (ends,) = call(column_kernel, "column", [(2 * NGY, NX)], [columns.reshape(NGY * VALUES, NX)])
    ends = lax.all_to_all(ends, "gy", split_axis=0, concat_axis=0, tiled=True)
    second, sums, last_row = call(
        second_kernel, "second", [block, (5, NB, NX), (3, NB, NX)], [ends, back, spikes, coeffs, top])
    sums = [sums] + [around(sums, "zg", j) for j in range(1, NZG)]
    (local,) = call(local_z_kernel, "local_z", [block], [second, z_plan, z_ends, t])
    (out,) = call(last_kernel, "last", [block], [local, spikes, last_row] + sums,
                  scratch=[pltpu.VMEM((NZG, 5, NB, NX), jnp.float32), pltpu.VMEM((NZG + 1, NB, NX), jnp.float32)])
    return out


def solution(mesh):
    return jax.shard_map(
        shards,
        mesh=mesh,
        in_specs=(P("gy", "zg", None), P("gy", "zg", None)),
        out_specs=P("gy", "zg", None),
        check_vma=False,
    )
```

```python
import jax
import jax.numpy as jnp
from jax import lax
from jax.experimental import pallas as pl
from jax.experimental.pallas import tpu as pltpu
from jax.sharding import PartitionSpec as P

mesh_courant_number = 300.0

NB, NZB, NX = 4, 64, 128
NGY, NZG = 64, 4
LANES = 8
XC, ZC, YC = NX // LANES, NZB // LANES, NGY // LANES
STRIDES = (1, 2, 4)
VALUES = 5

LOAD_GRANT = 54816


def face(k, q):
    return (2.0 * mesh_courant_number) * k * q / (k + q)


def shift(v, by, axis):
    return pltpu.roll(v, by % v.shape[axis], axis)


def rows_of(shape, axis):
    return lax.broadcasted_iota(jnp.int32, shape, axis)


def chunked(load, count):
    return jnp.concatenate([load(pl.ds(a, LANES, stride=count)) for a in range(count)], axis=0)


def split(v):
    return [v[LANES * a:LANES * (a + 1)] for a in range(v.shape[0] // LANES)]


def before(v):
    last = v.shape[0] - LANES
    return jnp.concatenate([shift(v[last:], 1, 0), v[:last]], axis=0)


def after(v):
    return jnp.concatenate([v[LANES:], shift(v[:LANES], -1, 0)], axis=0)


def order(count):
    step = 1
    while step < count:
        for a in range(step, count, 2 * step):
            yield a, step
        step *= 2


def fold(leaks, couples, closed=None):
    leaks, couples, plan, over = list(leaks), list(couples), [], 0.0
    count = len(leaks)
    for a, step in order(count):
        low, high = couples[a - step], couples[a]
        inverse = 1.0 / (leaks[a] + low + high)
        left, right = low * inverse, high * inverse
        if closed is not None and a == count - 1:
            inverse = jnp.where(closed, 0.0, inverse)
            left = jnp.where(closed, 0.0, left)
            right = jnp.where(closed, 1.0, right)
        plan.append((inverse, left, right))
        leaks[a - step] = leaks[a - step] + left * leaks[a]
        if a + step < count:
            leaks[a + step] = leaks[a + step] + right * leaks[a]
        else:
            over = over + right * leaks[a]
        couples[a - step] = low * right
    return plan, leaks[0], over, couples[0]


def fold_sources(plan, sources):
    sources, over = list(sources), 0.0
    count = len(sources)
    for (a, step), (_, left, right) in zip(order(count), plan):
        sources[a - step] = sources[a - step] + left * sources[a]
        if a + step < count:
            sources[a + step] = sources[a + step] + right * sources[a]
        else:
            over = over + right * sources[a]
    return sources, over


def unfold(plan, sources, head, following):
    count = len(plan) + 1
    x = [head] + [None] * (count - 1) + [following]
    for (a, step), (inverse, left, right) in reversed(list(zip(order(count), plan))):
        x[a] = left * x[a - step] + right * x[min(a + step, count)]
        if sources is not None:
            x[a] = x[a] + inverse * sources[a]
    return x[:count]


def put_plan(ref, at, plan):
    for i, entries in enumerate(plan):
        for j, entry in enumerate(entries):
            ref[at + (i, j)] = entry


def get_plan(ref, at, count):
    return [tuple(ref[at + (i, j)] for j in range(3)) for i in range(count - 1)]


def separator_factors(leak, low, high):
    factors = []
    for s in STRIDES:
        inverse = 1.0 / (leak + low + high)
        from_low = low * shift(inverse, s, 0)
        from_high = high * shift(inverse, -s, 0)
        factors += [from_low, from_high]
        leak = leak + from_low * shift(leak, s, 0) + from_high * shift(leak, -s, 0)
        low = from_low * shift(low, s, 0)
        high = from_high * shift(high, -s, 0)
    return factors + [1.0 / (leak + low + high)]


def separator_solve(factors, b):
    for j, s in enumerate(STRIDES):
        b = b + factors[2 * j] * shift(b, s, 0) + factors[2 * j + 1] * shift(b, -s, 0)
    return b * factors[2 * len(STRIDES)]


def load_kernel(t_hbm, k_hbm, t_ref, k_ref, across_ref, inside_ref, z_even_ref, z_odd_ref, sems):
    odd = lax.rem(lax.axis_index("gy"), 2)
    upper = lax.rem(lax.axis_index("zg"), 2) == 1
    copies = [pltpu.make_async_copy(t_hbm, t_ref, sems.at[0]), pltpu.make_async_copy(k_hbm, k_ref, sems.at[1])]
    for copy in copies:
        copy.start()
    for j, (copy, ref) in enumerate(zip(copies, (t_ref, k_ref))):
        copy.wait()
        across_ref[j] = ref[odd * (NB - 1)]
        inside_ref[j] = ref[(1 - odd) * (NB - 1)]
        for y in range(NB):
            first, last = ref[y, :1], ref[y, NZB - 1:]
            z_even_ref[j, y:y + 1] = jnp.where(upper, first, last)
            z_odd_ref[j, y:y + 1] = jnp.where(upper, last, first)


def block_row(ref, *at):
    return chunked(lambda rows: ref[at + (rows, slice(None))], ZC)


def inner_kernel(t_ref, k_ref, inner_ref, faces_ref, x_plan_ref, x_ends_ref, z_plan_ref, z_ends_ref, spikes_ref,
                 coeffs_ref, turned):
    lane = rows_of((NZB, NX), 1)
    row = rows_of((NZB, NX), 0)
    chunk = rows_of((LANES, NX), 0)
    ts = [block_row(t_ref, y) for y in range(NB)]
    ks = [block_row(k_ref, y) for y in range(NB)]
    flux_y = None
    for y in range(NB):
        k, t = ks[y], ts[y]
        low = jnp.where(lane > 0, face(k, shift(k, 1, 1)), 0.0)
        flux = low * (t - shift(t, 1, 1))
        total = shift(flux, -1, 1) - flux
        face_z = jnp.where(row > 0, face(k, before(k)), 0.0)
        flux = face_z * (t - before(t))
        total = total + (after(flux) - flux)
        if y > 0:
            total = total - flux_y
        if y < NB - 1:
            next_face = face(ks[y + 1], k)
            faces_ref[y] = next_face
            flux_y = next_face * (ts[y + 1] - t)
            total = total + flux_y
        inner_ref[y] = total

        ones = [jnp.ones((LANES, NX), jnp.float32)] * ZC
        plan, leak, over, couple = fold(ones, split(after(face_z)), chunk == LANES - 1)
        put_plan(z_plan_ref, (y,), plan)
        over = shift(over, 1, 0)
        leak_end = over[:1]
        leak = leak + jnp.where(chunk > 0, over, 0.0)
        low = shift(couple, 1, 0)
        at_first = jnp.where(chunk == 1, low, 0.0)
        at_last = jnp.where(chunk == LANES - 1, couple, 0.0)
        factors = separator_factors(leak + at_first + at_last, jnp.where(chunk > 1, low, 0.0),
                                    jnp.where((chunk > 0) & (chunk < LANES - 1), couple, 0.0))
        for j, factor in enumerate(factors):
            z_ends_ref[y, j] = factor
        lam = jnp.where(chunk == 0, 1.0, separator_solve(factors, at_first))
        rho = separator_solve(factors, at_last)
        coeffs_ref[0, y:y + 1] = jnp.sum(lam * leak, axis=0, keepdims=True)
        coeffs_ref[1, y:y + 1] = jnp.sum(rho * leak, axis=0, keepdims=True) + leak_end
        coeffs_ref[2, y:y + 1] = couple[LANES - 1:] * lam[LANES - 1:]
        following = jnp.where(chunk == LANES - 1, 0.0, shift(lam, -1, 0))
        spikes_ref[0, y] = jnp.concatenate(unfold(plan, None, lam, following), axis=0)
        following = jnp.where(chunk == LANES - 1, 1.0, shift(rho, -1, 0))
        spikes_ref[1, y] = jnp.concatenate(unfold(plan, None, rho, following), axis=0)

    for h in range(NB // 2):
        turned[h] = jnp.concatenate(ks[2 * h:2 * h + 2], axis=0).T
        k = block_line(turned, h)
        couples = face(k, after(k))
        couples = jnp.where((rows_of(couples.shape, 0) == NX - 1), 0.0, couples)
        ones = [jnp.ones((LANES, 2 * NZB), jnp.float32)] * XC
        plan, leak, over, couple = fold(ones, split(couples))
        put_plan(x_plan_ref, (h,), plan)
        factors = separator_factors(leak + shift(over, 1, 0), shift(couple, 1, 0), couple)
        for j, factor in enumerate(factors):
            x_ends_ref[h, j] = factor


def block_line(ref, h):
    return chunked(lambda rows: ref[h, rows, :], XC)


def first_kernel(t_ref, k_ref, inner_ref, faces_ref, x_plan_ref, x_ends_ref, across_ref, inside_ref, z_even_ref, z_odd_ref,
                 bundle_ref, back_ref, top_ref, turned):
    gy = lax.axis_index("gy")
    zg = lax.axis_index("zg")
    odd = lax.rem(gy, 2) == 1
    across = [block_row(across_ref, j) for j in range(2)]
    inside = [block_row(inside_ref, j) for j in range(2)]
    yp = [jnp.where(odd, b, a) for a, b in zip(across, inside)]
    yn = [jnp.where(odd, a, b) for a, b in zip(across, inside)]
    upper = lax.rem(zg, 2) == 1
    zp = jnp.where(upper, z_even_ref[...], z_odd_ref[...])
    zn = jnp.where(upper, z_odd_ref[...], z_even_ref[...])
    has_south = jnp.where(gy > 0, 1.0, 0.0)
    has_north = jnp.where(gy < NGY - 1, 1.0, 0.0)
    has_below = jnp.where(zg > 0, 1.0, 0.0)
    has_above = jnp.where(zg < NZG - 1, 1.0, 0.0)
    row = rows_of((NZB, NX), 0)
    sources = []
    g4 = None
    for y in range(NB):
        b = inner_ref[y]
        if y == 0:
            b = b + face(block_row(k_ref, y), yp[1] * has_south) * (yp[0] - block_row(t_ref, y))
        if y == NB - 1:
            g4 = face(block_row(k_ref, y), yn[1] * has_north)
            b = b + g4 * (yn[0] - block_row(t_ref, y))
        k_low, k_high = k_ref[y, :1], k_ref[y, NZB - 1:]
        below = face(k_low, zp[1, y:y + 1] * has_below) * (zp[0, y:y + 1] - t_ref[y, :1])
        top = face(k_high, zn[1, y:y + 1] * has_above)
        top_ref[y:y + 1] = top
        above = top * (zn[0, y:y + 1] - t_ref[y, NZB - 1:])
        b = b + jnp.where(row == 0, below, 0.0) + jnp.where(row == NZB - 1, above, 0.0)
        sources.append(b)
    solved = []
    for h in range(NB // 2):
        turned[h] = jnp.concatenate(sources[2 * h:2 * h + 2], axis=0).T
        plan = get_plan(x_plan_ref, (h,), XC)
        b, over = fold_sources(plan, split(block_line(turned, h)))
        head = separator_solve([x_ends_ref[h, j] for j in range(2 * len(STRIDES) + 1)], b[0] + shift(over, 1, 0))
        for a, x in enumerate(unfold(plan, b, head, shift(head, -1, 0))):
            turned[h, pl.ds(a, LANES, stride=XC), :] = x
        b = turned[h].T
        solved += [b[:NZB], b[NZB:]]
    b0, b1, b2, b3 = solved
    g1, g2, g3 = faces_ref[0], faces_ref[1], faces_ref[2]
    i1 = 1.0 / (1.0 + g1 + g2)
    left, right = g1 * i1, g2 * i1
    source = b0 + left * b1
    b2 = b2 + right * b1
    leak = 1.0 + left
    m2 = 1.0 + right
    a2 = g1 * right
    i2 = 1.0 / (m2 + a2 + g3)
    left, right = a2 * i2, g3 * i2
    source = source + left * b2
    b3 = b3 + right * b2
    leak = leak + left * m2
    m3 = 1.0 + right * m2
    a3 = a2 * right
    i3 = 1.0 / (m3 + a3 + g4)
    left, right = a3 * i3, g4 * i3

    def put(v, x):
        for a, part in enumerate(split(x)):
            bundle_ref[pl.ds(VALUES * a + v, LANES, stride=VALUES * ZC), :] = part

    put(0, leak + left * m3)
    put(1, right * m3)
    put(2, a3 * right)
    put(3, source + left * b3)
    put(4, right * b3)
    beta, lam, rho = b3 * i3, left, right
    back_ref[0, 2], back_ref[1, 2], back_ref[2, 2] = beta, lam, rho
    beta, lam, rho = (b2 + g3 * beta) * i2, (a2 + g3 * lam) * i2, g3 * rho * i2
    back_ref[0, 1], back_ref[1, 1], back_ref[2, 1] = beta, lam, rho
    beta, lam, rho = (b1 + g2 * beta) * i1, (g1 + g2 * lam) * i1, g2 * rho * i1
    back_ref[0, 0], back_ref[1, 0], back_ref[2, 0] = beta, lam, rho


def column_kernel(bundle_ref, out_ref):
    get = lambda v: [bundle_ref[pl.ds(VALUES * a + v, LANES, stride=VALUES * YC), :] for a in range(YC)]
    joined = lambda own, pushed: split(jnp.concatenate(own, axis=0) + before(jnp.concatenate(pushed, axis=0)))
    plan, leak, over, couple = fold(joined(get(0), get(1)), get(2))
    b, over_source = fold_sources(plan, joined(get(3), get(4)))
    factors = separator_factors(leak + shift(over, 1, 0), shift(couple, 1, 0), couple)
    head = separator_solve(factors, b[0] + shift(over_source, 1, 0))
    following = shift(head, -1, 0)
    x = unfold(plan, b, head, following) + [following]
    for a in range(YC):
        out_ref[pl.ds(2 * a, LANES, stride=2 * YC), :] = x[a]
        out_ref[pl.ds(2 * a + 1, LANES, stride=2 * YC), :] = x[a + 1]


def second_kernel(ends_ref, back_ref, spikes_ref, coeffs_ref, top_ref, second_ref, sums_ref, last_row_ref):
    get = lambda v: jnp.concatenate(
        [ends_ref[pl.ds(2 * a + v, LANES, stride=2 * ZC), :] for a in range(ZC)], axis=0)
    own, following = get(0), get(1)
    firsts, lasts = [], []
    for y in range(NB):
        if y == 0:
            u = own
        else:
            u = back_ref[0, y - 1] + back_ref[1, y - 1] * own + back_ref[2, y - 1] * following
        second_ref[y] = u
        firsts.append(jnp.sum(spikes_ref[0, y] * u, axis=0, keepdims=True))
        lasts.append(jnp.sum(spikes_ref[1, y] * u, axis=0, keepdims=True))
    first, last = jnp.concatenate(firsts, axis=0), jnp.concatenate(lasts, axis=0)
    leak, couple, top = coeffs_ref[1], coeffs_ref[2], top_ref[...]
    inverse = 1.0 / (leak + couple + top)
    left, right = couple * inverse, top * inverse
    sums_ref[0] = coeffs_ref[0] + left * leak
    sums_ref[1] = right * leak
    sums_ref[2] = left * top
    sums_ref[3] = first + left * last
    sums_ref[4] = right * last
    last_row_ref[0] = last * inverse
    last_row_ref[1] = left
    last_row_ref[2] = right


def local_z_kernel(second_ref, z_plan_ref, z_ends_ref, t_ref, out_ref):
    chunk = rows_of((LANES, NX), 0)
    for y in range(NB):
        plan = get_plan(z_plan_ref, (y,), ZC)
        b, over = fold_sources(plan, split(second_ref[y]))
        b0 = jnp.where(chunk > 0, b[0] + shift(over, 1, 0), 0.0)
        head = separator_solve([z_ends_ref[y, j] for j in range(2 * len(STRIDES) + 1)], b0)
        following = jnp.where(chunk == LANES - 1, 0.0, shift(head, -1, 0))
        x = jnp.concatenate(unfold(plan, b, head, following), axis=0)
        out_ref[y] = block_row(t_ref, y) + x


def last_kernel(local_ref, spikes_ref, last_row_ref, e0_ref, e1_ref, e2_ref, e3_ref, out_ref, line, ends):
    zg = lax.axis_index("zg")
    for j, e_ref in enumerate((e0_ref, e1_ref, e2_ref, e3_ref)):
        line[lax.bitwise_xor(zg, j)] = e_ref[...]
    inverses, sources = [], []
    leak, source = line[0, 0], line[0, 3]
    for d in range(NZG):
        couple = line[d, 2]
        inverse = 1.0 / (leak + couple)
        inverses.append(inverse)
        sources.append(source)
        if d + 1 < NZG:
            passed = couple * inverse
            leak = line[d + 1, 0] + line[d, 1] + passed * leak
            source = line[d + 1, 3] + line[d, 4] + passed * source
    value = jnp.zeros_like(source)
    ends[NZG] = value
    for d in reversed(range(NZG)):
        value = (sources[d] + line[d, 2] * value) * inverses[d]
        ends[d] = value
    own = ends[zg]
    following = last_row_ref[0] + last_row_ref[1] * own + last_row_ref[2] * ends[zg + 1]
    for y in range(NB):
        x = local_ref[y] + spikes_ref[0, y] * own[y:y + 1] + spikes_ref[1, y] * following[y:y + 1]
        for a, part in enumerate(split(x)):
            out_ref[y, pl.ds(a, LANES, stride=ZC), :] = part


def call(kernel, name, outs, args, scratch=(), cost=2000000, granted=0):
    shapes = [jax.ShapeDtypeStruct(o, jnp.float32) for o in outs]
    vmem = pl.BlockSpec(memory_space=pltpu.VMEM)
    return pl.pallas_call(
        kernel,
        name=name,
        out_shape=shapes,
        in_specs=[pl.BlockSpec(memory_space=pltpu.HBM)] * len(args) if granted else [vmem] * len(args),
        out_specs=[vmem] * len(outs),
        scratch_shapes=scratch,
        cost_estimate=pl.CostEstimate(flops=cost, bytes_accessed=cost, transcendentals=0),
        compiler_params=pltpu.CompilerParams(vmem_limit_bytes=(granted or 24576) * 1024),
    )(*args)


def swapped(x, axis, first):
    count = lax.axis_size(axis)
    partner = lambda i: ((i - first) ^ 1) + first
    return lax.ppermute(x, axis, [(i, partner(i) if 0 <= partner(i) < count else i) for i in range(count)])


def crossed(x, axis, by):
    return lax.ppermute(x, axis, [(i, i ^ by) for i in range(lax.axis_size(axis))])


def shards(t, k):
    block = (NB, NZB, NX)
    t, k, across, inside, z_even, z_odd = call(
        load_kernel, "load", [block, block, (2, NZB, NX), (2, NZB, NX), (2, NB, NX), (2, NB, NX)], [t, k],
        scratch=[pltpu.SemaphoreType.DMA((2,))], granted=LOAD_GRANT)
    across = swapped(across, "gy", 1)
    z_odd = swapped(z_odd, "zg", 1)
    z_even = swapped(z_even, "zg", 0)
    inside = swapped(inside, "gy", 0)
    turned = pltpu.VMEM((NB // 2, NX, 2 * NZB), jnp.float32)
    ends = (2 * len(STRIDES) + 1, LANES, NX)
    inner, faces, x_plan, x_ends, z_plan, z_ends, spikes, coeffs = call(
        inner_kernel, "inner",
        [block, (NB - 1, NZB, NX), (NB // 2, XC - 1, 3, LANES, 2 * NZB), (NB // 2,) + ends,
         (NB, ZC - 1, 3, LANES, NX), (NB,) + ends, (2,) + block, (3, NB, NX)], [t, k], scratch=[turned])
    bundle, back, top = call(
        first_kernel, "first", [(NZB * VALUES, NX), (3, NB - 1, NZB, NX), (NB, NX)],
        [t, k, inner, faces, x_plan, x_ends, across, inside, z_even, z_odd], scratch=[turned])
    columns = lax.all_to_all(bundle.reshape(NZB * VALUES, 1, NX), "gy", split_axis=0, concat_axis=0, tiled=True)
    (ends,) = call(column_kernel, "column", [(2 * NGY, NX)], [columns.reshape(NGY * VALUES, NX)])
    ends = lax.all_to_all(ends, "gy", split_axis=0, concat_axis=0, tiled=True)
    second, sums, last_row = call(
        second_kernel, "second", [block, (5, NB, NX), (3, NB, NX)], [ends, back, spikes, coeffs, top])
    sums = [sums] + [crossed(sums, "zg", j) for j in range(1, NZG)]
    (local,) = call(local_z_kernel, "local_z", [block], [second, z_plan, z_ends, t])
    (out,) = call(last_kernel, "last", [block], [local, spikes, last_row] + sums,
                  scratch=[pltpu.VMEM((NZG, 5, NB, NX), jnp.float32), pltpu.VMEM((NZG + 1, NB, NX), jnp.float32)])
    return out


def solution(mesh):
    return jax.shard_map(
        shards,
        mesh=mesh,
        in_specs=(P("gy", "zg", None), P("gy", "zg", None)),
        out_specs=P("gy", "zg", None),
        check_vma=False,
    )
```

```python
import jax
import jax.numpy as jnp
from jax import lax
from jax.experimental import pallas as pl
from jax.experimental.pallas import tpu as pltpu
from jax.sharding import PartitionSpec as P

mesh_courant_number = 300.0

NB, NZB, NX = 4, 64, 128
NGY, NZG = 64, 4
LANES = 8
XC, ZC, YC = NX // LANES, NZB // LANES, NGY // LANES
STRIDES = (1, 2, 4)
VALUES = 5

LOAD_GRANT = 54816


def face(k, q):
    return (2.0 * mesh_courant_number) * k * q / (k + q)


def shift(v, by, axis):
    return pltpu.roll(v, by % v.shape[axis], axis)


def rows_of(shape, axis):
    return lax.broadcasted_iota(jnp.int32, shape, axis)


def chunked(load, count):
    return jnp.concatenate([load(pl.ds(a, LANES, stride=count)) for a in range(count)], axis=0)


def split(v):
    return [v[LANES * a:LANES * (a + 1)] for a in range(v.shape[0] // LANES)]


def before(v):
    last = v.shape[0] - LANES
    return jnp.concatenate([shift(v[last:], 1, 0), v[:last]], axis=0)


def after(v):
    return jnp.concatenate([v[LANES:], shift(v[:LANES], -1, 0)], axis=0)


def order(count):
    step = 1
    while step < count:
        for a in range(step, count, 2 * step):
            yield a, step
        step *= 2


def fold(leaks, couples, closed=None):
    leaks, couples, plan, over = list(leaks), list(couples), [], 0.0
    count = len(leaks)
    for a, step in order(count):
        low, high = couples[a - step], couples[a]
        inverse = 1.0 / (leaks[a] + low + high)
        left, right = low * inverse, high * inverse
        if closed is not None and a == count - 1:
            inverse = jnp.where(closed, 0.0, inverse)
            left = jnp.where(closed, 0.0, left)
            right = jnp.where(closed, 1.0, right)
        plan.append((inverse, left, right))
        leaks[a - step] = leaks[a - step] + left * leaks[a]
        if a + step < count:
            leaks[a + step] = leaks[a + step] + right * leaks[a]
        else:
            over = over + right * leaks[a]
        couples[a - step] = low * right
    return plan, leaks[0], over, couples[0]


def fold_sources(plan, sources):
    sources, over = list(sources), 0.0
    count = len(sources)
    for (a, step), (_, left, right) in zip(order(count), plan):
        sources[a - step] = sources[a - step] + left * sources[a]
        if a + step < count:
            sources[a + step] = sources[a + step] + right * sources[a]
        else:
            over = over + right * sources[a]
    return sources, over


def unfold(plan, sources, head, following):
    count = len(plan) + 1
    x = [head] + [None] * (count - 1) + [following]
    for (a, step), (inverse, left, right) in reversed(list(zip(order(count), plan))):
        x[a] = left * x[a - step] + right * x[min(a + step, count)]
        if sources is not None:
            x[a] = x[a] + inverse * sources[a]
    return x[:count]


def put_plan(ref, at, plan):
    for i, entries in enumerate(plan):
        for j, entry in enumerate(entries):
            ref[at + (i, j)] = entry


def get_plan(ref, at, count):
    return [tuple(ref[at + (i, j)] for j in range(3)) for i in range(count - 1)]


def separator_factors(leak, low, high):
    factors = []
    for s in STRIDES:
        inverse = 1.0 / (leak + low + high)
        from_low = low * shift(inverse, s, 0)
        from_high = high * shift(inverse, -s, 0)
        factors += [from_low, from_high]
        leak = leak + from_low * shift(leak, s, 0) + from_high * shift(leak, -s, 0)
        low = from_low * shift(low, s, 0)
        high = from_high * shift(high, -s, 0)
    return factors + [1.0 / (leak + low + high)]


def separator_solve(factors, b):
    for j, s in enumerate(STRIDES):
        b = b + factors[2 * j] * shift(b, s, 0) + factors[2 * j + 1] * shift(b, -s, 0)
    return b * factors[2 * len(STRIDES)]


def load_kernel(t_hbm, k_hbm, t_ref, k_ref, across_ref, inside_ref, z_even_ref, z_odd_ref, sems):
    odd = lax.rem(lax.axis_index("gy"), 2)
    upper = lax.rem(lax.axis_index("zg"), 2) == 1
    copies = [pltpu.make_async_copy(t_hbm, t_ref, sems.at[0]), pltpu.make_async_copy(k_hbm, k_ref, sems.at[1])]
    for copy in copies:
        copy.start()
    for j, (copy, ref) in enumerate(zip(copies, (t_ref, k_ref))):
        copy.wait()
        across_ref[j] = ref[odd * (NB - 1)]
        inside_ref[j] = ref[(1 - odd) * (NB - 1)]
        for y in range(NB):
            first, last = ref[y, :1], ref[y, NZB - 1:]
            z_even_ref[j, y:y + 1] = jnp.where(upper, first, last)
            z_odd_ref[j, y:y + 1] = jnp.where(upper, last, first)


def block_row(ref, *at):
    return chunked(lambda rows: ref[at + (rows, slice(None))], ZC)


def inner_kernel(t_ref, k_ref, inner_ref, faces_ref, x_plan_ref, x_ends_ref, z_plan_ref, z_ends_ref, spikes_ref,
                 coeffs_ref, turned):
    lane = rows_of((NZB, NX), 1)
    row = rows_of((NZB, NX), 0)
    chunk = rows_of((LANES, NX), 0)
    ts = [block_row(t_ref, y) for y in range(NB)]
    ks = [block_row(k_ref, y) for y in range(NB)]
    flux_y = None
    for y in range(NB):
        k, t = ks[y], ts[y]
        low = jnp.where(lane > 0, face(k, shift(k, 1, 1)), 0.0)
        flux = low * (t - shift(t, 1, 1))
        total = shift(flux, -1, 1) - flux
        face_z = jnp.where(row > 0, face(k, before(k)), 0.0)
        flux = face_z * (t - before(t))
        total = total + (after(flux) - flux)
        if y > 0:
            total = total - flux_y
        if y < NB - 1:
            next_face = face(ks[y + 1], k)
            faces_ref[y] = next_face
            flux_y = next_face * (ts[y + 1] - t)
            total = total + flux_y
        inner_ref[y] = total

        ones = [jnp.ones((LANES, NX), jnp.float32)] * ZC
        plan, leak, over, couple = fold(ones, split(after(face_z)), chunk == LANES - 1)
        put_plan(z_plan_ref, (y,), plan)
        over = shift(over, 1, 0)
        leak_end = over[:1]
        leak = leak + jnp.where(chunk > 0, over, 0.0)
        low = shift(couple, 1, 0)
        at_first = jnp.where(chunk == 1, low, 0.0)
        at_last = jnp.where(chunk == LANES - 1, couple, 0.0)
        factors = separator_factors(leak + at_first + at_last, jnp.where(chunk > 1, low, 0.0),
                                    jnp.where((chunk > 0) & (chunk < LANES - 1), couple, 0.0))
        for j, factor in enumerate(factors):
            z_ends_ref[y, j] = factor
        lam = jnp.where(chunk == 0, 1.0, separator_solve(factors, at_first))
        rho = separator_solve(factors, at_last)
        coeffs_ref[0, y:y + 1] = jnp.sum(lam * leak, axis=0, keepdims=True)
        coeffs_ref[1, y:y + 1] = jnp.sum(rho * leak, axis=0, keepdims=True) + leak_end
        coeffs_ref[2, y:y + 1] = couple[LANES - 1:] * lam[LANES - 1:]
        following = jnp.where(chunk == LANES - 1, 0.0, shift(lam, -1, 0))
        spikes_ref[0, y] = jnp.concatenate(unfold(plan, None, lam, following), axis=0)
        following = jnp.where(chunk == LANES - 1, 1.0, shift(rho, -1, 0))
        spikes_ref[1, y] = jnp.concatenate(unfold(plan, None, rho, following), axis=0)

    for h in range(NB // 2):
        turned[h] = jnp.concatenate(ks[2 * h:2 * h + 2], axis=0).T
        k = block_line(turned, h)
        couples = face(k, after(k))
        couples = jnp.where((rows_of(couples.shape, 0) == NX - 1), 0.0, couples)
        ones = [jnp.ones((LANES, 2 * NZB), jnp.float32)] * XC
        plan, leak, over, couple = fold(ones, split(couples))
        put_plan(x_plan_ref, (h,), plan)
        factors = separator_factors(leak + shift(over, 1, 0), shift(couple, 1, 0), couple)
        for j, factor in enumerate(factors):
            x_ends_ref[h, j] = factor


def block_line(ref, h):
    return chunked(lambda rows: ref[h, rows, :], XC)


def first_kernel(t_ref, k_ref, inner_ref, faces_ref, x_plan_ref, x_ends_ref, across_ref, inside_ref, z_even_ref, z_odd_ref,
                 bundle_ref, back_ref, top_ref, turned):
    gy = lax.axis_index("gy")
    zg = lax.axis_index("zg")
    odd = lax.rem(gy, 2) == 1
    across = [block_row(across_ref, j) for j in range(2)]
    inside = [block_row(inside_ref, j) for j in range(2)]
    yp = [jnp.where(odd, b, a) for a, b in zip(across, inside)]
    yn = [jnp.where(odd, a, b) for a, b in zip(across, inside)]
    upper = lax.rem(zg, 2) == 1
    zp = jnp.where(upper, z_even_ref[...], z_odd_ref[...])
    zn = jnp.where(upper, z_odd_ref[...], z_even_ref[...])
    has_south = jnp.where(gy > 0, 1.0, 0.0)
    has_north = jnp.where(gy < NGY - 1, 1.0, 0.0)
    has_below = jnp.where(zg > 0, 1.0, 0.0)
    has_above = jnp.where(zg < NZG - 1, 1.0, 0.0)
    row = rows_of((NZB, NX), 0)
    sources = []
    g4 = None
    for y in range(NB):
        b = inner_ref[y]
        if y == 0:
            b = b + face(block_row(k_ref, y), yp[1] * has_south) * (yp[0] - block_row(t_ref, y))
        if y == NB - 1:
            g4 = face(block_row(k_ref, y), yn[1] * has_north)
            b = b + g4 * (yn[0] - block_row(t_ref, y))
        k_low, k_high = k_ref[y, :1], k_ref[y, NZB - 1:]
        below = face(k_low, zp[1, y:y + 1] * has_below) * (zp[0, y:y + 1] - t_ref[y, :1])
        top = face(k_high, zn[1, y:y + 1] * has_above)
        top_ref[y:y + 1] = top
        above = top * (zn[0, y:y + 1] - t_ref[y, NZB - 1:])
        b = b + jnp.where(row == 0, below, 0.0) + jnp.where(row == NZB - 1, above, 0.0)
        sources.append(b)
    solved = []
    for h in range(NB // 2):
        turned[h] = jnp.concatenate(sources[2 * h:2 * h + 2], axis=0).T
        plan = get_plan(x_plan_ref, (h,), XC)
        b, over = fold_sources(plan, split(block_line(turned, h)))
        head = separator_solve([x_ends_ref[h, j] for j in range(2 * len(STRIDES) + 1)], b[0] + shift(over, 1, 0))
        for a, x in enumerate(unfold(plan, b, head, shift(head, -1, 0))):
            turned[h, pl.ds(a, LANES, stride=XC), :] = x
        b = turned[h].T
        solved += [b[:NZB], b[NZB:]]
    b0, b1, b2, b3 = solved
    g1, g2, g3 = faces_ref[0], faces_ref[1], faces_ref[2]
    i1 = 1.0 / (1.0 + g1 + g2)
    left, right = g1 * i1, g2 * i1
    source = b0 + left * b1
    b2 = b2 + right * b1
    leak = 1.0 + left
    m2 = 1.0 + right
    a2 = g1 * right
    i2 = 1.0 / (m2 + a2 + g3)
    left, right = a2 * i2, g3 * i2
    source = source + left * b2
    b3 = b3 + right * b2
    leak = leak + left * m2
    m3 = 1.0 + right * m2
    a3 = a2 * right
    i3 = 1.0 / (m3 + a3 + g4)
    left, right = a3 * i3, g4 * i3

    def put(v, x):
        for a, part in enumerate(split(x)):
            bundle_ref[pl.ds(VALUES * a + v, LANES, stride=VALUES * ZC), :] = part

    put(0, leak + left * m3)
    put(1, right * m3)
    put(2, a3 * right)
    put(3, source + left * b3)
    put(4, right * b3)
    beta, lam, rho = b3 * i3, left, right
    back_ref[0, 2], back_ref[1, 2], back_ref[2, 2] = beta, lam, rho
    beta, lam, rho = (b2 + g3 * beta) * i2, (a2 + g3 * lam) * i2, g3 * rho * i2
    back_ref[0, 1], back_ref[1, 1], back_ref[2, 1] = beta, lam, rho
    beta, lam, rho = (b1 + g2 * beta) * i1, (g1 + g2 * lam) * i1, g2 * rho * i1
    back_ref[0, 0], back_ref[1, 0], back_ref[2, 0] = beta, lam, rho


def column_kernel(bundle_ref, out_ref):
    get = lambda v: [bundle_ref[pl.ds(VALUES * a + v, LANES, stride=VALUES * YC), :] for a in range(YC)]
    joined = lambda own, pushed: split(jnp.concatenate(own, axis=0) + before(jnp.concatenate(pushed, axis=0)))
    plan, leak, over, couple = fold(joined(get(0), get(1)), get(2))
    b, over_source = fold_sources(plan, joined(get(3), get(4)))
    factors = separator_factors(leak + shift(over, 1, 0), shift(couple, 1, 0), couple)
    head = separator_solve(factors, b[0] + shift(over_source, 1, 0))
    following = shift(head, -1, 0)
    x = unfold(plan, b, head, following) + [following]
    for a in range(YC):
        out_ref[pl.ds(2 * a, LANES, stride=2 * YC), :] = x[a]
        out_ref[pl.ds(2 * a + 1, LANES, stride=2 * YC), :] = x[a + 1]


def second_kernel(ends_ref, back_ref, spikes_ref, coeffs_ref, top_ref, second_ref, sums_ref, last_row_ref):
    get = lambda v: jnp.concatenate(
        [ends_ref[pl.ds(2 * a + v, LANES, stride=2 * ZC), :] for a in range(ZC)], axis=0)
    own, following = get(0), get(1)
    firsts, lasts = [], []
    for y in range(NB):
        if y == 0:
            u = own
        else:
            u = back_ref[0, y - 1] + back_ref[1, y - 1] * own + back_ref[2, y - 1] * following
        second_ref[y] = u
        firsts.append(jnp.sum(spikes_ref[0, y] * u, axis=0, keepdims=True))
        lasts.append(jnp.sum(spikes_ref[1, y] * u, axis=0, keepdims=True))
    first, last = jnp.concatenate(firsts, axis=0), jnp.concatenate(lasts, axis=0)
    leak, couple, top = coeffs_ref[1], coeffs_ref[2], top_ref[...]
    inverse = 1.0 / (leak + couple + top)
    left, right = couple * inverse, top * inverse
    sums_ref[0] = coeffs_ref[0] + left * leak
    sums_ref[1] = right * leak
    sums_ref[2] = left * top
    sums_ref[3] = first + left * last
    sums_ref[4] = right * last
    last_row_ref[0] = last * inverse
    last_row_ref[1] = left
    last_row_ref[2] = right


def local_z_kernel(second_ref, z_plan_ref, z_ends_ref, t_ref, out_ref):
    chunk = rows_of((LANES, NX), 0)
    for y in range(NB):
        plan = get_plan(z_plan_ref, (y,), ZC)
        b, over = fold_sources(plan, split(second_ref[y]))
        b0 = jnp.where(chunk > 0, b[0] + shift(over, 1, 0), 0.0)
        head = separator_solve([z_ends_ref[y, j] for j in range(2 * len(STRIDES) + 1)], b0)
        following = jnp.where(chunk == LANES - 1, 0.0, shift(head, -1, 0))
        x = jnp.concatenate(unfold(plan, b, head, following), axis=0)
        out_ref[y] = block_row(t_ref, y) + x


def last_kernel(local_ref, spikes_ref, last_row_ref, e0_ref, e1_ref, e2_ref, e3_ref, out_ref, line, ends):
    zg = lax.axis_index("zg")
    for j, e_ref in enumerate((e0_ref, e1_ref, e2_ref, e3_ref)):
        line[lax.rem(zg + (NZG - j), NZG)] = e_ref[...]
    inverses, sources = [], []
    leak, source = line[0, 0], line[0, 3]
    for d in range(NZG):
        couple = line[d, 2]
        inverse = 1.0 / (leak + couple)
        inverses.append(inverse)
        sources.append(source)
        if d + 1 < NZG:
            passed = couple * inverse
            leak = line[d + 1, 0] + line[d, 1] + passed * leak
            source = line[d + 1, 3] + line[d, 4] + passed * source
    value = jnp.zeros_like(source)
    ends[NZG] = value
    for d in reversed(range(NZG)):
        value = (sources[d] + line[d, 2] * value) * inverses[d]
        ends[d] = value
    own = ends[zg]
    following = last_row_ref[0] + last_row_ref[1] * own + last_row_ref[2] * ends[zg + 1]
    for y in range(NB):
        x = local_ref[y] + spikes_ref[0, y] * own[y:y + 1] + spikes_ref[1, y] * following[y:y + 1]
        for a, part in enumerate(split(x)):
            out_ref[y, pl.ds(a, LANES, stride=ZC), :] = part


def call(kernel, name, outs, args, scratch=(), cost=2000000, granted=0):
    shapes = [jax.ShapeDtypeStruct(o, jnp.float32) for o in outs]
    vmem = pl.BlockSpec(memory_space=pltpu.VMEM)
    return pl.pallas_call(
        kernel,
        name=name,
        out_shape=shapes,
        in_specs=[pl.BlockSpec(memory_space=pltpu.HBM)] * len(args) if granted else [vmem] * len(args),
        out_specs=[vmem] * len(outs),
        scratch_shapes=scratch,
        cost_estimate=pl.CostEstimate(flops=cost, bytes_accessed=cost, transcendentals=0),
        compiler_params=pltpu.CompilerParams(vmem_limit_bytes=(granted or 24576) * 1024),
    )(*args)


def swapped(x, axis, first):
    pairs = []
    for zg in range(NZG):
        for gy in range(NGY):
            place, count = (zg, NZG) if axis == "zg" else (gy, NGY)
            partner = ((place - first) ^ 1) + first
            if not 0 <= partner < count:
                target = (zg, gy ^ 1) if axis == "zg" else (zg ^ 1, gy)
            else:
                target = (partner, gy) if axis == "zg" else (zg, partner)
            pairs.append((zg * NGY + gy, target[0] * NGY + target[1]))
    return lax.ppermute(x, ("zg", "gy"), pairs)


def around(x, axis, by):
    count = lax.axis_size(axis)
    return lax.ppermute(x, axis, [(i, (i + by) % count) for i in range(count)])


def shards(t, k):
    block = (NB, NZB, NX)
    t, k, across, inside, z_even, z_odd = call(
        load_kernel, "load", [block, block, (2, NZB, NX), (2, NZB, NX), (2, NB, NX), (2, NB, NX)], [t, k],
        scratch=[pltpu.SemaphoreType.DMA((2,))], granted=LOAD_GRANT)
    across = swapped(across, "gy", 1)
    z_odd = swapped(z_odd, "zg", 1)
    z_even = swapped(z_even, "zg", 0)
    inside = swapped(inside, "gy", 0)
    turned = pltpu.VMEM((NB // 2, NX, 2 * NZB), jnp.float32)
    ends = (2 * len(STRIDES) + 1, LANES, NX)
    inner, faces, x_plan, x_ends, z_plan, z_ends, spikes, coeffs = call(
        inner_kernel, "inner",
        [block, (NB - 1, NZB, NX), (NB // 2, XC - 1, 3, LANES, 2 * NZB), (NB // 2,) + ends,
         (NB, ZC - 1, 3, LANES, NX), (NB,) + ends, (2,) + block, (3, NB, NX)], [t, k], scratch=[turned])
    bundle, back, top = call(
        first_kernel, "first", [(NZB * VALUES, NX), (3, NB - 1, NZB, NX), (NB, NX)],
        [t, k, inner, faces, x_plan, x_ends, across, inside, z_even, z_odd], scratch=[turned])
    columns = lax.all_to_all(bundle.reshape(NZB * VALUES, 1, NX), "gy", split_axis=0, concat_axis=0, tiled=True)
    (ends,) = call(column_kernel, "column", [(2 * NGY, NX)], [columns.reshape(NGY * VALUES, NX)])
    ends = lax.all_to_all(ends, "gy", split_axis=0, concat_axis=0, tiled=True)
    second, sums, last_row = call(
        second_kernel, "second", [block, (5, NB, NX), (3, NB, NX)], [ends, back, spikes, coeffs, top])
    sums = [sums] + [around(sums, "zg", j) for j in range(1, NZG)]
    (local,) = call(local_z_kernel, "local_z", [block], [second, z_plan, z_ends, t])
    (out,) = call(last_kernel, "last", [block], [local, spikes, last_row] + sums,
                  scratch=[pltpu.VMEM((NZG, 5, NB, NX), jnp.float32), pltpu.VMEM((NZG + 1, NB, NX), jnp.float32)])
    return out


def solution(mesh):
    return jax.shard_map(
        shards,
        mesh=mesh,
        in_specs=(P("gy", "zg", None), P("gy", "zg", None)),
        out_specs=P("gy", "zg", None),
        check_vma=False,
    )
```

```python
import jax
import jax.numpy as jnp
from jax import lax
from jax.experimental import pallas as pl
from jax.experimental.pallas import tpu as pltpu
from jax.sharding import PartitionSpec as P

mesh_courant_number = 300.0

NB, NZB, NX = 4, 64, 128
NGY, NZG = 64, 4
LANES = 8
XC, ZC, YC = NX // LANES, NZB // LANES, NGY // LANES
STRIDES = (1, 2, 4)
VALUES = 5
SHIFTS = (1, 3, 2)

LOAD_GRANT = 54816


def face(k, q):
    return (2.0 * mesh_courant_number) * k * q / (k + q)


def shift(v, by, axis):
    return pltpu.roll(v, by % v.shape[axis], axis)


def rows_of(shape, axis):
    return lax.broadcasted_iota(jnp.int32, shape, axis)


def chunked(load, count):
    return jnp.concatenate([load(pl.ds(a, LANES, stride=count)) for a in range(count)], axis=0)


def split(v):
    return [v[LANES * a:LANES * (a + 1)] for a in range(v.shape[0] // LANES)]


def before(v):
    last = v.shape[0] - LANES
    return jnp.concatenate([shift(v[last:], 1, 0), v[:last]], axis=0)


def after(v):
    return jnp.concatenate([v[LANES:], shift(v[:LANES], -1, 0)], axis=0)


def order(count):
    step = 1
    while step < count:
        for a in range(step, count, 2 * step):
            yield a, step
        step *= 2


def fold(leaks, couples, closed=None):
    leaks, couples, plan, over = list(leaks), list(couples), [], 0.0
    count = len(leaks)
    for a, step in order(count):
        low, high = couples[a - step], couples[a]
        inverse = 1.0 / (leaks[a] + low + high)
        left, right = low * inverse, high * inverse
        if closed is not None and a == count - 1:
            inverse = jnp.where(closed, 0.0, inverse)
            left = jnp.where(closed, 0.0, left)
            right = jnp.where(closed, 1.0, right)
        plan.append((inverse, left, right))
        leaks[a - step] = leaks[a - step] + left * leaks[a]
        if a + step < count:
            leaks[a + step] = leaks[a + step] + right * leaks[a]
        else:
            over = over + right * leaks[a]
        couples[a - step] = low * right
    return plan, leaks[0], over, couples[0]


def fold_sources(plan, sources):
    sources, over = list(sources), 0.0
    count = len(sources)
    for (a, step), (_, left, right) in zip(order(count), plan):
        sources[a - step] = sources[a - step] + left * sources[a]
        if a + step < count:
            sources[a + step] = sources[a + step] + right * sources[a]
        else:
            over = over + right * sources[a]
    return sources, over


def unfold(plan, sources, head, following):
    count = len(plan) + 1
    x = [head] + [None] * (count - 1) + [following]
    for (a, step), (inverse, left, right) in reversed(list(zip(order(count), plan))):
        x[a] = left * x[a - step] + right * x[min(a + step, count)]
        if sources is not None:
            x[a] = x[a] + inverse * sources[a]
    return x[:count]


def put_plan(ref, at, plan):
    for i, entries in enumerate(plan):
        for j, entry in enumerate(entries):
            ref[at + (i, j)] = entry


def get_plan(ref, at, count):
    return [tuple(ref[at + (i, j)] for j in range(3)) for i in range(count - 1)]


def separator_factors(leak, low, high):
    factors = []
    for s in STRIDES:
        inverse = 1.0 / (leak + low + high)
        from_low = low * shift(inverse, s, 0)
        from_high = high * shift(inverse, -s, 0)
        factors += [from_low, from_high]
        leak = leak + from_low * shift(leak, s, 0) + from_high * shift(leak, -s, 0)
        low = from_low * shift(low, s, 0)
        high = from_high * shift(high, -s, 0)
    return factors + [1.0 / (leak + low + high)]


def separator_solve(factors, b):
    for j, s in enumerate(STRIDES):
        b = b + factors[2 * j] * shift(b, s, 0) + factors[2 * j + 1] * shift(b, -s, 0)
    return b * factors[2 * len(STRIDES)]


def load_kernel(t_hbm, k_hbm, t_ref, k_ref, across_ref, inside_ref, z_even_ref, z_odd_ref, sems):
    odd = lax.rem(lax.axis_index("gy"), 2)
    upper = lax.rem(lax.axis_index("zg"), 2) == 1
    copies = [pltpu.make_async_copy(t_hbm, t_ref, sems.at[0]), pltpu.make_async_copy(k_hbm, k_ref, sems.at[1])]
    for copy in copies:
        copy.start()
    for j, (copy, ref) in enumerate(zip(copies, (t_ref, k_ref))):
        copy.wait()
        across_ref[j] = ref[odd * (NB - 1)]
        inside_ref[j] = ref[(1 - odd) * (NB - 1)]
        for y in range(NB):
            first, last = ref[y, :1], ref[y, NZB - 1:]
            z_even_ref[j, y:y + 1] = jnp.where(upper, first, last)
            z_odd_ref[j, y:y + 1] = jnp.where(upper, last, first)


def block_row(ref, *at):
    return chunked(lambda rows: ref[at + (rows, slice(None))], ZC)


def inner_kernel(t_ref, k_ref, inner_ref, faces_ref, x_plan_ref, x_ends_ref, z_plan_ref, z_ends_ref, spikes_ref,
                 coeffs_ref, turned):
    lane = rows_of((NZB, NX), 1)
    row = rows_of((NZB, NX), 0)
    chunk = rows_of((LANES, NX), 0)
    ts = [block_row(t_ref, y) for y in range(NB)]
    ks = [block_row(k_ref, y) for y in range(NB)]
    flux_y = None
    for y in range(NB):
        k, t = ks[y], ts[y]
        low = jnp.where(lane > 0, face(k, shift(k, 1, 1)), 0.0)
        flux = low * (t - shift(t, 1, 1))
        total = shift(flux, -1, 1) - flux
        face_z = jnp.where(row > 0, face(k, before(k)), 0.0)
        flux = face_z * (t - before(t))
        total = total + (after(flux) - flux)
        if y > 0:
            total = total - flux_y
        if y < NB - 1:
            next_face = face(ks[y + 1], k)
            faces_ref[y] = next_face
            flux_y = next_face * (ts[y + 1] - t)
            total = total + flux_y
        inner_ref[y] = total

        ones = [jnp.ones((LANES, NX), jnp.float32)] * ZC
        plan, leak, over, couple = fold(ones, split(after(face_z)), chunk == LANES - 1)
        put_plan(z_plan_ref, (y,), plan)
        over = shift(over, 1, 0)
        leak_end = over[:1]
        leak = leak + jnp.where(chunk > 0, over, 0.0)
        low = shift(couple, 1, 0)
        at_first = jnp.where(chunk == 1, low, 0.0)
        at_last = jnp.where(chunk == LANES - 1, couple, 0.0)
        factors = separator_factors(leak + at_first + at_last, jnp.where(chunk > 1, low, 0.0),
                                    jnp.where((chunk > 0) & (chunk < LANES - 1), couple, 0.0))
        for j, factor in enumerate(factors):
            z_ends_ref[y, j] = factor
        lam = jnp.where(chunk == 0, 1.0, separator_solve(factors, at_first))
        rho = separator_solve(factors, at_last)
        coeffs_ref[0, y:y + 1] = jnp.sum(lam * leak, axis=0, keepdims=True)
        coeffs_ref[1, y:y + 1] = jnp.sum(rho * leak, axis=0, keepdims=True) + leak_end
        coeffs_ref[2, y:y + 1] = couple[LANES - 1:] * lam[LANES - 1:]
        following = jnp.where(chunk == LANES - 1, 0.0, shift(lam, -1, 0))
        spikes_ref[0, y] = jnp.concatenate(unfold(plan, None, lam, following), axis=0)
        following = jnp.where(chunk == LANES - 1, 1.0, shift(rho, -1, 0))
        spikes_ref[1, y] = jnp.concatenate(unfold(plan, None, rho, following), axis=0)

    for h in range(NB // 2):
        turned[h] = jnp.concatenate(ks[2 * h:2 * h + 2], axis=0).T
        k = block_line(turned, h)
        couples = face(k, after(k))
        couples = jnp.where((rows_of(couples.shape, 0) == NX - 1), 0.0, couples)
        ones = [jnp.ones((LANES, 2 * NZB), jnp.float32)] * XC
        plan, leak, over, couple = fold(ones, split(couples))
        put_plan(x_plan_ref, (h,), plan)
        factors = separator_factors(leak + shift(over, 1, 0), shift(couple, 1, 0), couple)
        for j, factor in enumerate(factors):
            x_ends_ref[h, j] = factor


def block_line(ref, h):
    return chunked(lambda rows: ref[h, rows, :], XC)


def first_kernel(t_ref, k_ref, inner_ref, faces_ref, x_plan_ref, x_ends_ref, across_ref, inside_ref, z_even_ref, z_odd_ref,
                 bundle_ref, back_ref, top_ref, turned):
    gy = lax.axis_index("gy")
    zg = lax.axis_index("zg")
    odd = lax.rem(gy, 2) == 1
    across = [block_row(across_ref, j) for j in range(2)]
    inside = [block_row(inside_ref, j) for j in range(2)]
    yp = [jnp.where(odd, b, a) for a, b in zip(across, inside)]
    yn = [jnp.where(odd, a, b) for a, b in zip(across, inside)]
    upper = lax.rem(zg, 2) == 1
    zp = jnp.where(upper, z_even_ref[...], z_odd_ref[...])
    zn = jnp.where(upper, z_odd_ref[...], z_even_ref[...])
    has_south = jnp.where(gy > 0, 1.0, 0.0)
    has_north = jnp.where(gy < NGY - 1, 1.0, 0.0)
    has_below = jnp.where(zg > 0, 1.0, 0.0)
    has_above = jnp.where(zg < NZG - 1, 1.0, 0.0)
    row = rows_of((NZB, NX), 0)
    sources = []
    g4 = None
    for y in range(NB):
        b = inner_ref[y]
        if y == 0:
            b = b + face(block_row(k_ref, y), yp[1] * has_south) * (yp[0] - block_row(t_ref, y))
        if y == NB - 1:
            g4 = face(block_row(k_ref, y), yn[1] * has_north)
            b = b + g4 * (yn[0] - block_row(t_ref, y))
        k_low, k_high = k_ref[y, :1], k_ref[y, NZB - 1:]
        below = face(k_low, zp[1, y:y + 1] * has_below) * (zp[0, y:y + 1] - t_ref[y, :1])
        top = face(k_high, zn[1, y:y + 1] * has_above)
        top_ref[y:y + 1] = top
        above = top * (zn[0, y:y + 1] - t_ref[y, NZB - 1:])
        b = b + jnp.where(row == 0, below, 0.0) + jnp.where(row == NZB - 1, above, 0.0)
        sources.append(b)
    solved = []
    for h in range(NB // 2):
        turned[h] = jnp.concatenate(sources[2 * h:2 * h + 2], axis=0).T
        plan = get_plan(x_plan_ref, (h,), XC)
        b, over = fold_sources(plan, split(block_line(turned, h)))
        head = separator_solve([x_ends_ref[h, j] for j in range(2 * len(STRIDES) + 1)], b[0] + shift(over, 1, 0))
        for a, x in enumerate(unfold(plan, b, head, shift(head, -1, 0))):
            turned[h, pl.ds(a, LANES, stride=XC), :] = x
        b = turned[h].T
        solved += [b[:NZB], b[NZB:]]
    b0, b1, b2, b3 = solved
    g1, g2, g3 = faces_ref[0], faces_ref[1], faces_ref[2]
    i1 = 1.0 / (1.0 + g1 + g2)
    left, right = g1 * i1, g2 * i1
    source = b0 + left * b1
    b2 = b2 + right * b1
    leak = 1.0 + left
    m2 = 1.0 + right
    a2 = g1 * right
    i2 = 1.0 / (m2 + a2 + g3)
    left, right = a2 * i2, g3 * i2
    source = source + left * b2
    b3 = b3 + right * b2
    leak = leak + left * m2
    m3 = 1.0 + right * m2
    a3 = a2 * right
    i3 = 1.0 / (m3 + a3 + g4)
    left, right = a3 * i3, g4 * i3

    def put(v, x):
        for a, part in enumerate(split(x)):
            bundle_ref[pl.ds(VALUES * a + v, LANES, stride=VALUES * ZC), :] = part

    put(0, leak + left * m3)
    put(1, right * m3)
    put(2, a3 * right)
    put(3, source + left * b3)
    put(4, right * b3)
    beta, lam, rho = b3 * i3, left, right
    back_ref[0, 2], back_ref[1, 2], back_ref[2, 2] = beta, lam, rho
    beta, lam, rho = (b2 + g3 * beta) * i2, (a2 + g3 * lam) * i2, g3 * rho * i2
    back_ref[0, 1], back_ref[1, 1], back_ref[2, 1] = beta, lam, rho
    beta, lam, rho = (b1 + g2 * beta) * i1, (g1 + g2 * lam) * i1, g2 * rho * i1
    back_ref[0, 0], back_ref[1, 0], back_ref[2, 0] = beta, lam, rho


def column_kernel(bundle_ref, out_ref):
    get = lambda v: [bundle_ref[pl.ds(VALUES * a + v, LANES, stride=VALUES * YC), :] for a in range(YC)]
    joined = lambda own, pushed: split(jnp.concatenate(own, axis=0) + before(jnp.concatenate(pushed, axis=0)))
    plan, leak, over, couple = fold(joined(get(0), get(1)), get(2))
    b, over_source = fold_sources(plan, joined(get(3), get(4)))
    factors = separator_factors(leak + shift(over, 1, 0), shift(couple, 1, 0), couple)
    head = separator_solve(factors, b[0] + shift(over_source, 1, 0))
    following = shift(head, -1, 0)
    x = unfold(plan, b, head, following) + [following]
    for a in range(YC):
        out_ref[pl.ds(2 * a, LANES, stride=2 * YC), :] = x[a]
        out_ref[pl.ds(2 * a + 1, LANES, stride=2 * YC), :] = x[a + 1]


def second_kernel(ends_ref, back_ref, spikes_ref, coeffs_ref, top_ref, second_ref, sums_ref, last_row_ref):
    get = lambda v: jnp.concatenate(
        [ends_ref[pl.ds(2 * a + v, LANES, stride=2 * ZC), :] for a in range(ZC)], axis=0)
    own, following = get(0), get(1)
    firsts, lasts = [], []
    for y in range(NB):
        if y == 0:
            u = own
        else:
            u = back_ref[0, y - 1] + back_ref[1, y - 1] * own + back_ref[2, y - 1] * following
        second_ref[y] = u
        firsts.append(jnp.sum(spikes_ref[0, y] * u, axis=0, keepdims=True))
        lasts.append(jnp.sum(spikes_ref[1, y] * u, axis=0, keepdims=True))
    first, last = jnp.concatenate(firsts, axis=0), jnp.concatenate(lasts, axis=0)
    leak, couple, top = coeffs_ref[1], coeffs_ref[2], top_ref[...]
    inverse = 1.0 / (leak + couple + top)
    left, right = couple * inverse, top * inverse
    sums_ref[0] = coeffs_ref[0] + left * leak
    sums_ref[1] = right * leak
    sums_ref[2] = left * top
    sums_ref[3] = first + left * last
    sums_ref[4] = right * last
    last_row_ref[0] = last * inverse
    last_row_ref[1] = left
    last_row_ref[2] = right


def local_z_kernel(second_ref, z_plan_ref, z_ends_ref, t_ref, out_ref):
    chunk = rows_of((LANES, NX), 0)
    for y in range(NB):
        plan = get_plan(z_plan_ref, (y,), ZC)
        b, over = fold_sources(plan, split(second_ref[y]))
        b0 = jnp.where(chunk > 0, b[0] + shift(over, 1, 0), 0.0)
        head = separator_solve([z_ends_ref[y, j] for j in range(2 * len(STRIDES) + 1)], b0)
        following = jnp.where(chunk == LANES - 1, 0.0, shift(head, -1, 0))
        x = jnp.concatenate(unfold(plan, b, head, following), axis=0)
        out_ref[y] = block_row(t_ref, y) + x


def last_kernel(local_ref, spikes_ref, last_row_ref, e0_ref, e1_ref, e2_ref, e3_ref, out_ref, line, ends):
    zg = lax.axis_index("zg")
    for j, e_ref in zip((0,) + SHIFTS, (e0_ref, e1_ref, e2_ref, e3_ref)):
        line[lax.rem(zg + (NZG - j), NZG)] = e_ref[...]
    inverses, sources = [], []
    leak, source = line[0, 0], line[0, 3]
    for d in range(NZG):
        couple = line[d, 2]
        inverse = 1.0 / (leak + couple)
        inverses.append(inverse)
        sources.append(source)
        if d + 1 < NZG:
            passed = couple * inverse
            leak = line[d + 1, 0] + line[d, 1] + passed * leak
            source = line[d + 1, 3] + line[d, 4] + passed * source
    value = jnp.zeros_like(source)
    ends[NZG] = value
    for d in reversed(range(NZG)):
        value = (sources[d] + line[d, 2] * value) * inverses[d]
        ends[d] = value
    own = ends[zg]
    following = last_row_ref[0] + last_row_ref[1] * own + last_row_ref[2] * ends[zg + 1]
    for y in range(NB):
        x = local_ref[y] + spikes_ref[0, y] * own[y:y + 1] + spikes_ref[1, y] * following[y:y + 1]
        for a, part in enumerate(split(x)):
            out_ref[y, pl.ds(a, LANES, stride=ZC), :] = part


def call(kernel, name, outs, args, scratch=(), cost=2000000, granted=0):
    shapes = [jax.ShapeDtypeStruct(o, jnp.float32) for o in outs]
    vmem = pl.BlockSpec(memory_space=pltpu.VMEM)
    return pl.pallas_call(
        kernel,
        name=name,
        out_shape=shapes,
        in_specs=[pl.BlockSpec(memory_space=pltpu.HBM)] * len(args) if granted else [vmem] * len(args),
        out_specs=[vmem] * len(outs),
        scratch_shapes=scratch,
        cost_estimate=pl.CostEstimate(flops=cost, bytes_accessed=cost, transcendentals=0),
        compiler_params=pltpu.CompilerParams(vmem_limit_bytes=(granted or 24576) * 1024),
    )(*args)


def swapped(x, axis, first):
    pairs = []
    for zg in range(NZG):
        for gy in range(NGY):
            place, count = (zg, NZG) if axis == "zg" else (gy, NGY)
            partner = ((place - first) ^ 1) + first
            if not 0 <= partner < count:
                target = (zg, gy ^ 1) if axis == "zg" else (zg ^ 1, gy)
            else:
                target = (partner, gy) if axis == "zg" else (zg, partner)
            pairs.append((zg * NGY + gy, target[0] * NGY + target[1]))
    return lax.ppermute(x, ("zg", "gy"), pairs)


def around(x, axis, by):
    count = lax.axis_size(axis)
    return lax.ppermute(x, axis, [(i, (i + by) % count) for i in range(count)])


def shards(t, k):
    block = (NB, NZB, NX)
    t, k, across, inside, z_even, z_odd = call(
        load_kernel, "load", [block, block, (2, NZB, NX), (2, NZB, NX), (2, NB, NX), (2, NB, NX)], [t, k],
        scratch=[pltpu.SemaphoreType.DMA((2,))], granted=LOAD_GRANT)
    across = swapped(across, "gy", 1)
    z_odd = swapped(z_odd, "zg", 1)
    z_even = swapped(z_even, "zg", 0)
    inside = swapped(inside, "gy", 0)
    turned = pltpu.VMEM((NB // 2, NX, 2 * NZB), jnp.float32)
    ends = (2 * len(STRIDES) + 1, LANES, NX)
    inner, faces, x_plan, x_ends, z_plan, z_ends, spikes, coeffs = call(
        inner_kernel, "inner",
        [block, (NB - 1, NZB, NX), (NB // 2, XC - 1, 3, LANES, 2 * NZB), (NB // 2,) + ends,
         (NB, ZC - 1, 3, LANES, NX), (NB,) + ends, (2,) + block, (3, NB, NX)], [t, k], scratch=[turned])
    bundle, back, top = call(
        first_kernel, "first", [(NZB * VALUES, NX), (3, NB - 1, NZB, NX), (NB, NX)],
        [t, k, inner, faces, x_plan, x_ends, across, inside, z_even, z_odd], scratch=[turned])
    columns = lax.all_to_all(bundle.reshape(NZB * VALUES, 1, NX), "gy", split_axis=0, concat_axis=0, tiled=True)
    (ends,) = call(column_kernel, "column", [(2 * NGY, NX)], [columns.reshape(NGY * VALUES, NX)])
    ends = lax.all_to_all(ends, "gy", split_axis=0, concat_axis=0, tiled=True)
    second, sums, last_row = call(
        second_kernel, "second", [block, (5, NB, NX), (3, NB, NX)], [ends, back, spikes, coeffs, top])
    sums = [sums] + [around(sums, "zg", j) for j in SHIFTS]
    (local,) = call(local_z_kernel, "local_z", [block], [second, z_plan, z_ends, t])
    (out,) = call(last_kernel, "last", [block], [local, spikes, last_row] + sums,
                  scratch=[pltpu.VMEM((NZG, 5, NB, NX), jnp.float32), pltpu.VMEM((NZG + 1, NB, NX), jnp.float32)])
    return out


def solution(mesh):
    return jax.shard_map(
        shards,
        mesh=mesh,
        in_specs=(P("gy", "zg", None), P("gy", "zg", None)),
        out_specs=P("gy", "zg", None),
        check_vma=False,
    )
```

```python
import jax
import jax.numpy as jnp
from jax import lax
from jax.experimental import pallas as pl
from jax.experimental.pallas import tpu as pltpu
from jax.sharding import PartitionSpec as P

mesh_courant_number = 300.0

NB, NZB, NX = 4, 64, 128
NGY, NZG = 64, 4
LANES = 8
XC, ZC, YC = NX // LANES, NZB // LANES, NGY // LANES
STRIDES = (1, 2, 4)
VALUES = 5

LOAD_GRANT = 54816


def face(k, q):
    return (2.0 * mesh_courant_number) * k * q / (k + q)


def shift(v, by, axis):
    return pltpu.roll(v, by % v.shape[axis], axis)


def rows_of(shape, axis):
    return lax.broadcasted_iota(jnp.int32, shape, axis)


def chunked(load, count):
    return jnp.concatenate([load(pl.ds(a, LANES, stride=count)) for a in range(count)], axis=0)


def split(v):
    return [v[LANES * a:LANES * (a + 1)] for a in range(v.shape[0] // LANES)]


def before(v):
    last = v.shape[0] - LANES
    return jnp.concatenate([shift(v[last:], 1, 0), v[:last]], axis=0)


def after(v):
    return jnp.concatenate([v[LANES:], shift(v[:LANES], -1, 0)], axis=0)


def order(count):
    step = 1
    while step < count:
        for a in range(step, count, 2 * step):
            yield a, step
        step *= 2


def fold(leaks, couples, closed=None):
    leaks, couples, plan, over = list(leaks), list(couples), [], 0.0
    count = len(leaks)
    for a, step in order(count):
        low, high = couples[a - step], couples[a]
        inverse = 1.0 / (leaks[a] + low + high)
        left, right = low * inverse, high * inverse
        if closed is not None and a == count - 1:
            inverse = jnp.where(closed, 0.0, inverse)
            left = jnp.where(closed, 0.0, left)
            right = jnp.where(closed, 1.0, right)
        plan.append((inverse, left, right))
        leaks[a - step] = leaks[a - step] + left * leaks[a]
        if a + step < count:
            leaks[a + step] = leaks[a + step] + right * leaks[a]
        else:
            over = over + right * leaks[a]
        couples[a - step] = low * right
    return plan, leaks[0], over, couples[0]


def fold_sources(plan, sources):
    sources, over = list(sources), 0.0
    count = len(sources)
    for (a, step), (_, left, right) in zip(order(count), plan):
        sources[a - step] = sources[a - step] + left * sources[a]
        if a + step < count:
            sources[a + step] = sources[a + step] + right * sources[a]
        else:
            over = over + right * sources[a]
    return sources, over


def unfold(plan, sources, head, following):
    count = len(plan) + 1
    x = [head] + [None] * (count - 1) + [following]
    for (a, step), (inverse, left, right) in reversed(list(zip(order(count), plan))):
        x[a] = left * x[a - step] + right * x[min(a + step, count)]
        if sources is not None:
            x[a] = x[a] + inverse * sources[a]
    return x[:count]


def put_plan(ref, at, plan):
    for i, entries in enumerate(plan):
        for j, entry in enumerate(entries):
            ref[at + (i, j)] = entry


def get_plan(ref, at, count):
    return [tuple(ref[at + (i, j)] for j in range(3)) for i in range(count - 1)]


def separator_factors(leak, low, high):
    factors = []
    for s in STRIDES:
        inverse = 1.0 / (leak + low + high)
        from_low = low * shift(inverse, s, 0)
        from_high = high * shift(inverse, -s, 0)
        factors += [from_low, from_high]
        leak = leak + from_low * shift(leak, s, 0) + from_high * shift(leak, -s, 0)
        low = from_low * shift(low, s, 0)
        high = from_high * shift(high, -s, 0)
    return factors + [1.0 / (leak + low + high)]


def separator_solve(factors, b):
    for j, s in enumerate(STRIDES):
        b = b + factors[2 * j] * shift(b, s, 0) + factors[2 * j + 1] * shift(b, -s, 0)
    return b * factors[2 * len(STRIDES)]


def load_kernel(t_hbm, k_hbm, t_ref, k_ref, across_ref, inside_ref, z_even_ref, z_odd_ref, sems):
    odd = lax.rem(lax.axis_index("gy"), 2)
    upper = lax.rem(lax.axis_index("zg"), 2) == 1
    copies = [pltpu.make_async_copy(t_hbm, t_ref, sems.at[0]), pltpu.make_async_copy(k_hbm, k_ref, sems.at[1])]
    for copy in copies:
        copy.start()
    for j, (copy, ref) in enumerate(zip(copies, (t_ref, k_ref))):
        copy.wait()
        across_ref[j] = ref[odd * (NB - 1)]
        inside_ref[j] = ref[(1 - odd) * (NB - 1)]
        for y in range(NB):
            first, last = ref[y, :1], ref[y, NZB - 1:]
            z_even_ref[j, y:y + 1] = jnp.where(upper, first, last)
            z_odd_ref[j, y:y + 1] = jnp.where(upper, last, first)


def block_row(ref, *at):
    return chunked(lambda rows: ref[at + (rows, slice(None))], ZC)


def inner_kernel(t_ref, k_ref, inner_ref, faces_ref, x_plan_ref, x_ends_ref, z_plan_ref, z_ends_ref, spikes_ref,
                 coeffs_ref, turned):
    lane = rows_of((NZB, NX), 1)
    row = rows_of((NZB, NX), 0)
    chunk = rows_of((LANES, NX), 0)
    ts = [block_row(t_ref, y) for y in range(NB)]
    ks = [block_row(k_ref, y) for y in range(NB)]
    flux_y = None
    for y in range(NB):
        k, t = ks[y], ts[y]
        low = jnp.where(lane > 0, face(k, shift(k, 1, 1)), 0.0)
        flux = low * (t - shift(t, 1, 1))
        total = shift(flux, -1, 1) - flux
        face_z = jnp.where(row > 0, face(k, before(k)), 0.0)
        flux = face_z * (t - before(t))
        total = total + (after(flux) - flux)
        if y > 0:
            total = total - flux_y
        if y < NB - 1:
            next_face = face(ks[y + 1], k)
            faces_ref[y] = next_face
            flux_y = next_face * (ts[y + 1] - t)
            total = total + flux_y
        inner_ref[y] = total

        ones = [jnp.ones((LANES, NX), jnp.float32)] * ZC
        plan, leak, over, couple = fold(ones, split(after(face_z)), chunk == LANES - 1)
        put_plan(z_plan_ref, (y,), plan)
        over = shift(over, 1, 0)
        leak_end = over[:1]
        leak = leak + jnp.where(chunk > 0, over, 0.0)
        low = shift(couple, 1, 0)
        at_first = jnp.where(chunk == 1, low, 0.0)
        at_last = jnp.where(chunk == LANES - 1, couple, 0.0)
        factors = separator_factors(leak + at_first + at_last, jnp.where(chunk > 1, low, 0.0),
                                    jnp.where((chunk > 0) & (chunk < LANES - 1), couple, 0.0))
        for j, factor in enumerate(factors):
            z_ends_ref[y, j] = factor
        lam = jnp.where(chunk == 0, 1.0, separator_solve(factors, at_first))
        rho = separator_solve(factors, at_last)
        coeffs_ref[0, y:y + 1] = jnp.sum(lam * leak, axis=0, keepdims=True)
        coeffs_ref[1, y:y + 1] = jnp.sum(rho * leak, axis=0, keepdims=True) + leak_end
        coeffs_ref[2, y:y + 1] = couple[LANES - 1:] * lam[LANES - 1:]
        following = jnp.where(chunk == LANES - 1, 0.0, shift(lam, -1, 0))
        spikes_ref[0, y] = jnp.concatenate(unfold(plan, None, lam, following), axis=0)
        following = jnp.where(chunk == LANES - 1, 1.0, shift(rho, -1, 0))
        spikes_ref[1, y] = jnp.concatenate(unfold(plan, None, rho, following), axis=0)

    for h in range(NB // 2):
        turned[h] = jnp.concatenate(ks[2 * h:2 * h + 2], axis=0).T
        k = block_line(turned, h)
        couples = face(k, after(k))
        couples = jnp.where((rows_of(couples.shape, 0) == NX - 1), 0.0, couples)
        ones = [jnp.ones((LANES, 2 * NZB), jnp.float32)] * XC
        plan, leak, over, couple = fold(ones, split(couples))
        put_plan(x_plan_ref, (h,), plan)
        factors = separator_factors(leak + shift(over, 1, 0), shift(couple, 1, 0), couple)
        for j, factor in enumerate(factors):
            x_ends_ref[h, j] = factor


def block_line(ref, h):
    return chunked(lambda rows: ref[h, rows, :], XC)


def first_kernel(t_ref, k_ref, inner_ref, faces_ref, x_plan_ref, x_ends_ref, across_ref, inside_ref, z_even_ref, z_odd_ref,
                 bundle_ref, back_ref, top_ref, turned):
    gy = lax.axis_index("gy")
    zg = lax.axis_index("zg")
    odd = lax.rem(gy, 2) == 1
    across = [block_row(across_ref, j) for j in range(2)]
    inside = [block_row(inside_ref, j) for j in range(2)]
    yp = [jnp.where(odd, b, a) for a, b in zip(across, inside)]
    yn = [jnp.where(odd, a, b) for a, b in zip(across, inside)]
    upper = lax.rem(zg, 2) == 1
    zp = jnp.where(upper, z_even_ref[...], z_odd_ref[...])
    zn = jnp.where(upper, z_odd_ref[...], z_even_ref[...])
    has_south = jnp.where(gy > 0, 1.0, 0.0)
    has_north = jnp.where(gy < NGY - 1, 1.0, 0.0)
    has_below = jnp.where(zg > 0, 1.0, 0.0)
    has_above = jnp.where(zg < NZG - 1, 1.0, 0.0)
    row = rows_of((NZB, NX), 0)
    sources = []
    g4 = None
    for y in range(NB):
        b = inner_ref[y]
        if y == 0:
            b = b + face(block_row(k_ref, y), yp[1] * has_south) * (yp[0] - block_row(t_ref, y))
        if y == NB - 1:
            g4 = face(block_row(k_ref, y), yn[1] * has_north)
            b = b + g4 * (yn[0] - block_row(t_ref, y))
        k_low, k_high = k_ref[y, :1], k_ref[y, NZB - 1:]
        below = face(k_low, zp[1, y:y + 1] * has_below) * (zp[0, y:y + 1] - t_ref[y, :1])
        top = face(k_high, zn[1, y:y + 1] * has_above)
        top_ref[y:y + 1] = top
        above = top * (zn[0, y:y + 1] - t_ref[y, NZB - 1:])
        b = b + jnp.where(row == 0, below, 0.0) + jnp.where(row == NZB - 1, above, 0.0)
        sources.append(b)
    solved = []
    for h in range(NB // 2):
        turned[h] = jnp.concatenate(sources[2 * h:2 * h + 2], axis=0).T
        plan = get_plan(x_plan_ref, (h,), XC)
        b, over = fold_sources(plan, split(block_line(turned, h)))
        head = separator_solve([x_ends_ref[h, j] for j in range(2 * len(STRIDES) + 1)], b[0] + shift(over, 1, 0))
        for a, x in enumerate(unfold(plan, b, head, shift(head, -1, 0))):
            turned[h, pl.ds(a, LANES, stride=XC), :] = x
        b = turned[h].T
        solved += [b[:NZB], b[NZB:]]
    b0, b1, b2, b3 = solved
    g1, g2, g3 = faces_ref[0], faces_ref[1], faces_ref[2]
    i1 = 1.0 / (1.0 + g1 + g2)
    left, right = g1 * i1, g2 * i1
    source = b0 + left * b1
    b2 = b2 + right * b1
    leak = 1.0 + left
    m2 = 1.0 + right
    a2 = g1 * right
    i2 = 1.0 / (m2 + a2 + g3)
    left, right = a2 * i2, g3 * i2
    source = source + left * b2
    b3 = b3 + right * b2
    leak = leak + left * m2
    m3 = 1.0 + right * m2
    a3 = a2 * right
    i3 = 1.0 / (m3 + a3 + g4)
    left, right = a3 * i3, g4 * i3

    def put(v, x):
        for a, part in enumerate(split(x)):
            bundle_ref[pl.ds(VALUES * a + v, LANES, stride=VALUES * ZC), :] = part

    put(0, leak + left * m3)
    put(1, right * m3)
    put(2, a3 * right)
    put(3, source + left * b3)
    put(4, right * b3)
    beta, lam, rho = b3 * i3, left, right
    back_ref[0, 2], back_ref[1, 2], back_ref[2, 2] = beta, lam, rho
    beta, lam, rho = (b2 + g3 * beta) * i2, (a2 + g3 * lam) * i2, g3 * rho * i2
    back_ref[0, 1], back_ref[1, 1], back_ref[2, 1] = beta, lam, rho
    beta, lam, rho = (b1 + g2 * beta) * i1, (g1 + g2 * lam) * i1, g2 * rho * i1
    back_ref[0, 0], back_ref[1, 0], back_ref[2, 0] = beta, lam, rho


def column_kernel(bundle_ref, out_ref):
    get = lambda v: [bundle_ref[pl.ds(VALUES * a + v, LANES, stride=VALUES * YC), :] for a in range(YC)]
    joined = lambda own, pushed: split(jnp.concatenate(own, axis=0) + before(jnp.concatenate(pushed, axis=0)))
    plan, leak, over, couple = fold(joined(get(0), get(1)), get(2))
    b, over_source = fold_sources(plan, joined(get(3), get(4)))
    factors = separator_factors(leak + shift(over, 1, 0), shift(couple, 1, 0), couple)
    head = separator_solve(factors, b[0] + shift(over_source, 1, 0))
    following = shift(head, -1, 0)
    x = unfold(plan, b, head, following) + [following]
    for a in range(YC):
        out_ref[pl.ds(2 * a, LANES, stride=2 * YC), :] = x[a]
        out_ref[pl.ds(2 * a + 1, LANES, stride=2 * YC), :] = x[a + 1]


def second_kernel(ends_ref, back_ref, spikes_ref, coeffs_ref, top_ref, second_ref, sums_ref, last_row_ref):
    get = lambda v: jnp.concatenate(
        [ends_ref[pl.ds(2 * a + v, LANES, stride=2 * ZC), :] for a in range(ZC)], axis=0)
    own, following = get(0), get(1)
    firsts, lasts = [], []
    for y in range(NB):
        if y == 0:
            u = own
        else:
            u = back_ref[0, y - 1] + back_ref[1, y - 1] * own + back_ref[2, y - 1] * following
        second_ref[y] = u
        firsts.append(jnp.sum(spikes_ref[0, y] * u, axis=0, keepdims=True))
        lasts.append(jnp.sum(spikes_ref[1, y] * u, axis=0, keepdims=True))
    first, last = jnp.concatenate(firsts, axis=0), jnp.concatenate(lasts, axis=0)
    leak, couple, top = coeffs_ref[1], coeffs_ref[2], top_ref[...]
    inverse = 1.0 / (leak + couple + top)
    left, right = couple * inverse, top * inverse
    sums = (coeffs_ref[0] + left * leak, right * leak, left * top, first + left * last, right * last)
    for d in range(NZG):
        for j, entry in enumerate(sums):
            sums_ref[VALUES * d + j] = entry
    last_row_ref[0] = last * inverse
    last_row_ref[1] = left
    last_row_ref[2] = right


def local_z(second, plan, factors):
    chunk = rows_of((LANES, NX), 0)
    b, over = fold_sources(plan, split(second))
    head = separator_solve(factors, jnp.where(chunk > 0, b[0] + shift(over, 1, 0), 0.0))
    following = jnp.where(chunk == LANES - 1, 0.0, shift(head, -1, 0))
    return jnp.concatenate(unfold(plan, b, head, following), axis=0)


def last_kernel(t_ref, second_ref, z_plan_ref, z_ends_ref, spikes_ref, last_row_ref, line_ref, out_ref, ends):
    zg = lax.axis_index("zg")
    line = [[line_ref[VALUES * d + j] for j in range(VALUES)] for d in range(NZG)]
    inverses, sources = [], []
    leak, source = line[0][0], line[0][3]
    for d in range(NZG):
        couple = line[d][2]
        inverse = 1.0 / (leak + couple)
        inverses.append(inverse)
        sources.append(source)
        if d + 1 < NZG:
            passed = couple * inverse
            leak = line[d + 1][0] + line[d][1] + passed * leak
            source = line[d + 1][3] + line[d][4] + passed * source
    value = jnp.zeros_like(source)
    ends[NZG] = value
    for d in reversed(range(NZG)):
        value = (sources[d] + line[d][2] * value) * inverses[d]
        ends[d] = value
    own = ends[zg]
    following = last_row_ref[0] + last_row_ref[1] * own + last_row_ref[2] * ends[zg + 1]
    for y in range(NB):
        x = local_z(second_ref[y], get_plan(z_plan_ref, (y,), ZC),
                    [z_ends_ref[y, j] for j in range(2 * len(STRIDES) + 1)])
        x = block_row(t_ref, y) + x
        x = x + spikes_ref[0, y] * own[y:y + 1] + spikes_ref[1, y] * following[y:y + 1]
        for a, part in enumerate(split(x)):
            out_ref[y, pl.ds(a, LANES, stride=ZC), :] = part


def call(kernel, name, outs, args, scratch=(), cost=2000000, granted=0):
    shapes = [jax.ShapeDtypeStruct(o, jnp.float32) for o in outs]
    vmem = pl.BlockSpec(memory_space=pltpu.VMEM)
    return pl.pallas_call(
        kernel,
        name=name,
        out_shape=shapes,
        in_specs=[pl.BlockSpec(memory_space=pltpu.HBM)] * len(args) if granted else [vmem] * len(args),
        out_specs=[vmem] * len(outs),
        scratch_shapes=scratch,
        cost_estimate=pl.CostEstimate(flops=cost, bytes_accessed=cost, transcendentals=0),
        compiler_params=pltpu.CompilerParams(vmem_limit_bytes=(granted or 24576) * 1024),
    )(*args)


def swapped(x, axis, first):
    pairs = []
    for zg in range(NZG):
        for gy in range(NGY):
            place, count = (zg, NZG) if axis == "zg" else (gy, NGY)
            partner = ((place - first) ^ 1) + first
            if not 0 <= partner < count:
                target = (zg, gy ^ 1) if axis == "zg" else (zg ^ 1, gy)
            else:
                target = (partner, gy) if axis == "zg" else (zg, partner)
            pairs.append((zg * NGY + gy, target[0] * NGY + target[1]))
    return lax.ppermute(x, ("zg", "gy"), pairs)


def shards(t, k):
    block = (NB, NZB, NX)
    t, k, across, inside, z_even, z_odd = call(
        load_kernel, "load", [block, block, (2, NZB, NX), (2, NZB, NX), (2, NB, NX), (2, NB, NX)], [t, k],
        scratch=[pltpu.SemaphoreType.DMA((2,))], granted=LOAD_GRANT)
    across = swapped(across, "gy", 1)
    z_odd = swapped(z_odd, "zg", 1)
    z_even = swapped(z_even, "zg", 0)
    inside = swapped(inside, "gy", 0)
    turned = pltpu.VMEM((NB // 2, NX, 2 * NZB), jnp.float32)
    ends = (2 * len(STRIDES) + 1, LANES, NX)
    inner, faces, x_plan, x_ends, z_plan, z_ends, spikes, coeffs = call(
        inner_kernel, "inner",
        [block, (NB - 1, NZB, NX), (NB // 2, XC - 1, 3, LANES, 2 * NZB), (NB // 2,) + ends,
         (NB, ZC - 1, 3, LANES, NX), (NB,) + ends, (2,) + block, (3, NB, NX)], [t, k], scratch=[turned])
    bundle, back, top = call(
        first_kernel, "first", [(NZB * VALUES, NX), (3, NB - 1, NZB, NX), (NB, NX)],
        [t, k, inner, faces, x_plan, x_ends, across, inside, z_even, z_odd], scratch=[turned])
    columns = lax.all_to_all(bundle.reshape(NZB * VALUES, 1, NX), "gy", split_axis=0, concat_axis=0, tiled=True)
    (ends,) = call(column_kernel, "column", [(2 * NGY, NX)], [columns.reshape(NGY * VALUES, NX)])
    ends = lax.all_to_all(ends, "gy", split_axis=0, concat_axis=0, tiled=True)
    second, sums, last_row = call(
        second_kernel, "second", [block, (NZG * VALUES, NB, NX), (3, NB, NX)], [ends, back, spikes, coeffs, top])
    line = lax.all_to_all(sums, "zg", split_axis=0, concat_axis=0, tiled=True)
    (out,) = call(last_kernel, "last", [block], [t, second, z_plan, z_ends, spikes, last_row, line],
                  scratch=[pltpu.VMEM((NZG + 1, NB, NX), jnp.float32)])
    return out


def solution(mesh):
    return jax.shard_map(
        shards,
        mesh=mesh,
        in_specs=(P("gy", "zg", None), P("gy", "zg", None)),
        out_specs=P("gy", "zg", None),
        check_vma=False,
    )
```

```python
import jax
import jax.numpy as jnp
from jax import lax
from jax.experimental import pallas as pl
from jax.experimental.pallas import tpu as pltpu
from jax.sharding import PartitionSpec as P

mesh_courant_number = 300.0

NB, NZB, NX = 4, 64, 128
NGY, NZG = 64, 4
LANES = 8
XC, ZC, YC = NX // LANES, NZB // LANES, NGY // LANES
STRIDES = (1, 2, 4)
VALUES = 5

LOAD_GRANT = 54816


def face(k, q):
    return (2.0 * mesh_courant_number) * k * q / (k + q)


def shift(v, by, axis):
    return pltpu.roll(v, by % v.shape[axis], axis)


def rows_of(shape, axis):
    return lax.broadcasted_iota(jnp.int32, shape, axis)


def chunked(load, count):
    return jnp.concatenate([load(pl.ds(a, LANES, stride=count)) for a in range(count)], axis=0)


def split(v):
    return [v[LANES * a:LANES * (a + 1)] for a in range(v.shape[0] // LANES)]


def before(v):
    last = v.shape[0] - LANES
    return jnp.concatenate([shift(v[last:], 1, 0), v[:last]], axis=0)


def after(v):
    return jnp.concatenate([v[LANES:], shift(v[:LANES], -1, 0)], axis=0)


def order(count):
    step = 1
    while step < count:
        for a in range(step, count, 2 * step):
            yield a, step
        step *= 2


def fold(leaks, couples, closed=None):
    leaks, couples, plan, over = list(leaks), list(couples), [], 0.0
    count = len(leaks)
    for a, step in order(count):
        low, high = couples[a - step], couples[a]
        inverse = 1.0 / (leaks[a] + low + high)
        left, right = low * inverse, high * inverse
        if closed is not None and a == count - 1:
            inverse = jnp.where(closed, 0.0, inverse)
            left = jnp.where(closed, 0.0, left)
            right = jnp.where(closed, 1.0, right)
        plan.append((inverse, left, right))
        leaks[a - step] = leaks[a - step] + left * leaks[a]
        if a + step < count:
            leaks[a + step] = leaks[a + step] + right * leaks[a]
        else:
            over = over + right * leaks[a]
        couples[a - step] = low * right
    return plan, leaks[0], over, couples[0]


def fold_sources(plan, sources):
    sources, over = list(sources), 0.0
    count = len(sources)
    for (a, step), (_, left, right) in zip(order(count), plan):
        sources[a - step] = sources[a - step] + left * sources[a]
        if a + step < count:
            sources[a + step] = sources[a + step] + right * sources[a]
        else:
            over = over + right * sources[a]
    return sources, over


def unfold(plan, sources, head, following):
    count = len(plan) + 1
    x = [head] + [None] * (count - 1) + [following]
    for (a, step), (inverse, left, right) in reversed(list(zip(order(count), plan))):
        x[a] = left * x[a - step] + right * x[min(a + step, count)]
        if sources is not None:
            x[a] = x[a] + inverse * sources[a]
    return x[:count]


def put_plan(ref, at, plan):
    for i, entries in enumerate(plan):
        for j, entry in enumerate(entries):
            ref[at + (i, j)] = entry


def get_plan(ref, at, count):
    return [tuple(ref[at + (i, j)] for j in range(3)) for i in range(count - 1)]


def separator_factors(leak, low, high):
    factors = []
    for s in STRIDES:
        inverse = 1.0 / (leak + low + high)
        from_low = low * shift(inverse, s, 0)
        from_high = high * shift(inverse, -s, 0)
        factors += [from_low, from_high]
        leak = leak + from_low * shift(leak, s, 0) + from_high * shift(leak, -s, 0)
        low = from_low * shift(low, s, 0)
        high = from_high * shift(high, -s, 0)
    return factors + [1.0 / (leak + low + high)]


def separator_solve(factors, b):
    for j, s in enumerate(STRIDES):
        b = b + factors[2 * j] * shift(b, s, 0) + factors[2 * j + 1] * shift(b, -s, 0)
    return b * factors[2 * len(STRIDES)]


def load_kernel(t_hbm, k_hbm, t_ref, k_ref, across_ref, inside_ref, z_even_ref, z_odd_ref, sems):
    odd = lax.rem(lax.axis_index("gy"), 2)
    upper = lax.rem(lax.axis_index("zg"), 2) == 1
    copies = [pltpu.make_async_copy(t_hbm, t_ref, sems.at[0]), pltpu.make_async_copy(k_hbm, k_ref, sems.at[1])]
    for copy in copies:
        copy.start()
    for j, (copy, ref) in enumerate(zip(copies, (t_ref, k_ref))):
        copy.wait()
        across_ref[j] = ref[odd * (NB - 1)]
        inside_ref[j] = ref[(1 - odd) * (NB - 1)]
        for y in range(NB):
            first, last = ref[y, :1], ref[y, NZB - 1:]
            z_even_ref[j, y:y + 1] = jnp.where(upper, first, last)
            z_odd_ref[j, y:y + 1] = jnp.where(upper, last, first)


def block_row(ref, *at):
    return chunked(lambda rows: ref[at + (rows, slice(None))], ZC)


def inner_kernel(t_ref, k_ref, inner_ref, faces_ref, x_plan_ref, x_ends_ref, z_plan_ref, z_ends_ref, spikes_ref,
                 coeffs_ref, turned):
    lane = rows_of((NZB, NX), 1)
    row = rows_of((NZB, NX), 0)
    chunk = rows_of((LANES, NX), 0)
    ts = [block_row(t_ref, y) for y in range(NB)]
    ks = [block_row(k_ref, y) for y in range(NB)]
    flux_y = None
    for y in range(NB):
        k, t = ks[y], ts[y]
        low = jnp.where(lane > 0, face(k, shift(k, 1, 1)), 0.0)
        flux = low * (t - shift(t, 1, 1))
        total = shift(flux, -1, 1) - flux
        face_z = jnp.where(row > 0, face(k, before(k)), 0.0)
        flux = face_z * (t - before(t))
        total = total + (after(flux) - flux)
        if y > 0:
            total = total - flux_y
        if y < NB - 1:
            next_face = face(ks[y + 1], k)
            faces_ref[y] = next_face
            flux_y = next_face * (ts[y + 1] - t)
            total = total + flux_y
        inner_ref[y] = total

        ones = [jnp.ones((LANES, NX), jnp.float32)] * ZC
        plan, leak, over, couple = fold(ones, split(after(face_z)), chunk == LANES - 1)
        put_plan(z_plan_ref, (y,), plan)
        over = shift(over, 1, 0)
        leak_end = over[:1]
        leak = leak + jnp.where(chunk > 0, over, 0.0)
        low = shift(couple, 1, 0)
        at_first = jnp.where(chunk == 1, low, 0.0)
        at_last = jnp.where(chunk == LANES - 1, couple, 0.0)
        factors = separator_factors(leak + at_first + at_last, jnp.where(chunk > 1, low, 0.0),
                                    jnp.where((chunk > 0) & (chunk < LANES - 1), couple, 0.0))
        for j, factor in enumerate(factors):
            z_ends_ref[y, j] = factor
        lam = jnp.where(chunk == 0, 1.0, separator_solve(factors, at_first))
        rho = separator_solve(factors, at_last)
        coeffs_ref[0, y:y + 1] = jnp.sum(lam * leak, axis=0, keepdims=True)
        coeffs_ref[1, y:y + 1] = jnp.sum(rho * leak, axis=0, keepdims=True) + leak_end
        coeffs_ref[2, y:y + 1] = couple[LANES - 1:] * lam[LANES - 1:]
        following = jnp.where(chunk == LANES - 1, 0.0, shift(lam, -1, 0))
        spikes_ref[0, y] = jnp.concatenate(unfold(plan, None, lam, following), axis=0)
        following = jnp.where(chunk == LANES - 1, 1.0, shift(rho, -1, 0))
        spikes_ref[1, y] = jnp.concatenate(unfold(plan, None, rho, following), axis=0)

    for h in range(NB // 2):
        turned[h] = jnp.concatenate(ks[2 * h:2 * h + 2], axis=0).T
        k = block_line(turned, h)
        couples = face(k, after(k))
        couples = jnp.where((rows_of(couples.shape, 0) == NX - 1), 0.0, couples)
        ones = [jnp.ones((LANES, 2 * NZB), jnp.float32)] * XC
        plan, leak, over, couple = fold(ones, split(couples))
        put_plan(x_plan_ref, (h,), plan)
        factors = separator_factors(leak + shift(over, 1, 0), shift(couple, 1, 0), couple)
        for j, factor in enumerate(factors):
            x_ends_ref[h, j] = factor


def block_line(ref, h):
    return chunked(lambda rows: ref[h, rows, :], XC)


def first_kernel(t_ref, k_ref, inner_ref, faces_ref, x_plan_ref, x_ends_ref, across_ref, inside_ref, z_even_ref, z_odd_ref,
                 bundle_ref, back_ref, top_ref, turned):
    gy = lax.axis_index("gy")
    zg = lax.axis_index("zg")
    odd = lax.rem(gy, 2) == 1
    across = [block_row(across_ref, j) for j in range(2)]
    inside = [block_row(inside_ref, j) for j in range(2)]
    yp = [jnp.where(odd, b, a) for a, b in zip(across, inside)]
    yn = [jnp.where(odd, a, b) for a, b in zip(across, inside)]
    upper = lax.rem(zg, 2) == 1
    zp = jnp.where(upper, z_even_ref[...], z_odd_ref[...])
    zn = jnp.where(upper, z_odd_ref[...], z_even_ref[...])
    has_south = jnp.where(gy > 0, 1.0, 0.0)
    has_north = jnp.where(gy < NGY - 1, 1.0, 0.0)
    has_below = jnp.where(zg > 0, 1.0, 0.0)
    has_above = jnp.where(zg < NZG - 1, 1.0, 0.0)
    row = rows_of((NZB, NX), 0)
    sources = []
    g4 = None
    for y in range(NB):
        b = inner_ref[y]
        if y == 0:
            b = b + face(block_row(k_ref, y), yp[1] * has_south) * (yp[0] - block_row(t_ref, y))
        if y == NB - 1:
            g4 = face(block_row(k_ref, y), yn[1] * has_north)
            b = b + g4 * (yn[0] - block_row(t_ref, y))
        k_low, k_high = k_ref[y, :1], k_ref[y, NZB - 1:]
        below = face(k_low, zp[1, y:y + 1] * has_below) * (zp[0, y:y + 1] - t_ref[y, :1])
        top = face(k_high, zn[1, y:y + 1] * has_above)
        top_ref[y:y + 1] = top
        above = top * (zn[0, y:y + 1] - t_ref[y, NZB - 1:])
        b = b + jnp.where(row == 0, below, 0.0) + jnp.where(row == NZB - 1, above, 0.0)
        sources.append(b)
    solved = []
    for h in range(NB // 2):
        turned[h] = jnp.concatenate(sources[2 * h:2 * h + 2], axis=0).T
        plan = get_plan(x_plan_ref, (h,), XC)
        b, over = fold_sources(plan, split(block_line(turned, h)))
        head = separator_solve([x_ends_ref[h, j] for j in range(2 * len(STRIDES) + 1)], b[0] + shift(over, 1, 0))
        for a, x in enumerate(unfold(plan, b, head, shift(head, -1, 0))):
            turned[h, pl.ds(a, LANES, stride=XC), :] = x
        b = turned[h].T
        solved += [b[:NZB], b[NZB:]]
    b0, b1, b2, b3 = solved
    g1, g2, g3 = faces_ref[0], faces_ref[1], faces_ref[2]
    i1 = 1.0 / (1.0 + g1 + g2)
    left, right = g1 * i1, g2 * i1
    source = b0 + left * b1
    b2 = b2 + right * b1
    leak = 1.0 + left
    m2 = 1.0 + right
    a2 = g1 * right
    i2 = 1.0 / (m2 + a2 + g3)
    left, right = a2 * i2, g3 * i2
    source = source + left * b2
    b3 = b3 + right * b2
    leak = leak + left * m2
    m3 = 1.0 + right * m2
    a3 = a2 * right
    i3 = 1.0 / (m3 + a3 + g4)
    left, right = a3 * i3, g4 * i3

    def put(v, x):
        for a, part in enumerate(split(x)):
            bundle_ref[pl.ds(VALUES * a + v, LANES, stride=VALUES * ZC), :] = part

    put(0, leak + left * m3)
    put(1, right * m3)
    put(2, a3 * right)
    put(3, source + left * b3)
    put(4, right * b3)
    beta, lam, rho = b3 * i3, left, right
    back_ref[0, 2], back_ref[1, 2], back_ref[2, 2] = beta, lam, rho
    beta, lam, rho = (b2 + g3 * beta) * i2, (a2 + g3 * lam) * i2, g3 * rho * i2
    back_ref[0, 1], back_ref[1, 1], back_ref[2, 1] = beta, lam, rho
    beta, lam, rho = (b1 + g2 * beta) * i1, (g1 + g2 * lam) * i1, g2 * rho * i1
    back_ref[0, 0], back_ref[1, 0], back_ref[2, 0] = beta, lam, rho


def column_kernel(bundle_ref, out_ref):
    get = lambda v: [bundle_ref[pl.ds(VALUES * a + v, LANES, stride=VALUES * YC), :] for a in range(YC)]
    joined = lambda own, pushed: split(jnp.concatenate(own, axis=0) + before(jnp.concatenate(pushed, axis=0)))
    plan, leak, over, couple = fold(joined(get(0), get(1)), get(2))
    b, over_source = fold_sources(plan, joined(get(3), get(4)))
    factors = separator_factors(leak + shift(over, 1, 0), shift(couple, 1, 0), couple)
    head = separator_solve(factors, b[0] + shift(over_source, 1, 0))
    following = shift(head, -1, 0)
    x = unfold(plan, b, head, following) + [following]
    for a in range(YC):
        out_ref[pl.ds(2 * a, LANES, stride=2 * YC), :] = x[a]
        out_ref[pl.ds(2 * a + 1, LANES, stride=2 * YC), :] = x[a + 1]


def second_kernel(ends_ref, back_ref, spikes_ref, coeffs_ref, top_ref, second_ref, sums_ref, last_row_ref):
    get = lambda v: jnp.concatenate(
        [ends_ref[pl.ds(2 * a + v, LANES, stride=2 * ZC), :] for a in range(ZC)], axis=0)
    own, following = get(0), get(1)
    firsts, lasts = [], []
    for y in range(NB):
        if y == 0:
            u = own
        else:
            u = back_ref[0, y - 1] + back_ref[1, y - 1] * own + back_ref[2, y - 1] * following
        second_ref[y] = u
        firsts.append(jnp.sum(spikes_ref[0, y] * u, axis=0, keepdims=True))
        lasts.append(jnp.sum(spikes_ref[1, y] * u, axis=0, keepdims=True))
    first, last = jnp.concatenate(firsts, axis=0), jnp.concatenate(lasts, axis=0)
    leak, couple, top = coeffs_ref[1], coeffs_ref[2], top_ref[...]
    inverse = 1.0 / (leak + couple + top)
    left, right = couple * inverse, top * inverse
    sums_ref[0] = coeffs_ref[0] + left * leak
    sums_ref[1] = right * leak
    sums_ref[2] = left * top
    sums_ref[3] = first + left * last
    sums_ref[4] = right * last
    last_row_ref[0] = last * inverse
    last_row_ref[1] = left
    last_row_ref[2] = right


def local_z_kernel(second_ref, z_plan_ref, z_ends_ref, t_ref, out_ref):
    chunk = rows_of((LANES, NX), 0)
    for y in range(NB):
        plan = get_plan(z_plan_ref, (y,), ZC)
        b, over = fold_sources(plan, split(second_ref[y]))
        b0 = jnp.where(chunk > 0, b[0] + shift(over, 1, 0), 0.0)
        head = separator_solve([z_ends_ref[y, j] for j in range(2 * len(STRIDES) + 1)], b0)
        following = jnp.where(chunk == LANES - 1, 0.0, shift(head, -1, 0))
        x = jnp.concatenate(unfold(plan, b, head, following), axis=0)
        out_ref[y] = block_row(t_ref, y) + x


def last_kernel(local_ref, spikes_ref, last_row_ref, e0_ref, e1_ref, e2_ref, e3_ref, out_ref, line, ends):
    zg = lax.axis_index("zg")
    for j, e_ref in enumerate((e0_ref, e1_ref, e2_ref, e3_ref)):
        line[lax.bitwise_xor(zg, j)] = e_ref[...]
    inverses, sources = [], []
    leak, source = line[0, 0], line[0, 3]
    for d in range(NZG):
        couple = line[d, 2]
        inverse = 1.0 / (leak + couple)
        inverses.append(inverse)
        sources.append(source)
        if d + 1 < NZG:
            passed = couple * inverse
            leak = line[d + 1, 0] + line[d, 1] + passed * leak
            source = line[d + 1, 3] + line[d, 4] + passed * source
    value = jnp.zeros_like(source)
    ends[NZG] = value
    for d in reversed(range(NZG)):
        value = (sources[d] + line[d, 2] * value) * inverses[d]
        ends[d] = value
    own = ends[zg]
    following = last_row_ref[0] + last_row_ref[1] * own + last_row_ref[2] * ends[zg + 1]
    for y in range(NB):
        x = local_ref[y] + spikes_ref[0, y] * own[y:y + 1] + spikes_ref[1, y] * following[y:y + 1]
        for a, part in enumerate(split(x)):
            out_ref[y, pl.ds(a, LANES, stride=ZC), :] = part


def call(kernel, name, outs, args, scratch=(), cost=2000000, granted=0):
    shapes = [jax.ShapeDtypeStruct(o, jnp.float32) for o in outs]
    vmem = pl.BlockSpec(memory_space=pltpu.VMEM)
    return pl.pallas_call(
        kernel,
        name=name,
        out_shape=shapes,
        in_specs=[pl.BlockSpec(memory_space=pltpu.HBM)] * len(args) if granted else [vmem] * len(args),
        out_specs=[vmem] * len(outs),
        scratch_shapes=scratch,
        cost_estimate=pl.CostEstimate(flops=cost, bytes_accessed=cost, transcendentals=0),
        compiler_params=pltpu.CompilerParams(vmem_limit_bytes=(granted or 24576) * 1024),
    )(*args)


def swapped(x, axis, first):
    pairs = []
    for zg in range(NZG):
        for gy in range(NGY):
            place, count = (zg, NZG) if axis == "zg" else (gy, NGY)
            partner = ((place - first) ^ 1) + first
            if not 0 <= partner < count:
                target = (zg, gy ^ 1) if axis == "zg" else (zg ^ 1, gy)
            else:
                target = (partner, gy) if axis == "zg" else (zg, partner)
            pairs.append((zg * NGY + gy, target[0] * NGY + target[1]))
    return lax.ppermute(x, ("zg", "gy"), pairs)


def crossed(x, axis, by):
    return lax.ppermute(x, axis, [(i, i ^ by) for i in range(lax.axis_size(axis))])


def shards(t, k):
    block = (NB, NZB, NX)
    t, k, across, inside, z_even, z_odd = call(
        load_kernel, "load", [block, block, (2, NZB, NX), (2, NZB, NX), (2, NB, NX), (2, NB, NX)], [t, k],
        scratch=[pltpu.SemaphoreType.DMA((2,))], granted=LOAD_GRANT)
    across = swapped(across, "gy", 1)
    z_odd = swapped(z_odd, "zg", 1)
    z_even = swapped(z_even, "zg", 0)
    inside = swapped(inside, "gy", 0)
    turned = pltpu.VMEM((NB // 2, NX, 2 * NZB), jnp.float32)
    ends = (2 * len(STRIDES) + 1, LANES, NX)
    inner, faces, x_plan, x_ends, z_plan, z_ends, spikes, coeffs = call(
        inner_kernel, "inner",
        [block, (NB - 1, NZB, NX), (NB // 2, XC - 1, 3, LANES, 2 * NZB), (NB // 2,) + ends,
         (NB, ZC - 1, 3, LANES, NX), (NB,) + ends, (2,) + block, (3, NB, NX)], [t, k], scratch=[turned])
    bundle, back, top = call(
        first_kernel, "first", [(NZB * VALUES, NX), (3, NB - 1, NZB, NX), (NB, NX)],
        [t, k, inner, faces, x_plan, x_ends, across, inside, z_even, z_odd], scratch=[turned])
    columns = lax.all_to_all(bundle.reshape(NZB * VALUES, 1, NX), "gy", split_axis=0, concat_axis=0, tiled=True)
    (ends,) = call(column_kernel, "column", [(2 * NGY, NX)], [columns.reshape(NGY * VALUES, NX)])
    ends = lax.all_to_all(ends, "gy", split_axis=0, concat_axis=0, tiled=True)
    second, sums, last_row = call(
        second_kernel, "second", [block, (5, NB, NX), (3, NB, NX)], [ends, back, spikes, coeffs, top])
    sums = [sums] + [crossed(sums, "zg", j) for j in range(1, NZG)]
    (local,) = call(local_z_kernel, "local_z", [block], [second, z_plan, z_ends, t])
    (out,) = call(last_kernel, "last", [block], [local, spikes, last_row] + sums,
                  scratch=[pltpu.VMEM((NZG, 5, NB, NX), jnp.float32), pltpu.VMEM((NZG + 1, NB, NX), jnp.float32)])
    return out


def solution(mesh):
    return jax.shard_map(
        shards,
        mesh=mesh,
        in_specs=(P("gy", "zg", None), P("gy", "zg", None)),
        out_specs=P("gy", "zg", None),
        check_vma=False,
    )
```

```python
import jax
import jax.numpy as jnp
from jax import lax
from jax.experimental import pallas as pl
from jax.experimental.pallas import tpu as pltpu
from jax.sharding import PartitionSpec as P

mesh_courant_number = 300.0

NB, NZB, NX = 4, 64, 128
NGY, NZG = 64, 4
LANES = 8
XC, ZC, YC = NX // LANES, NZB // LANES, NGY // LANES
STRIDES = (1, 2, 4)
VALUES = 5
CROSSINGS = (1, 3, 2)

LOAD_GRANT = 54816


def face(k, q):
    return (2.0 * mesh_courant_number) * k * q / (k + q)


def shift(v, by, axis):
    return pltpu.roll(v, by % v.shape[axis], axis)


def rows_of(shape, axis):
    return lax.broadcasted_iota(jnp.int32, shape, axis)


def chunked(load, count):
    return jnp.concatenate([load(pl.ds(a, LANES, stride=count)) for a in range(count)], axis=0)


def split(v):
    return [v[LANES * a:LANES * (a + 1)] for a in range(v.shape[0] // LANES)]


def before(v):
    last = v.shape[0] - LANES
    return jnp.concatenate([shift(v[last:], 1, 0), v[:last]], axis=0)


def after(v):
    return jnp.concatenate([v[LANES:], shift(v[:LANES], -1, 0)], axis=0)


def order(count):
    step = 1
    while step < count:
        for a in range(step, count, 2 * step):
            yield a, step
        step *= 2


def fold(leaks, couples, closed=None):
    leaks, couples, plan, over = list(leaks), list(couples), [], 0.0
    count = len(leaks)
    for a, step in order(count):
        low, high = couples[a - step], couples[a]
        inverse = 1.0 / (leaks[a] + low + high)
        left, right = low * inverse, high * inverse
        if closed is not None and a == count - 1:
            inverse = jnp.where(closed, 0.0, inverse)
            left = jnp.where(closed, 0.0, left)
            right = jnp.where(closed, 1.0, right)
        plan.append((inverse, left, right))
        leaks[a - step] = leaks[a - step] + left * leaks[a]
        if a + step < count:
            leaks[a + step] = leaks[a + step] + right * leaks[a]
        else:
            over = over + right * leaks[a]
        couples[a - step] = low * right
    return plan, leaks[0], over, couples[0]


def fold_sources(plan, sources):
    sources, over = list(sources), 0.0
    count = len(sources)
    for (a, step), (_, left, right) in zip(order(count), plan):
        sources[a - step] = sources[a - step] + left * sources[a]
        if a + step < count:
            sources[a + step] = sources[a + step] + right * sources[a]
        else:
            over = over + right * sources[a]
    return sources, over


def unfold(plan, sources, head, following):
    count = len(plan) + 1
    x = [head] + [None] * (count - 1) + [following]
    for (a, step), (inverse, left, right) in reversed(list(zip(order(count), plan))):
        x[a] = left * x[a - step] + right * x[min(a + step, count)]
        if sources is not None:
            x[a] = x[a] + inverse * sources[a]
    return x[:count]


def put_plan(ref, at, plan):
    for i, entries in enumerate(plan):
        for j, entry in enumerate(entries):
            ref[at + (i, j)] = entry


def get_plan(ref, at, count):
    return [tuple(ref[at + (i, j)] for j in range(3)) for i in range(count - 1)]


def separator_factors(leak, low, high):
    factors = []
    for s in STRIDES:
        inverse = 1.0 / (leak + low + high)
        from_low = low * shift(inverse, s, 0)
        from_high = high * shift(inverse, -s, 0)
        factors += [from_low, from_high]
        leak = leak + from_low * shift(leak, s, 0) + from_high * shift(leak, -s, 0)
        low = from_low * shift(low, s, 0)
        high = from_high * shift(high, -s, 0)
    return factors + [1.0 / (leak + low + high)]


def separator_solve(factors, b):
    for j, s in enumerate(STRIDES):
        b = b + factors[2 * j] * shift(b, s, 0) + factors[2 * j + 1] * shift(b, -s, 0)
    return b * factors[2 * len(STRIDES)]


def load_kernel(t_hbm, k_hbm, t_ref, k_ref, across_ref, inside_ref, z_even_ref, z_odd_ref, sems):
    odd = lax.rem(lax.axis_index("gy"), 2)
    upper = lax.rem(lax.axis_index("zg"), 2) == 1
    copies = [pltpu.make_async_copy(t_hbm, t_ref, sems.at[0]), pltpu.make_async_copy(k_hbm, k_ref, sems.at[1])]
    for copy in copies:
        copy.start()
    for j, (copy, ref) in enumerate(zip(copies, (t_ref, k_ref))):
        copy.wait()
        across_ref[j] = ref[odd * (NB - 1)]
        inside_ref[j] = ref[(1 - odd) * (NB - 1)]
        for y in range(NB):
            first, last = ref[y, :1], ref[y, NZB - 1:]
            z_even_ref[j, y:y + 1] = jnp.where(upper, first, last)
            z_odd_ref[j, y:y + 1] = jnp.where(upper, last, first)


def block_row(ref, *at):
    return chunked(lambda rows: ref[at + (rows, slice(None))], ZC)


def inner_kernel(t_ref, k_ref, inner_ref, faces_ref, x_plan_ref, x_ends_ref, z_plan_ref, z_ends_ref, spikes_ref,
                 coeffs_ref, turned):
    lane = rows_of((NZB, NX), 1)
    row = rows_of((NZB, NX), 0)
    chunk = rows_of((LANES, NX), 0)
    ts = [block_row(t_ref, y) for y in range(NB)]
    ks = [block_row(k_ref, y) for y in range(NB)]
    flux_y = None
    for y in range(NB):
        k, t = ks[y], ts[y]
        low = jnp.where(lane > 0, face(k, shift(k, 1, 1)), 0.0)
        flux = low * (t - shift(t, 1, 1))
        total = shift(flux, -1, 1) - flux
        face_z = jnp.where(row > 0, face(k, before(k)), 0.0)
        flux = face_z * (t - before(t))
        total = total + (after(flux) - flux)
        if y > 0:
            total = total - flux_y
        if y < NB - 1:
            next_face = face(ks[y + 1], k)
            faces_ref[y] = next_face
            flux_y = next_face * (ts[y + 1] - t)
            total = total + flux_y
        inner_ref[y] = total

        ones = [jnp.ones((LANES, NX), jnp.float32)] * ZC
        plan, leak, over, couple = fold(ones, split(after(face_z)), chunk == LANES - 1)
        put_plan(z_plan_ref, (y,), plan)
        over = shift(over, 1, 0)
        leak_end = over[:1]
        leak = leak + jnp.where(chunk > 0, over, 0.0)
        low = shift(couple, 1, 0)
        at_first = jnp.where(chunk == 1, low, 0.0)
        at_last = jnp.where(chunk == LANES - 1, couple, 0.0)
        factors = separator_factors(leak + at_first + at_last, jnp.where(chunk > 1, low, 0.0),
                                    jnp.where((chunk > 0) & (chunk < LANES - 1), couple, 0.0))
        for j, factor in enumerate(factors):
            z_ends_ref[y, j] = factor
        lam = jnp.where(chunk == 0, 1.0, separator_solve(factors, at_first))
        rho = separator_solve(factors, at_last)
        coeffs_ref[0, y:y + 1] = jnp.sum(lam * leak, axis=0, keepdims=True)
        coeffs_ref[1, y:y + 1] = jnp.sum(rho * leak, axis=0, keepdims=True) + leak_end
        coeffs_ref[2, y:y + 1] = couple[LANES - 1:] * lam[LANES - 1:]
        following = jnp.where(chunk == LANES - 1, 0.0, shift(lam, -1, 0))
        spikes_ref[0, y] = jnp.concatenate(unfold(plan, None, lam, following), axis=0)
        following = jnp.where(chunk == LANES - 1, 1.0, shift(rho, -1, 0))
        spikes_ref[1, y] = jnp.concatenate(unfold(plan, None, rho, following), axis=0)

    for h in range(NB // 2):
        turned[h] = jnp.concatenate(ks[2 * h:2 * h + 2], axis=0).T
        k = block_line(turned, h)
        couples = face(k, after(k))
        couples = jnp.where((rows_of(couples.shape, 0) == NX - 1), 0.0, couples)
        ones = [jnp.ones((LANES, 2 * NZB), jnp.float32)] * XC
        plan, leak, over, couple = fold(ones, split(couples))
        put_plan(x_plan_ref, (h,), plan)
        factors = separator_factors(leak + shift(over, 1, 0), shift(couple, 1, 0), couple)
        for j, factor in enumerate(factors):
            x_ends_ref[h, j] = factor


def block_line(ref, h):
    return chunked(lambda rows: ref[h, rows, :], XC)


def first_kernel(t_ref, k_ref, inner_ref, faces_ref, x_plan_ref, x_ends_ref, across_ref, inside_ref, z_even_ref, z_odd_ref,
                 bundle_ref, back_ref, top_ref, turned):
    gy = lax.axis_index("gy")
    zg = lax.axis_index("zg")
    odd = lax.rem(gy, 2) == 1
    across = [block_row(across_ref, j) for j in range(2)]
    inside = [block_row(inside_ref, j) for j in range(2)]
    yp = [jnp.where(odd, b, a) for a, b in zip(across, inside)]
    yn = [jnp.where(odd, a, b) for a, b in zip(across, inside)]
    upper = lax.rem(zg, 2) == 1
    zp = jnp.where(upper, z_even_ref[...], z_odd_ref[...])
    zn = jnp.where(upper, z_odd_ref[...], z_even_ref[...])
    has_south = jnp.where(gy > 0, 1.0, 0.0)
    has_north = jnp.where(gy < NGY - 1, 1.0, 0.0)
    has_below = jnp.where(zg > 0, 1.0, 0.0)
    has_above = jnp.where(zg < NZG - 1, 1.0, 0.0)
    row = rows_of((NZB, NX), 0)
    sources = []
    g4 = None
    for y in range(NB):
        b = inner_ref[y]
        if y == 0:
            b = b + face(block_row(k_ref, y), yp[1] * has_south) * (yp[0] - block_row(t_ref, y))
        if y == NB - 1:
            g4 = face(block_row(k_ref, y), yn[1] * has_north)
            b = b + g4 * (yn[0] - block_row(t_ref, y))
        k_low, k_high = k_ref[y, :1], k_ref[y, NZB - 1:]
        below = face(k_low, zp[1, y:y + 1] * has_below) * (zp[0, y:y + 1] - t_ref[y, :1])
        top = face(k_high, zn[1, y:y + 1] * has_above)
        top_ref[y:y + 1] = top
        above = top * (zn[0, y:y + 1] - t_ref[y, NZB - 1:])
        b = b + jnp.where(row == 0, below, 0.0) + jnp.where(row == NZB - 1, above, 0.0)
        sources.append(b)
    solved = []
    for h in range(NB // 2):
        turned[h] = jnp.concatenate(sources[2 * h:2 * h + 2], axis=0).T
        plan = get_plan(x_plan_ref, (h,), XC)
        b, over = fold_sources(plan, split(block_line(turned, h)))
        head = separator_solve([x_ends_ref[h, j] for j in range(2 * len(STRIDES) + 1)], b[0] + shift(over, 1, 0))
        for a, x in enumerate(unfold(plan, b, head, shift(head, -1, 0))):
            turned[h, pl.ds(a, LANES, stride=XC), :] = x
        b = turned[h].T
        solved += [b[:NZB], b[NZB:]]
    b0, b1, b2, b3 = solved
    g1, g2, g3 = faces_ref[0], faces_ref[1], faces_ref[2]
    i1 = 1.0 / (1.0 + g1 + g2)
    left, right = g1 * i1, g2 * i1
    source = b0 + left * b1
    b2 = b2 + right * b1
    leak = 1.0 + left
    m2 = 1.0 + right
    a2 = g1 * right
    i2 = 1.0 / (m2 + a2 + g3)
    left, right = a2 * i2, g3 * i2
    source = source + left * b2
    b3 = b3 + right * b2
    leak = leak + left * m2
    m3 = 1.0 + right * m2
    a3 = a2 * right
    i3 = 1.0 / (m3 + a3 + g4)
    left, right = a3 * i3, g4 * i3

    def put(v, x):
        for a, part in enumerate(split(x)):
            bundle_ref[pl.ds(VALUES * a + v, LANES, stride=VALUES * ZC), :] = part

    put(0, leak + left * m3)
    put(1, right * m3)
    put(2, a3 * right)
    put(3, source + left * b3)
    put(4, right * b3)
    beta, lam, rho = b3 * i3, left, right
    back_ref[0, 2], back_ref[1, 2], back_ref[2, 2] = beta, lam, rho
    beta, lam, rho = (b2 + g3 * beta) * i2, (a2 + g3 * lam) * i2, g3 * rho * i2
    back_ref[0, 1], back_ref[1, 1], back_ref[2, 1] = beta, lam, rho
    beta, lam, rho = (b1 + g2 * beta) * i1, (g1 + g2 * lam) * i1, g2 * rho * i1
    back_ref[0, 0], back_ref[1, 0], back_ref[2, 0] = beta, lam, rho


def column_kernel(bundle_ref, out_ref):
    get = lambda v: [bundle_ref[pl.ds(VALUES * a + v, LANES, stride=VALUES * YC), :] for a in range(YC)]
    joined = lambda own, pushed: split(jnp.concatenate(own, axis=0) + before(jnp.concatenate(pushed, axis=0)))
    plan, leak, over, couple = fold(joined(get(0), get(1)), get(2))
    b, over_source = fold_sources(plan, joined(get(3), get(4)))
    factors = separator_factors(leak + shift(over, 1, 0), shift(couple, 1, 0), couple)
    head = separator_solve(factors, b[0] + shift(over_source, 1, 0))
    following = shift(head, -1, 0)
    x = unfold(plan, b, head, following) + [following]
    for a in range(YC):
        out_ref[pl.ds(2 * a, LANES, stride=2 * YC), :] = x[a]
        out_ref[pl.ds(2 * a + 1, LANES, stride=2 * YC), :] = x[a + 1]


def second_kernel(ends_ref, back_ref, spikes_ref, coeffs_ref, top_ref, second_ref, sums_ref, last_row_ref):
    get = lambda v: jnp.concatenate(
        [ends_ref[pl.ds(2 * a + v, LANES, stride=2 * ZC), :] for a in range(ZC)], axis=0)
    own, following = get(0), get(1)
    firsts, lasts = [], []
    for y in range(NB):
        if y == 0:
            u = own
        else:
            u = back_ref[0, y - 1] + back_ref[1, y - 1] * own + back_ref[2, y - 1] * following
        second_ref[y] = u
        firsts.append(jnp.sum(spikes_ref[0, y] * u, axis=0, keepdims=True))
        lasts.append(jnp.sum(spikes_ref[1, y] * u, axis=0, keepdims=True))
    first, last = jnp.concatenate(firsts, axis=0), jnp.concatenate(lasts, axis=0)
    leak, couple, top = coeffs_ref[1], coeffs_ref[2], top_ref[...]
    inverse = 1.0 / (leak + couple + top)
    left, right = couple * inverse, top * inverse
    sums_ref[0] = coeffs_ref[0] + left * leak
    sums_ref[1] = right * leak
    sums_ref[2] = left * top
    sums_ref[3] = first + left * last
    sums_ref[4] = right * last
    last_row_ref[0] = last * inverse
    last_row_ref[1] = left
    last_row_ref[2] = right


def local_z_kernel(second_ref, z_plan_ref, z_ends_ref, t_ref, out_ref):
    chunk = rows_of((LANES, NX), 0)
    for y in range(NB):
        plan = get_plan(z_plan_ref, (y,), ZC)
        b, over = fold_sources(plan, split(second_ref[y]))
        b0 = jnp.where(chunk > 0, b[0] + shift(over, 1, 0), 0.0)
        head = separator_solve([z_ends_ref[y, j] for j in range(2 * len(STRIDES) + 1)], b0)
        following = jnp.where(chunk == LANES - 1, 0.0, shift(head, -1, 0))
        x = jnp.concatenate(unfold(plan, b, head, following), axis=0)
        out_ref[y] = block_row(t_ref, y) + x


def last_kernel(local_ref, spikes_ref, last_row_ref, e0_ref, e1_ref, e2_ref, e3_ref, out_ref, line, ends):
    zg = lax.axis_index("zg")
    for j, e_ref in zip((0,) + CROSSINGS, (e0_ref, e1_ref, e2_ref, e3_ref)):
        line[lax.bitwise_xor(zg, j)] = e_ref[...]
    inverses, sources = [], []
    leak, source = line[0, 0], line[0, 3]
    for d in range(NZG):
        couple = line[d, 2]
        inverse = 1.0 / (leak + couple)
        inverses.append(inverse)
        sources.append(source)
        if d + 1 < NZG:
            passed = couple * inverse
            leak = line[d + 1, 0] + line[d, 1] + passed * leak
            source = line[d + 1, 3] + line[d, 4] + passed * source
    value = jnp.zeros_like(source)
    ends[NZG] = value
    for d in reversed(range(NZG)):
        value = (sources[d] + line[d, 2] * value) * inverses[d]
        ends[d] = value
    own = ends[zg]
    following = last_row_ref[0] + last_row_ref[1] * own + last_row_ref[2] * ends[zg + 1]
    for y in range(NB):
        x = local_ref[y] + spikes_ref[0, y] * own[y:y + 1] + spikes_ref[1, y] * following[y:y + 1]
        for a, part in enumerate(split(x)):
            out_ref[y, pl.ds(a, LANES, stride=ZC), :] = part


def call(kernel, name, outs, args, scratch=(), cost=2000000, granted=0):
    shapes = [jax.ShapeDtypeStruct(o, jnp.float32) for o in outs]
    vmem = pl.BlockSpec(memory_space=pltpu.VMEM)
    return pl.pallas_call(
        kernel,
        name=name,
        out_shape=shapes,
        in_specs=[pl.BlockSpec(memory_space=pltpu.HBM)] * len(args) if granted else [vmem] * len(args),
        out_specs=[vmem] * len(outs),
        scratch_shapes=scratch,
        cost_estimate=pl.CostEstimate(flops=cost, bytes_accessed=cost, transcendentals=0),
        compiler_params=pltpu.CompilerParams(vmem_limit_bytes=(granted or 24576) * 1024),
    )(*args)


def swapped(x, axis, first):
    pairs = []
    for zg in range(NZG):
        for gy in range(NGY):
            place, count = (zg, NZG) if axis == "zg" else (gy, NGY)
            partner = ((place - first) ^ 1) + first
            if not 0 <= partner < count:
                target = (zg, gy ^ 1) if axis == "zg" else (zg ^ 1, gy)
            else:
                target = (partner, gy) if axis == "zg" else (zg, partner)
            pairs.append((zg * NGY + gy, target[0] * NGY + target[1]))
    return lax.ppermute(x, ("zg", "gy"), pairs)


def crossed(x, axis, by):
    return lax.ppermute(x, axis, [(i, i ^ by) for i in range(lax.axis_size(axis))])


def shards(t, k):
    block = (NB, NZB, NX)
    t, k, across, inside, z_even, z_odd = call(
        load_kernel, "load", [block, block, (2, NZB, NX), (2, NZB, NX), (2, NB, NX), (2, NB, NX)], [t, k],
        scratch=[pltpu.SemaphoreType.DMA((2,))], granted=LOAD_GRANT)
    across = swapped(across, "gy", 1)
    z_odd = swapped(z_odd, "zg", 1)
    z_even = swapped(z_even, "zg", 0)
    inside = swapped(inside, "gy", 0)
    turned = pltpu.VMEM((NB // 2, NX, 2 * NZB), jnp.float32)
    ends = (2 * len(STRIDES) + 1, LANES, NX)
    inner, faces, x_plan, x_ends, z_plan, z_ends, spikes, coeffs = call(
        inner_kernel, "inner",
        [block, (NB - 1, NZB, NX), (NB // 2, XC - 1, 3, LANES, 2 * NZB), (NB // 2,) + ends,
         (NB, ZC - 1, 3, LANES, NX), (NB,) + ends, (2,) + block, (3, NB, NX)], [t, k], scratch=[turned])
    bundle, back, top = call(
        first_kernel, "first", [(NZB * VALUES, NX), (3, NB - 1, NZB, NX), (NB, NX)],
        [t, k, inner, faces, x_plan, x_ends, across, inside, z_even, z_odd], scratch=[turned])
    columns = lax.all_to_all(bundle.reshape(NZB * VALUES, 1, NX), "gy", split_axis=0, concat_axis=0, tiled=True)
    (ends,) = call(column_kernel, "column", [(2 * NGY, NX)], [columns.reshape(NGY * VALUES, NX)])
    ends = lax.all_to_all(ends, "gy", split_axis=0, concat_axis=0, tiled=True)
    second, sums, last_row = call(
        second_kernel, "second", [block, (5, NB, NX), (3, NB, NX)], [ends, back, spikes, coeffs, top])
    sums = [sums] + [crossed(sums, "zg", j) for j in CROSSINGS]
    (local,) = call(local_z_kernel, "local_z", [block], [second, z_plan, z_ends, t])
    (out,) = call(last_kernel, "last", [block], [local, spikes, last_row] + sums,
                  scratch=[pltpu.VMEM((NZG, 5, NB, NX), jnp.float32), pltpu.VMEM((NZG + 1, NB, NX), jnp.float32)])
    return out


def solution(mesh):
    return jax.shard_map(
        shards,
        mesh=mesh,
        in_specs=(P("gy", "zg", None), P("gy", "zg", None)),
        out_specs=P("gy", "zg", None),
        check_vma=False,
    )
```

```python
import jax
import jax.numpy as jnp
from jax import lax
from jax.experimental import pallas as pl
from jax.experimental.pallas import tpu as pltpu
from jax.sharding import PartitionSpec as P

mesh_courant_number = 300.0

NB, NZB, NX = 4, 64, 128
NGY, NZG = 64, 4
LANES = 8
XC, ZC, YC = NX // LANES, NZB // LANES, NGY // LANES
STRIDES = (1, 2, 4)
VALUES = 5

LOAD_GRANT = 54816


def face(k, q):
    return (2.0 * mesh_courant_number) * k * q / (k + q)


def shift(v, by, axis):
    return pltpu.roll(v, by % v.shape[axis], axis)


def rows_of(shape, axis):
    return lax.broadcasted_iota(jnp.int32, shape, axis)


def chunked(load, count):
    return jnp.concatenate([load(pl.ds(a, LANES, stride=count)) for a in range(count)], axis=0)


def split(v):
    return [v[LANES * a:LANES * (a + 1)] for a in range(v.shape[0] // LANES)]


def before(v):
    last = v.shape[0] - LANES
    return jnp.concatenate([shift(v[last:], 1, 0), v[:last]], axis=0)


def after(v):
    return jnp.concatenate([v[LANES:], shift(v[:LANES], -1, 0)], axis=0)


def order(count):
    step = 1
    while step < count:
        for a in range(step, count, 2 * step):
            yield a, step
        step *= 2


def fold(leaks, couples, closed=None):
    leaks, couples, plan, over = list(leaks), list(couples), [], 0.0
    count = len(leaks)
    for a, step in order(count):
        low, high = couples[a - step], couples[a]
        inverse = 1.0 / (leaks[a] + low + high)
        left, right = low * inverse, high * inverse
        if closed is not None and a == count - 1:
            inverse = jnp.where(closed, 0.0, inverse)
            left = jnp.where(closed, 0.0, left)
            right = jnp.where(closed, 1.0, right)
        plan.append((inverse, left, right))
        leaks[a - step] = leaks[a - step] + left * leaks[a]
        if a + step < count:
            leaks[a + step] = leaks[a + step] + right * leaks[a]
        else:
            over = over + right * leaks[a]
        couples[a - step] = low * right
    return plan, leaks[0], over, couples[0]


def fold_sources(plan, sources):
    sources, over = list(sources), 0.0
    count = len(sources)
    for (a, step), (_, left, right) in zip(order(count), plan):
        sources[a - step] = sources[a - step] + left * sources[a]
        if a + step < count:
            sources[a + step] = sources[a + step] + right * sources[a]
        else:
            over = over + right * sources[a]
    return sources, over


def unfold(plan, sources, head, following):
    count = len(plan) + 1
    x = [head] + [None] * (count - 1) + [following]
    for (a, step), (inverse, left, right) in reversed(list(zip(order(count), plan))):
        x[a] = left * x[a - step] + right * x[min(a + step, count)]
        if sources is not None:
            x[a] = x[a] + inverse * sources[a]
    return x[:count]


def put_plan(ref, at, plan):
    for i, entries in enumerate(plan):
        for j, entry in enumerate(entries):
            ref[at + (i, j)] = entry


def get_plan(ref, at, count):
    return [tuple(ref[at + (i, j)] for j in range(3)) for i in range(count - 1)]


def separator_factors(leak, low, high):
    factors = []
    for s in STRIDES:
        inverse = 1.0 / (leak + low + high)
        from_low = low * shift(inverse, s, 0)
        from_high = high * shift(inverse, -s, 0)
        factors += [from_low, from_high]
        leak = leak + from_low * shift(leak, s, 0) + from_high * shift(leak, -s, 0)
        low = from_low * shift(low, s, 0)
        high = from_high * shift(high, -s, 0)
    return factors + [1.0 / (leak + low + high)]


def separator_solve(factors, b):
    for j, s in enumerate(STRIDES):
        b = b + factors[2 * j] * shift(b, s, 0) + factors[2 * j + 1] * shift(b, -s, 0)
    return b * factors[2 * len(STRIDES)]


def load_kernel(t_hbm, k_hbm, t_ref, k_ref, across_ref, inside_ref, z_even_ref, z_odd_ref, sems):
    odd = lax.rem(lax.axis_index("gy"), 2)
    upper = lax.rem(lax.axis_index("zg"), 2) == 1
    copies = [pltpu.make_async_copy(t_hbm, t_ref, sems.at[0]), pltpu.make_async_copy(k_hbm, k_ref, sems.at[1])]
    for copy in copies:
        copy.start()
    for j, (copy, ref) in enumerate(zip(copies, (t_ref, k_ref))):
        copy.wait()
        across_ref[j] = ref[odd * (NB - 1)]
        inside_ref[j] = ref[(1 - odd) * (NB - 1)]
        for y in range(NB):
            first, last = ref[y, :1], ref[y, NZB - 1:]
            z_even_ref[j, y:y + 1] = jnp.where(upper, first, last)
            z_odd_ref[j, y:y + 1] = jnp.where(upper, last, first)


def block_row(ref, *at):
    return chunked(lambda rows: ref[at + (rows, slice(None))], ZC)


def inner_kernel(t_ref, k_ref, inner_ref, faces_ref, x_plan_ref, x_ends_ref, z_plan_ref, z_ends_ref, spikes_ref,
                 coeffs_ref, turned):
    lane = rows_of((NZB, NX), 1)
    row = rows_of((NZB, NX), 0)
    chunk = rows_of((LANES, NX), 0)
    ts = [block_row(t_ref, y) for y in range(NB)]
    ks = [block_row(k_ref, y) for y in range(NB)]
    flux_y = None
    for y in range(NB):
        k, t = ks[y], ts[y]
        low = jnp.where(lane > 0, face(k, shift(k, 1, 1)), 0.0)
        flux = low * (t - shift(t, 1, 1))
        total = shift(flux, -1, 1) - flux
        face_z = jnp.where(row > 0, face(k, before(k)), 0.0)
        flux = face_z * (t - before(t))
        total = total + (after(flux) - flux)
        if y > 0:
            total = total - flux_y
        if y < NB - 1:
            next_face = face(ks[y + 1], k)
            faces_ref[y] = next_face
            flux_y = next_face * (ts[y + 1] - t)
            total = total + flux_y
        inner_ref[y] = total

        ones = [jnp.ones((LANES, NX), jnp.float32)] * ZC
        plan, leak, over, couple = fold(ones, split(after(face_z)), chunk == LANES - 1)
        put_plan(z_plan_ref, (y,), plan)
        over = shift(over, 1, 0)
        leak_end = over[:1]
        leak = leak + jnp.where(chunk > 0, over, 0.0)
        low = shift(couple, 1, 0)
        at_first = jnp.where(chunk == 1, low, 0.0)
        at_last = jnp.where(chunk == LANES - 1, couple, 0.0)
        factors = separator_factors(leak + at_first + at_last, jnp.where(chunk > 1, low, 0.0),
                                    jnp.where((chunk > 0) & (chunk < LANES - 1), couple, 0.0))
        for j, factor in enumerate(factors):
            z_ends_ref[y, j] = factor
        lam = jnp.where(chunk == 0, 1.0, separator_solve(factors, at_first))
        rho = separator_solve(factors, at_last)
        coeffs_ref[0, y:y + 1] = jnp.sum(lam * leak, axis=0, keepdims=True)
        coeffs_ref[1, y:y + 1] = jnp.sum(rho * leak, axis=0, keepdims=True) + leak_end
        coeffs_ref[2, y:y + 1] = couple[LANES - 1:] * lam[LANES - 1:]
        following = jnp.where(chunk == LANES - 1, 0.0, shift(lam, -1, 0))
        spikes_ref[0, y] = jnp.concatenate(unfold(plan, None, lam, following), axis=0)
        following = jnp.where(chunk == LANES - 1, 1.0, shift(rho, -1, 0))
        spikes_ref[1, y] = jnp.concatenate(unfold(plan, None, rho, following), axis=0)

    for h in range(NB // 2):
        turned[h] = jnp.concatenate(ks[2 * h:2 * h + 2], axis=0).T
        k = block_line(turned, h)
        couples = face(k, after(k))
        couples = jnp.where((rows_of(couples.shape, 0) == NX - 1), 0.0, couples)
        ones = [jnp.ones((LANES, 2 * NZB), jnp.float32)] * XC
        plan, leak, over, couple = fold(ones, split(couples))
        put_plan(x_plan_ref, (h,), plan)
        factors = separator_factors(leak + shift(over, 1, 0), shift(couple, 1, 0), couple)
        for j, factor in enumerate(factors):
            x_ends_ref[h, j] = factor


def block_line(ref, h):
    return chunked(lambda rows: ref[h, rows, :], XC)


def first_kernel(t_ref, k_ref, inner_ref, faces_ref, x_plan_ref, x_ends_ref, across_ref, inside_ref, z_odd_ref, z_even_ref,
                 bundle_ref, back_ref, top_ref, turned):
    gy = lax.axis_index("gy")
    zg = lax.axis_index("zg")
    odd = lax.rem(gy, 2) == 1
    across = [block_row(across_ref, j) for j in range(2)]
    inside = [block_row(inside_ref, j) for j in range(2)]
    yp = [jnp.where(odd, b, a) for a, b in zip(across, inside)]
    yn = [jnp.where(odd, a, b) for a, b in zip(across, inside)]
    upper = lax.rem(zg, 2) == 1
    zp = jnp.where(upper, z_even_ref[...], z_odd_ref[...])
    zn = jnp.where(upper, z_odd_ref[...], z_even_ref[...])
    has_south = jnp.where(gy > 0, 1.0, 0.0)
    has_north = jnp.where(gy < NGY - 1, 1.0, 0.0)
    has_below = jnp.where(zg > 0, 1.0, 0.0)
    has_above = jnp.where(zg < NZG - 1, 1.0, 0.0)
    row = rows_of((NZB, NX), 0)
    sources = []
    g4 = None
    for y in range(NB):
        b = inner_ref[y]
        if y == 0:
            b = b + face(block_row(k_ref, y), yp[1] * has_south) * (yp[0] - block_row(t_ref, y))
        if y == NB - 1:
            g4 = face(block_row(k_ref, y), yn[1] * has_north)
            b = b + g4 * (yn[0] - block_row(t_ref, y))
        k_low, k_high = k_ref[y, :1], k_ref[y, NZB - 1:]
        below = face(k_low, zp[1, y:y + 1] * has_below) * (zp[0, y:y + 1] - t_ref[y, :1])
        top = face(k_high, zn[1, y:y + 1] * has_above)
        top_ref[y:y + 1] = top
        above = top * (zn[0, y:y + 1] - t_ref[y, NZB - 1:])
        b = b + jnp.where(row == 0, below, 0.0) + jnp.where(row == NZB - 1, above, 0.0)
        sources.append(b)
    solved = []
    for h in range(NB // 2):
        turned[h] = jnp.concatenate(sources[2 * h:2 * h + 2], axis=0).T
        plan = get_plan(x_plan_ref, (h,), XC)
        b, over = fold_sources(plan, split(block_line(turned, h)))
        head = separator_solve([x_ends_ref[h, j] for j in range(2 * len(STRIDES) + 1)], b[0] + shift(over, 1, 0))
        for a, x in enumerate(unfold(plan, b, head, shift(head, -1, 0))):
            turned[h, pl.ds(a, LANES, stride=XC), :] = x
        b = turned[h].T
        solved += [b[:NZB], b[NZB:]]
    b0, b1, b2, b3 = solved
    g1, g2, g3 = faces_ref[0], faces_ref[1], faces_ref[2]
    i1 = 1.0 / (1.0 + g1 + g2)
    left, right = g1 * i1, g2 * i1
    source = b0 + left * b1
    b2 = b2 + right * b1
    leak = 1.0 + left
    m2 = 1.0 + right
    a2 = g1 * right
    i2 = 1.0 / (m2 + a2 + g3)
    left, right = a2 * i2, g3 * i2
    source = source + left * b2
    b3 = b3 + right * b2
    leak = leak + left * m2
    m3 = 1.0 + right * m2
    a3 = a2 * right
    i3 = 1.0 / (m3 + a3 + g4)
    left, right = a3 * i3, g4 * i3

    def put(v, x):
        for a, part in enumerate(split(x)):
            bundle_ref[pl.ds(VALUES * a + v, LANES, stride=VALUES * ZC), :] = part

    put(0, leak + left * m3)
    put(1, right * m3)
    put(2, a3 * right)
    put(3, source + left * b3)
    put(4, right * b3)
    beta, lam, rho = b3 * i3, left, right
    back_ref[0, 2], back_ref[1, 2], back_ref[2, 2] = beta, lam, rho
    beta, lam, rho = (b2 + g3 * beta) * i2, (a2 + g3 * lam) * i2, g3 * rho * i2
    back_ref[0, 1], back_ref[1, 1], back_ref[2, 1] = beta, lam, rho
    beta, lam, rho = (b1 + g2 * beta) * i1, (g1 + g2 * lam) * i1, g2 * rho * i1
    back_ref[0, 0], back_ref[1, 0], back_ref[2, 0] = beta, lam, rho


def column_kernel(bundle_ref, out_ref):
    get = lambda v: [bundle_ref[pl.ds(VALUES * a + v, LANES, stride=VALUES * YC), :] for a in range(YC)]
    joined = lambda own, pushed: split(jnp.concatenate(own, axis=0) + before(jnp.concatenate(pushed, axis=0)))
    plan, leak, over, couple = fold(joined(get(0), get(1)), get(2))
    b, over_source = fold_sources(plan, joined(get(3), get(4)))
    factors = separator_factors(leak + shift(over, 1, 0), shift(couple, 1, 0), couple)
    head = separator_solve(factors, b[0] + shift(over_source, 1, 0))
    following = shift(head, -1, 0)
    x = unfold(plan, b, head, following) + [following]
    for a in range(YC):
        out_ref[pl.ds(2 * a, LANES, stride=2 * YC), :] = x[a]
        out_ref[pl.ds(2 * a + 1, LANES, stride=2 * YC), :] = x[a + 1]


def second_kernel(ends_ref, back_ref, spikes_ref, coeffs_ref, top_ref, second_ref, sums_ref, last_row_ref):
    get = lambda v: jnp.concatenate(
        [ends_ref[pl.ds(2 * a + v, LANES, stride=2 * ZC), :] for a in range(ZC)], axis=0)
    own, following = get(0), get(1)
    firsts, lasts = [], []
    for y in range(NB):
        if y == 0:
            u = own
        else:
            u = back_ref[0, y - 1] + back_ref[1, y - 1] * own + back_ref[2, y - 1] * following
        second_ref[y] = u
        firsts.append(jnp.sum(spikes_ref[0, y] * u, axis=0, keepdims=True))
        lasts.append(jnp.sum(spikes_ref[1, y] * u, axis=0, keepdims=True))
    first, last = jnp.concatenate(firsts, axis=0), jnp.concatenate(lasts, axis=0)
    leak, couple, top = coeffs_ref[1], coeffs_ref[2], top_ref[...]
    inverse = 1.0 / (leak + couple + top)
    left, right = couple * inverse, top * inverse
    sums_ref[0] = coeffs_ref[0] + left * leak
    sums_ref[1] = right * leak
    sums_ref[2] = left * top
    sums_ref[3] = first + left * last
    sums_ref[4] = right * last
    last_row_ref[0] = last * inverse
    last_row_ref[1] = left
    last_row_ref[2] = right


def local_z_kernel(second_ref, z_plan_ref, z_ends_ref, t_ref, out_ref):
    chunk = rows_of((LANES, NX), 0)
    for y in range(NB):
        plan = get_plan(z_plan_ref, (y,), ZC)
        b, over = fold_sources(plan, split(second_ref[y]))
        b0 = jnp.where(chunk > 0, b[0] + shift(over, 1, 0), 0.0)
        head = separator_solve([z_ends_ref[y, j] for j in range(2 * len(STRIDES) + 1)], b0)
        following = jnp.where(chunk == LANES - 1, 0.0, shift(head, -1, 0))
        x = jnp.concatenate(unfold(plan, b, head, following), axis=0)
        out_ref[y] = block_row(t_ref, y) + x


def last_kernel(local_ref, spikes_ref, last_row_ref, e0_ref, e1_ref, e2_ref, e3_ref, out_ref, line, ends):
    zg = lax.axis_index("zg")
    for j, e_ref in enumerate((e0_ref, e1_ref, e2_ref, e3_ref)):
        line[lax.bitwise_xor(zg, j)] = e_ref[...]
    inverses, sources = [], []
    leak, source = line[0, 0], line[0, 3]
    for d in range(NZG):
        couple = line[d, 2]
        inverse = 1.0 / (leak + couple)
        inverses.append(inverse)
        sources.append(source)
        if d + 1 < NZG:
            passed = couple * inverse
            leak = line[d + 1, 0] + line[d, 1] + passed * leak
            source = line[d + 1, 3] + line[d, 4] + passed * source
    value = jnp.zeros_like(source)
    ends[NZG] = value
    for d in reversed(range(NZG)):
        value = (sources[d] + line[d, 2] * value) * inverses[d]
        ends[d] = value
    own = ends[zg]
    following = last_row_ref[0] + last_row_ref[1] * own + last_row_ref[2] * ends[zg + 1]
    for y in range(NB):
        x = local_ref[y] + spikes_ref[0, y] * own[y:y + 1] + spikes_ref[1, y] * following[y:y + 1]
        for a, part in enumerate(split(x)):
            out_ref[y, pl.ds(a, LANES, stride=ZC), :] = part


def call(kernel, name, outs, args, scratch=(), cost=2000000, granted=0):
    shapes = [jax.ShapeDtypeStruct(o, jnp.float32) for o in outs]
    vmem = pl.BlockSpec(memory_space=pltpu.VMEM)
    return pl.pallas_call(
        kernel,
        name=name,
        out_shape=shapes,
        in_specs=[pl.BlockSpec(memory_space=pltpu.HBM)] * len(args) if granted else [vmem] * len(args),
        out_specs=[vmem] * len(outs),
        scratch_shapes=scratch,
        cost_estimate=pl.CostEstimate(flops=cost, bytes_accessed=cost, transcendentals=0),
        compiler_params=pltpu.CompilerParams(vmem_limit_bytes=(granted or 24576) * 1024),
    )(*args)


def swapped(x, axis, first):
    pairs = []
    for zg in range(NZG):
        for gy in range(NGY):
            place, count = (zg, NZG) if axis == "zg" else (gy, NGY)
            partner = ((place - first) ^ 1) + first
            if not 0 <= partner < count:
                target = (zg, gy ^ 1) if axis == "zg" else (zg ^ 1, gy)
            else:
                target = (partner, gy) if axis == "zg" else (zg, partner)
            pairs.append((zg * NGY + gy, target[0] * NGY + target[1]))
    return lax.ppermute(x, ("zg", "gy"), pairs)


def crossed(x, axis, by):
    return lax.ppermute(x, axis, [(i, i ^ by) for i in range(lax.axis_size(axis))])


def shards(t, k):
    block = (NB, NZB, NX)
    t, k, across, inside, z_even, z_odd = call(
        load_kernel, "load", [block, block, (2, NZB, NX), (2, NZB, NX), (2, NB, NX), (2, NB, NX)], [t, k],
        scratch=[pltpu.SemaphoreType.DMA((2,))], granted=LOAD_GRANT)
    across = swapped(across, "gy", 1)
    z_odd = swapped(z_odd, "zg", 1)
    z_even = swapped(z_even, "zg", 0)
    inside = swapped(inside, "gy", 0)
    turned = pltpu.VMEM((NB // 2, NX, 2 * NZB), jnp.float32)
    ends = (2 * len(STRIDES) + 1, LANES, NX)
    inner, faces, x_plan, x_ends, z_plan, z_ends, spikes, coeffs = call(
        inner_kernel, "inner",
        [block, (NB - 1, NZB, NX), (NB // 2, XC - 1, 3, LANES, 2 * NZB), (NB // 2,) + ends,
         (NB, ZC - 1, 3, LANES, NX), (NB,) + ends, (2,) + block, (3, NB, NX)], [t, k], scratch=[turned])
    bundle, back, top = call(
        first_kernel, "first", [(NZB * VALUES, NX), (3, NB - 1, NZB, NX), (NB, NX)],
        [t, k, inner, faces, x_plan, x_ends, across, inside, z_odd, z_even], scratch=[turned])
    columns = lax.all_to_all(bundle.reshape(NZB * VALUES, 1, NX), "gy", split_axis=0, concat_axis=0, tiled=True)
    (ends,) = call(column_kernel, "column", [(2 * NGY, NX)], [columns.reshape(NGY * VALUES, NX)])
    ends = lax.all_to_all(ends, "gy", split_axis=0, concat_axis=0, tiled=True)
    second, sums, last_row = call(
        second_kernel, "second", [block, (5, NB, NX), (3, NB, NX)], [ends, back, spikes, coeffs, top])
    sums = [sums] + [crossed(sums, "zg", j) for j in range(1, NZG)]
    (local,) = call(local_z_kernel, "local_z", [block], [second, z_plan, z_ends, t])
    (out,) = call(last_kernel, "last", [block], [local, spikes, last_row] + sums,
                  scratch=[pltpu.VMEM((NZG, 5, NB, NX), jnp.float32), pltpu.VMEM((NZG + 1, NB, NX), jnp.float32)])
    return out


def solution(mesh):
    return jax.shard_map(
        shards,
        mesh=mesh,
        in_specs=(P("gy", "zg", None), P("gy", "zg", None)),
        out_specs=P("gy", "zg", None),
        check_vma=False,
    )
```

```python
import jax
import jax.numpy as jnp
from jax import lax
from jax.experimental import pallas as pl
from jax.experimental.pallas import tpu as pltpu
from jax.sharding import PartitionSpec as P

mesh_courant_number = 300.0

NB, NZB, NX = 4, 64, 128
NGY, NZG = 64, 4
LANES = 8
XC, ZC, YC = NX // LANES, NZB // LANES, NGY // LANES
STRIDES = (1, 2, 4)
VALUES = 5

LOAD_GRANT = 54816


def face(k, q):
    return (2.0 * mesh_courant_number) * k * q / (k + q)


def shift(v, by, axis):
    return pltpu.roll(v, by % v.shape[axis], axis)


def rows_of(shape, axis):
    return lax.broadcasted_iota(jnp.int32, shape, axis)


def chunked(load, count):
    return jnp.concatenate([load(pl.ds(a, LANES, stride=count)) for a in range(count)], axis=0)


def split(v):
    return [v[LANES * a:LANES * (a + 1)] for a in range(v.shape[0] // LANES)]


def before(v):
    last = v.shape[0] - LANES
    return jnp.concatenate([shift(v[last:], 1, 0), v[:last]], axis=0)


def after(v):
    return jnp.concatenate([v[LANES:], shift(v[:LANES], -1, 0)], axis=0)


def order(count):
    step = 1
    while step < count:
        for a in range(step, count, 2 * step):
            yield a, step
        step *= 2


def fold(leaks, couples, closed=None):
    leaks, couples, plan, over = list(leaks), list(couples), [], 0.0
    count = len(leaks)
    for a, step in order(count):
        low, high = couples[a - step], couples[a]
        inverse = 1.0 / (leaks[a] + low + high)
        left, right = low * inverse, high * inverse
        if closed is not None and a == count - 1:
            inverse = jnp.where(closed, 0.0, inverse)
            left = jnp.where(closed, 0.0, left)
            right = jnp.where(closed, 1.0, right)
        plan.append((inverse, left, right))
        leaks[a - step] = leaks[a - step] + left * leaks[a]
        if a + step < count:
            leaks[a + step] = leaks[a + step] + right * leaks[a]
        else:
            over = over + right * leaks[a]
        couples[a - step] = low * right
    return plan, leaks[0], over, couples[0]


def fold_sources(plan, sources):
    sources, over = list(sources), 0.0
    count = len(sources)
    for (a, step), (_, left, right) in zip(order(count), plan):
        sources[a - step] = sources[a - step] + left * sources[a]
        if a + step < count:
            sources[a + step] = sources[a + step] + right * sources[a]
        else:
            over = over + right * sources[a]
    return sources, over


def unfold(plan, sources, head, following):
    count = len(plan) + 1
    x = [head] + [None] * (count - 1) + [following]
    for (a, step), (inverse, left, right) in reversed(list(zip(order(count), plan))):
        x[a] = left * x[a - step] + right * x[min(a + step, count)]
        if sources is not None:
            x[a] = x[a] + inverse * sources[a]
    return x[:count]


def put_plan(ref, at, plan):
    for i, entries in enumerate(plan):
        for j, entry in enumerate(entries):
            ref[at + (i, j)] = entry


def get_plan(ref, at, count):
    return [tuple(ref[at + (i, j)] for j in range(3)) for i in range(count - 1)]


def separator_factors(leak, low, high):
    factors = []
    for s in STRIDES:
        inverse = 1.0 / (leak + low + high)
        from_low = low * shift(inverse, s, 0)
        from_high = high * shift(inverse, -s, 0)
        factors += [from_low, from_high]
        leak = leak + from_low * shift(leak, s, 0) + from_high * shift(leak, -s, 0)
        low = from_low * shift(low, s, 0)
        high = from_high * shift(high, -s, 0)
    return factors + [1.0 / (leak + low + high)]


def separator_solve(factors, b):
    for j, s in enumerate(STRIDES):
        b = b + factors[2 * j] * shift(b, s, 0) + factors[2 * j + 1] * shift(b, -s, 0)
    return b * factors[2 * len(STRIDES)]


def load_kernel(t_hbm, k_hbm, t_ref, k_ref, across_ref, inside_ref, z_even_ref, z_odd_ref, sems):
    odd = lax.rem(lax.axis_index("gy"), 2)
    upper = lax.rem(lax.axis_index("zg"), 2) == 1
    copies = [pltpu.make_async_copy(t_hbm, t_ref, sems.at[0]), pltpu.make_async_copy(k_hbm, k_ref, sems.at[1])]
    for copy in copies:
        copy.start()
    for j, (copy, ref) in enumerate(zip(copies, (t_ref, k_ref))):
        copy.wait()
        across_ref[j] = ref[odd * (NB - 1)]
        inside_ref[j] = ref[(1 - odd) * (NB - 1)]
        for y in range(NB):
            first, last = ref[y, :1], ref[y, NZB - 1:]
            z_even_ref[j, y:y + 1] = jnp.where(upper, first, last)
            z_odd_ref[j, y:y + 1] = jnp.where(upper, last, first)


def block_row(ref, *at):
    return chunked(lambda rows: ref[at + (rows, slice(None))], ZC)


def inner_kernel(t_ref, k_ref, inner_ref, faces_ref, x_plan_ref, x_ends_ref, z_plan_ref, z_ends_ref, spikes_ref,
                 coeffs_ref, turned):
    lane = rows_of((NZB, NX), 1)
    row = rows_of((NZB, NX), 0)
    chunk = rows_of((LANES, NX), 0)
    ts = [block_row(t_ref, y) for y in range(NB)]
    ks = [block_row(k_ref, y) for y in range(NB)]
    flux_y = None
    for y in range(NB):
        k, t = ks[y], ts[y]
        low = jnp.where(lane > 0, face(k, shift(k, 1, 1)), 0.0)
        flux = low * (t - shift(t, 1, 1))
        total = shift(flux, -1, 1) - flux
        face_z = jnp.where(row > 0, face(k, before(k)), 0.0)
        flux = face_z * (t - before(t))
        total = total + (after(flux) - flux)
        if y > 0:
            total = total - flux_y
        if y < NB - 1:
            next_face = face(ks[y + 1], k)
            faces_ref[y] = next_face
            flux_y = next_face * (ts[y + 1] - t)
            total = total + flux_y
        inner_ref[y] = total

        ones = [jnp.ones((LANES, NX), jnp.float32)] * ZC
        plan, leak, over, couple = fold(ones, split(after(face_z)), chunk == LANES - 1)
        put_plan(z_plan_ref, (y,), plan)
        over = shift(over, 1, 0)
        leak_end = over[:1]
        leak = leak + jnp.where(chunk > 0, over, 0.0)
        low = shift(couple, 1, 0)
        at_first = jnp.where(chunk == 1, low, 0.0)
        at_last = jnp.where(chunk == LANES - 1, couple, 0.0)
        factors = separator_factors(leak + at_first + at_last, jnp.where(chunk > 1, low, 0.0),
                                    jnp.where((chunk > 0) & (chunk < LANES - 1), couple, 0.0))
        for j, factor in enumerate(factors):
            z_ends_ref[y, j] = factor
        lam = jnp.where(chunk == 0, 1.0, separator_solve(factors, at_first))
        rho = separator_solve(factors, at_last)
        coeffs_ref[0, y:y + 1] = jnp.sum(lam * leak, axis=0, keepdims=True)
        coeffs_ref[1, y:y + 1] = jnp.sum(rho * leak, axis=0, keepdims=True) + leak_end
        coeffs_ref[2, y:y + 1] = couple[LANES - 1:] * lam[LANES - 1:]
        following = jnp.where(chunk == LANES - 1, 0.0, shift(lam, -1, 0))
        spikes_ref[0, y] = jnp.concatenate(unfold(plan, None, lam, following), axis=0)
        following = jnp.where(chunk == LANES - 1, 1.0, shift(rho, -1, 0))
        spikes_ref[1, y] = jnp.concatenate(unfold(plan, None, rho, following), axis=0)

    for h in range(NB // 2):
        turned[h] = jnp.concatenate(ks[2 * h:2 * h + 2], axis=0).T
        k = block_line(turned, h)
        couples = face(k, after(k))
        couples = jnp.where((rows_of(couples.shape, 0) == NX - 1), 0.0, couples)
        ones = [jnp.ones((LANES, 2 * NZB), jnp.float32)] * XC
        plan, leak, over, couple = fold(ones, split(couples))
        put_plan(x_plan_ref, (h,), plan)
        factors = separator_factors(leak + shift(over, 1, 0), shift(couple, 1, 0), couple)
        for j, factor in enumerate(factors):
            x_ends_ref[h, j] = factor


def block_line(ref, h):
    return chunked(lambda rows: ref[h, rows, :], XC)


def first_kernel(t_ref, k_ref, inner_ref, faces_ref, x_plan_ref, x_ends_ref, inside_ref, across_ref, z_even_ref, z_odd_ref,
                 bundle_ref, back_ref, top_ref, turned):
    gy = lax.axis_index("gy")
    zg = lax.axis_index("zg")
    odd = lax.rem(gy, 2) == 1
    across = [block_row(across_ref, j) for j in range(2)]
    inside = [block_row(inside_ref, j) for j in range(2)]
    yp = [jnp.where(odd, b, a) for a, b in zip(across, inside)]
    yn = [jnp.where(odd, a, b) for a, b in zip(across, inside)]
    upper = lax.rem(zg, 2) == 1
    zp = jnp.where(upper, z_even_ref[...], z_odd_ref[...])
    zn = jnp.where(upper, z_odd_ref[...], z_even_ref[...])
    has_south = jnp.where(gy > 0, 1.0, 0.0)
    has_north = jnp.where(gy < NGY - 1, 1.0, 0.0)
    has_below = jnp.where(zg > 0, 1.0, 0.0)
    has_above = jnp.where(zg < NZG - 1, 1.0, 0.0)
    row = rows_of((NZB, NX), 0)
    sources = []
    g4 = None
    for y in range(NB):
        b = inner_ref[y]
        if y == 0:
            b = b + face(block_row(k_ref, y), yp[1] * has_south) * (yp[0] - block_row(t_ref, y))
        if y == NB - 1:
            g4 = face(block_row(k_ref, y), yn[1] * has_north)
            b = b + g4 * (yn[0] - block_row(t_ref, y))
        k_low, k_high = k_ref[y, :1], k_ref[y, NZB - 1:]
        below = face(k_low, zp[1, y:y + 1] * has_below) * (zp[0, y:y + 1] - t_ref[y, :1])
        top = face(k_high, zn[1, y:y + 1] * has_above)
        top_ref[y:y + 1] = top
        above = top * (zn[0, y:y + 1] - t_ref[y, NZB - 1:])
        b = b + jnp.where(row == 0, below, 0.0) + jnp.where(row == NZB - 1, above, 0.0)
        sources.append(b)
    solved = []
    for h in range(NB // 2):
        turned[h] = jnp.concatenate(sources[2 * h:2 * h + 2], axis=0).T
        plan = get_plan(x_plan_ref, (h,), XC)
        b, over = fold_sources(plan, split(block_line(turned, h)))
        head = separator_solve([x_ends_ref[h, j] for j in range(2 * len(STRIDES) + 1)], b[0] + shift(over, 1, 0))
        for a, x in enumerate(unfold(plan, b, head, shift(head, -1, 0))):
            turned[h, pl.ds(a, LANES, stride=XC), :] = x
        b = turned[h].T
        solved += [b[:NZB], b[NZB:]]
    b0, b1, b2, b3 = solved
    g1, g2, g3 = faces_ref[0], faces_ref[1], faces_ref[2]
    i1 = 1.0 / (1.0 + g1 + g2)
    left, right = g1 * i1, g2 * i1
    source = b0 + left * b1
    b2 = b2 + right * b1
    leak = 1.0 + left
    m2 = 1.0 + right
    a2 = g1 * right
    i2 = 1.0 / (m2 + a2 + g3)
    left, right = a2 * i2, g3 * i2
    source = source + left * b2
    b3 = b3 + right * b2
    leak = leak + left * m2
    m3 = 1.0 + right * m2
    a3 = a2 * right
    i3 = 1.0 / (m3 + a3 + g4)
    left, right = a3 * i3, g4 * i3

    def put(v, x):
        for a, part in enumerate(split(x)):
            bundle_ref[pl.ds(VALUES * a + v, LANES, stride=VALUES * ZC), :] = part

    put(0, leak + left * m3)
    put(1, right * m3)
    put(2, a3 * right)
    put(3, source + left * b3)
    put(4, right * b3)
    beta, lam, rho = b3 * i3, left, right
    back_ref[0, 2], back_ref[1, 2], back_ref[2, 2] = beta, lam, rho
    beta, lam, rho = (b2 + g3 * beta) * i2, (a2 + g3 * lam) * i2, g3 * rho * i2
    back_ref[0, 1], back_ref[1, 1], back_ref[2, 1] = beta, lam, rho
    beta, lam, rho = (b1 + g2 * beta) * i1, (g1 + g2 * lam) * i1, g2 * rho * i1
    back_ref[0, 0], back_ref[1, 0], back_ref[2, 0] = beta, lam, rho


def column_kernel(bundle_ref, out_ref):
    get = lambda v: [bundle_ref[pl.ds(VALUES * a + v, LANES, stride=VALUES * YC), :] for a in range(YC)]
    joined = lambda own, pushed: split(jnp.concatenate(own, axis=0) + before(jnp.concatenate(pushed, axis=0)))
    plan, leak, over, couple = fold(joined(get(0), get(1)), get(2))
    b, over_source = fold_sources(plan, joined(get(3), get(4)))
    factors = separator_factors(leak + shift(over, 1, 0), shift(couple, 1, 0), couple)
    head = separator_solve(factors, b[0] + shift(over_source, 1, 0))
    following = shift(head, -1, 0)
    x = unfold(plan, b, head, following) + [following]
    for a in range(YC):
        out_ref[pl.ds(2 * a, LANES, stride=2 * YC), :] = x[a]
        out_ref[pl.ds(2 * a + 1, LANES, stride=2 * YC), :] = x[a + 1]


def second_kernel(ends_ref, back_ref, spikes_ref, coeffs_ref, top_ref, second_ref, sums_ref, last_row_ref):
    get = lambda v: jnp.concatenate(
        [ends_ref[pl.ds(2 * a + v, LANES, stride=2 * ZC), :] for a in range(ZC)], axis=0)
    own, following = get(0), get(1)
    firsts, lasts = [], []
    for y in range(NB):
        if y == 0:
            u = own
        else:
            u = back_ref[0, y - 1] + back_ref[1, y - 1] * own + back_ref[2, y - 1] * following
        second_ref[y] = u
        firsts.append(jnp.sum(spikes_ref[0, y] * u, axis=0, keepdims=True))
        lasts.append(jnp.sum(spikes_ref[1, y] * u, axis=0, keepdims=True))
    first, last = jnp.concatenate(firsts, axis=0), jnp.concatenate(lasts, axis=0)
    leak, couple, top = coeffs_ref[1], coeffs_ref[2], top_ref[...]
    inverse = 1.0 / (leak + couple + top)
    left, right = couple * inverse, top * inverse
    sums_ref[0] = coeffs_ref[0] + left * leak
    sums_ref[1] = right * leak
    sums_ref[2] = left * top
    sums_ref[3] = first + left * last
    sums_ref[4] = right * last
    last_row_ref[0] = last * inverse
    last_row_ref[1] = left
    last_row_ref[2] = right


def local_z_kernel(second_ref, z_plan_ref, z_ends_ref, t_ref, out_ref):
    chunk = rows_of((LANES, NX), 0)
    for y in range(NB):
        plan = get_plan(z_plan_ref, (y,), ZC)
        b, over = fold_sources(plan, split(second_ref[y]))
        b0 = jnp.where(chunk > 0, b[0] + shift(over, 1, 0), 0.0)
        head = separator_solve([z_ends_ref[y, j] for j in range(2 * len(STRIDES) + 1)], b0)
        following = jnp.where(chunk == LANES - 1, 0.0, shift(head, -1, 0))
        x = jnp.concatenate(unfold(plan, b, head, following), axis=0)
        out_ref[y] = block_row(t_ref, y) + x


def last_kernel(local_ref, spikes_ref, last_row_ref, e0_ref, e1_ref, e2_ref, e3_ref, out_ref, line, ends):
    zg = lax.axis_index("zg")
    for j, e_ref in enumerate((e0_ref, e1_ref, e2_ref, e3_ref)):
        line[lax.bitwise_xor(zg, j)] = e_ref[...]
    inverses, sources = [], []
    leak, source = line[0, 0], line[0, 3]
    for d in range(NZG):
        couple = line[d, 2]
        inverse = 1.0 / (leak + couple)
        inverses.append(inverse)
        sources.append(source)
        if d + 1 < NZG:
            passed = couple * inverse
            leak = line[d + 1, 0] + line[d, 1] + passed * leak
            source = line[d + 1, 3] + line[d, 4] + passed * source
    value = jnp.zeros_like(source)
    ends[NZG] = value
    for d in reversed(range(NZG)):
        value = (sources[d] + line[d, 2] * value) * inverses[d]
        ends[d] = value
    own = ends[zg]
    following = last_row_ref[0] + last_row_ref[1] * own + last_row_ref[2] * ends[zg + 1]
    for y in range(NB):
        x = local_ref[y] + spikes_ref[0, y] * own[y:y + 1] + spikes_ref[1, y] * following[y:y + 1]
        for a, part in enumerate(split(x)):
            out_ref[y, pl.ds(a, LANES, stride=ZC), :] = part


def call(kernel, name, outs, args, scratch=(), cost=2000000, granted=0):
    shapes = [jax.ShapeDtypeStruct(o, jnp.float32) for o in outs]
    vmem = pl.BlockSpec(memory_space=pltpu.VMEM)
    return pl.pallas_call(
        kernel,
        name=name,
        out_shape=shapes,
        in_specs=[pl.BlockSpec(memory_space=pltpu.HBM)] * len(args) if granted else [vmem] * len(args),
        out_specs=[vmem] * len(outs),
        scratch_shapes=scratch,
        cost_estimate=pl.CostEstimate(flops=cost, bytes_accessed=cost, transcendentals=0),
        compiler_params=pltpu.CompilerParams(vmem_limit_bytes=(granted or 24576) * 1024),
    )(*args)


def swapped(x, axis, first):
    pairs = []
    for zg in range(NZG):
        for gy in range(NGY):
            place, count = (zg, NZG) if axis == "zg" else (gy, NGY)
            partner = ((place - first) ^ 1) + first
            if not 0 <= partner < count:
                target = (zg, gy ^ 1) if axis == "zg" else (zg ^ 1, gy)
            else:
                target = (partner, gy) if axis == "zg" else (zg, partner)
            pairs.append((zg * NGY + gy, target[0] * NGY + target[1]))
    return lax.ppermute(x, ("zg", "gy"), pairs)


def crossed(x, axis, by):
    return lax.ppermute(x, axis, [(i, i ^ by) for i in range(lax.axis_size(axis))])


def shards(t, k):
    block = (NB, NZB, NX)
    t, k, across, inside, z_even, z_odd = call(
        load_kernel, "load", [block, block, (2, NZB, NX), (2, NZB, NX), (2, NB, NX), (2, NB, NX)], [t, k],
        scratch=[pltpu.SemaphoreType.DMA((2,))], granted=LOAD_GRANT)
    across = swapped(across, "gy", 1)
    z_odd = swapped(z_odd, "zg", 1)
    z_even = swapped(z_even, "zg", 0)
    inside = swapped(inside, "gy", 0)
    turned = pltpu.VMEM((NB // 2, NX, 2 * NZB), jnp.float32)
    ends = (2 * len(STRIDES) + 1, LANES, NX)
    inner, faces, x_plan, x_ends, z_plan, z_ends, spikes, coeffs = call(
        inner_kernel, "inner",
        [block, (NB - 1, NZB, NX), (NB // 2, XC - 1, 3, LANES, 2 * NZB), (NB // 2,) + ends,
         (NB, ZC - 1, 3, LANES, NX), (NB,) + ends, (2,) + block, (3, NB, NX)], [t, k], scratch=[turned])
    bundle, back, top = call(
        first_kernel, "first", [(NZB * VALUES, NX), (3, NB - 1, NZB, NX), (NB, NX)],
        [t, k, inner, faces, x_plan, x_ends, inside, across, z_even, z_odd], scratch=[turned])
    columns = lax.all_to_all(bundle.reshape(NZB * VALUES, 1, NX), "gy", split_axis=0, concat_axis=0, tiled=True)
    (ends,) = call(column_kernel, "column", [(2 * NGY, NX)], [columns.reshape(NGY * VALUES, NX)])
    ends = lax.all_to_all(ends, "gy", split_axis=0, concat_axis=0, tiled=True)
    second, sums, last_row = call(
        second_kernel, "second", [block, (5, NB, NX), (3, NB, NX)], [ends, back, spikes, coeffs, top])
    sums = [sums] + [crossed(sums, "zg", j) for j in range(1, NZG)]
    (local,) = call(local_z_kernel, "local_z", [block], [second, z_plan, z_ends, t])
    (out,) = call(last_kernel, "last", [block], [local, spikes, last_row] + sums,
                  scratch=[pltpu.VMEM((NZG, 5, NB, NX), jnp.float32), pltpu.VMEM((NZG + 1, NB, NX), jnp.float32)])
    return out


def solution(mesh):
    return jax.shard_map(
        shards,
        mesh=mesh,
        in_specs=(P("gy", "zg", None), P("gy", "zg", None)),
        out_specs=P("gy", "zg", None),
        check_vma=False,
    )
```

```python
import jax
import jax.numpy as jnp
from jax import lax
from jax.experimental import pallas as pl
from jax.experimental.pallas import tpu as pltpu
from jax.sharding import PartitionSpec as P

mesh_courant_number = 300.0

NB, NZB, NX = 4, 64, 128
NGY, NZG = 64, 4
LANES = 8
XC, ZC, YC = NX // LANES, NZB // LANES, NGY // LANES
STRIDES = (1, 2, 4)
VALUES = 5

LOAD_GRANT = 54816


def face(k, q):
    return (2.0 * mesh_courant_number) * k * q / (k + q)


def shift(v, by, axis):
    return pltpu.roll(v, by % v.shape[axis], axis)


def rows_of(shape, axis):
    return lax.broadcasted_iota(jnp.int32, shape, axis)


def chunked(load, count):
    return jnp.concatenate([load(pl.ds(a, LANES, stride=count)) for a in range(count)], axis=0)


def split(v):
    return [v[LANES * a:LANES * (a + 1)] for a in range(v.shape[0] // LANES)]


def before(v):
    last = v.shape[0] - LANES
    return jnp.concatenate([shift(v[last:], 1, 0), v[:last]], axis=0)


def after(v):
    return jnp.concatenate([v[LANES:], shift(v[:LANES], -1, 0)], axis=0)


def order(count):
    step = 1
    while step < count:
        for a in range(step, count, 2 * step):
            yield a, step
        step *= 2


def fold(leaks, couples, closed=None):
    leaks, couples, plan, over = list(leaks), list(couples), [], 0.0
    count = len(leaks)
    for a, step in order(count):
        low, high = couples[a - step], couples[a]
        inverse = 1.0 / (leaks[a] + low + high)
        left, right = low * inverse, high * inverse
        if closed is not None and a == count - 1:
            inverse = jnp.where(closed, 0.0, inverse)
            left = jnp.where(closed, 0.0, left)
            right = jnp.where(closed, 1.0, right)
        plan.append((inverse, left, right))
        leaks[a - step] = leaks[a - step] + left * leaks[a]
        if a + step < count:
            leaks[a + step] = leaks[a + step] + right * leaks[a]
        else:
            over = over + right * leaks[a]
        couples[a - step] = low * right
    return plan, leaks[0], over, couples[0]


def fold_sources(plan, sources):
    sources, over = list(sources), 0.0
    count = len(sources)
    for (a, step), (_, left, right) in zip(order(count), plan):
        sources[a - step] = sources[a - step] + left * sources[a]
        if a + step < count:
            sources[a + step] = sources[a + step] + right * sources[a]
        else:
            over = over + right * sources[a]
    return sources, over


def unfold(plan, sources, head, following):
    count = len(plan) + 1
    x = [head] + [None] * (count - 1) + [following]
    for (a, step), (inverse, left, right) in reversed(list(zip(order(count), plan))):
        x[a] = left * x[a - step] + right * x[min(a + step, count)]
        if sources is not None:
            x[a] = x[a] + inverse * sources[a]
    return x[:count]


def put_plan(ref, at, plan):
    for i, entries in enumerate(plan):
        for j, entry in enumerate(entries):
            ref[at + (i, j)] = entry


def get_plan(ref, at, count):
    return [tuple(ref[at + (i, j)] for j in range(3)) for i in range(count - 1)]


def separator_factors(leak, low, high):
    factors = []
    for s in STRIDES:
        inverse = 1.0 / (leak + low + high)
        from_low = low * shift(inverse, s, 0)
        from_high = high * shift(inverse, -s, 0)
        factors += [from_low, from_high]
        leak = leak + from_low * shift(leak, s, 0) + from_high * shift(leak, -s, 0)
        low = from_low * shift(low, s, 0)
        high = from_high * shift(high, -s, 0)
    return factors + [1.0 / (leak + low + high)]


def separator_solve(factors, b):
    for j, s in enumerate(STRIDES):
        b = b + factors[2 * j] * shift(b, s, 0) + factors[2 * j + 1] * shift(b, -s, 0)
    return b * factors[2 * len(STRIDES)]


def load_kernel(t_hbm, k_hbm, t_ref, k_ref, across_ref, inside_ref, z_even_ref, z_odd_ref, sems):
    odd = lax.rem(lax.axis_index("gy"), 2)
    upper = lax.rem(lax.axis_index("zg"), 2) == 1
    copies = [pltpu.make_async_copy(t_hbm, t_ref, sems.at[0]), pltpu.make_async_copy(k_hbm, k_ref, sems.at[1])]
    for copy in copies:
        copy.start()
    for j, (copy, ref) in enumerate(zip(copies, (t_ref, k_ref))):
        copy.wait()
        across_ref[j] = ref[odd * (NB - 1)]
        inside_ref[j] = ref[(1 - odd) * (NB - 1)]
        for y in range(NB):
            first, last = ref[y, :1], ref[y, NZB - 1:]
            z_even_ref[j, y:y + 1] = jnp.where(upper, first, last)
            z_odd_ref[j, y:y + 1] = jnp.where(upper, last, first)


def block_row(ref, *at):
    return chunked(lambda rows: ref[at + (rows, slice(None))], ZC)


def inner_kernel(t_ref, k_ref, inner_ref, faces_ref, x_plan_ref, x_ends_ref, z_plan_ref, z_ends_ref, spikes_ref,
                 coeffs_ref, turned):
    lane = rows_of((NZB, NX), 1)
    row = rows_of((NZB, NX), 0)
    chunk = rows_of((LANES, NX), 0)
    ts = [block_row(t_ref, y) for y in range(NB)]
    ks = [block_row(k_ref, y) for y in range(NB)]
    flux_y = None
    for y in range(NB):
        k, t = ks[y], ts[y]
        low = jnp.where(lane > 0, face(k, shift(k, 1, 1)), 0.0)
        flux = low * (t - shift(t, 1, 1))
        total = shift(flux, -1, 1) - flux
        face_z = jnp.where(row > 0, face(k, before(k)), 0.0)
        flux = face_z * (t - before(t))
        total = total + (after(flux) - flux)
        if y > 0:
            total = total - flux_y
        if y < NB - 1:
            next_face = face(ks[y + 1], k)
            faces_ref[y] = next_face
            flux_y = next_face * (ts[y + 1] - t)
            total = total + flux_y
        inner_ref[y] = total

        ones = [jnp.ones((LANES, NX), jnp.float32)] * ZC
        plan, leak, over, couple = fold(ones, split(after(face_z)), chunk == LANES - 1)
        put_plan(z_plan_ref, (y,), plan)
        over = shift(over, 1, 0)
        leak_end = over[:1]
        leak = leak + jnp.where(chunk > 0, over, 0.0)
        low = shift(couple, 1, 0)
        at_first = jnp.where(chunk == 1, low, 0.0)
        at_last = jnp.where(chunk == LANES - 1, couple, 0.0)
        factors = separator_factors(leak + at_first + at_last, jnp.where(chunk > 1, low, 0.0),
                                    jnp.where((chunk > 0) & (chunk < LANES - 1), couple, 0.0))
        for j, factor in enumerate(factors):
            z_ends_ref[y, j] = factor
        lam = jnp.where(chunk == 0, 1.0, separator_solve(factors, at_first))
        rho = separator_solve(factors, at_last)
        coeffs_ref[0, y:y + 1] = jnp.sum(lam * leak, axis=0, keepdims=True)
        coeffs_ref[1, y:y + 1] = jnp.sum(rho * leak, axis=0, keepdims=True) + leak_end
        coeffs_ref[2, y:y + 1] = couple[LANES - 1:] * lam[LANES - 1:]
        following = jnp.where(chunk == LANES - 1, 0.0, shift(lam, -1, 0))
        spikes_ref[0, y] = jnp.concatenate(unfold(plan, None, lam, following), axis=0)
        following = jnp.where(chunk == LANES - 1, 1.0, shift(rho, -1, 0))
        spikes_ref[1, y] = jnp.concatenate(unfold(plan, None, rho, following), axis=0)

    for h in range(NB // 2):
        turned[h] = jnp.concatenate(ks[2 * h:2 * h + 2], axis=0).T
        k = block_line(turned, h)
        couples = face(k, after(k))
        couples = jnp.where((rows_of(couples.shape, 0) == NX - 1), 0.0, couples)
        ones = [jnp.ones((LANES, 2 * NZB), jnp.float32)] * XC
        plan, leak, over, couple = fold(ones, split(couples))
        put_plan(x_plan_ref, (h,), plan)
        factors = separator_factors(leak + shift(over, 1, 0), shift(couple, 1, 0), couple)
        for j, factor in enumerate(factors):
            x_ends_ref[h, j] = factor


def block_line(ref, h):
    return chunked(lambda rows: ref[h, rows, :], XC)


def first_kernel(t_ref, k_ref, inner_ref, faces_ref, x_plan_ref, x_ends_ref, inside_ref, across_ref, z_even_ref, z_odd_ref,
                 bundle_ref, back_ref, top_ref, turned):
    gy = lax.axis_index("gy")
    zg = lax.axis_index("zg")
    odd = lax.rem(gy, 2) == 1
    across = [block_row(across_ref, j) for j in range(2)]
    inside = [block_row(inside_ref, j) for j in range(2)]
    yp = [jnp.where(odd, b, a) for a, b in zip(across, inside)]
    yn = [jnp.where(odd, a, b) for a, b in zip(across, inside)]
    upper = lax.rem(zg, 2) == 1
    zp = jnp.where(upper, z_even_ref[...], z_odd_ref[...])
    zn = jnp.where(upper, z_odd_ref[...], z_even_ref[...])
    has_south = jnp.where(gy > 0, 1.0, 0.0)
    has_north = jnp.where(gy < NGY - 1, 1.0, 0.0)
    has_below = jnp.where(zg > 0, 1.0, 0.0)
    has_above = jnp.where(zg < NZG - 1, 1.0, 0.0)
    row = rows_of((NZB, NX), 0)
    sources = []
    g4 = None
    for y in range(NB):
        b = inner_ref[y]
        if y == 0:
            b = b + face(block_row(k_ref, y), yp[1] * has_south) * (yp[0] - block_row(t_ref, y))
        if y == NB - 1:
            g4 = face(block_row(k_ref, y), yn[1] * has_north)
            b = b + g4 * (yn[0] - block_row(t_ref, y))
        k_low, k_high = k_ref[y, :1], k_ref[y, NZB - 1:]
        below = face(k_low, zp[1, y:y + 1] * has_below) * (zp[0, y:y + 1] - t_ref[y, :1])
        top = face(k_high, zn[1, y:y + 1] * has_above)
        top_ref[y:y + 1] = top
        above = top * (zn[0, y:y + 1] - t_ref[y, NZB - 1:])
        b = b + jnp.where(row == 0, below, 0.0) + jnp.where(row == NZB - 1, above, 0.0)
        sources.append(b)
    solved = []
    for h in range(NB // 2):
        turned[h] = jnp.concatenate(sources[2 * h:2 * h + 2], axis=0).T
        plan = get_plan(x_plan_ref, (h,), XC)
        b, over = fold_sources(plan, split(block_line(turned, h)))
        head = separator_solve([x_ends_ref[h, j] for j in range(2 * len(STRIDES) + 1)], b[0] + shift(over, 1, 0))
        for a, x in enumerate(unfold(plan, b, head, shift(head, -1, 0))):
            turned[h, pl.ds(a, LANES, stride=XC), :] = x
        b = turned[h].T
        solved += [b[:NZB], b[NZB:]]
    b0, b1, b2, b3 = solved
    g1, g2, g3 = faces_ref[0], faces_ref[1], faces_ref[2]
    i1 = 1.0 / (1.0 + g1 + g2)
    left, right = g1 * i1, g2 * i1
    source = b0 + left * b1
    b2 = b2 + right * b1
    leak = 1.0 + left
    m2 = 1.0 + right
    a2 = g1 * right
    i2 = 1.0 / (m2 + a2 + g3)
    left, right = a2 * i2, g3 * i2
    source = source + left * b2
    b3 = b3 + right * b2
    leak = leak + left * m2
    m3 = 1.0 + right * m2
    a3 = a2 * right
    i3 = 1.0 / (m3 + a3 + g4)
    left, right = a3 * i3, g4 * i3

    def put(v, x):
        for a, part in enumerate(split(x)):
            bundle_ref[pl.ds(VALUES * a + v, LANES, stride=VALUES * ZC), :] = part

    put(0, leak + left * m3)
    put(1, right * m3)
    put(2, a3 * right)
    put(3, source + left * b3)
    put(4, right * b3)
    beta, lam, rho = b3 * i3, left, right
    back_ref[0, 2], back_ref[1, 2], back_ref[2, 2] = beta, lam, rho
    beta, lam, rho = (b2 + g3 * beta) * i2, (a2 + g3 * lam) * i2, g3 * rho * i2
    back_ref[0, 1], back_ref[1, 1], back_ref[2, 1] = beta, lam, rho
    beta, lam, rho = (b1 + g2 * beta) * i1, (g1 + g2 * lam) * i1, g2 * rho * i1
    back_ref[0, 0], back_ref[1, 0], back_ref[2, 0] = beta, lam, rho


def column_kernel(bundle_ref, out_ref):
    get = lambda v: [bundle_ref[pl.ds(VALUES * a + v, LANES, stride=VALUES * YC), :] for a in range(YC)]
    joined = lambda own, pushed: split(jnp.concatenate(own, axis=0) + before(jnp.concatenate(pushed, axis=0)))
    plan, leak, over, couple = fold(joined(get(0), get(1)), get(2))
    b, over_source = fold_sources(plan, joined(get(3), get(4)))
    factors = separator_factors(leak + shift(over, 1, 0), shift(couple, 1, 0), couple)
    head = separator_solve(factors, b[0] + shift(over_source, 1, 0))
    following = shift(head, -1, 0)
    x = unfold(plan, b, head, following) + [following]
    for a in range(YC):
        out_ref[pl.ds(2 * a, LANES, stride=2 * YC), :] = x[a]
        out_ref[pl.ds(2 * a + 1, LANES, stride=2 * YC), :] = x[a + 1]


def second_kernel(ends_ref, back_ref, spikes_ref, coeffs_ref, top_ref, second_ref, sums_ref, last_row_ref):
    get = lambda v: jnp.concatenate(
        [ends_ref[pl.ds(2 * a + v, LANES, stride=2 * ZC), :] for a in range(ZC)], axis=0)
    own, following = get(0), get(1)
    firsts, lasts = [], []
    for y in range(NB):
        if y == 0:
            u = own
        else:
            u = back_ref[0, y - 1] + back_ref[1, y - 1] * own + back_ref[2, y - 1] * following
        second_ref[y] = u
        firsts.append(jnp.sum(spikes_ref[0, y] * u, axis=0, keepdims=True))
        lasts.append(jnp.sum(spikes_ref[1, y] * u, axis=0, keepdims=True))
    first, last = jnp.concatenate(firsts, axis=0), jnp.concatenate(lasts, axis=0)
    leak, couple, top = coeffs_ref[1], coeffs_ref[2], top_ref[...]
    inverse = 1.0 / (leak + couple + top)
    left, right = couple * inverse, top * inverse
    sums_ref[0] = coeffs_ref[0] + left * leak
    sums_ref[1] = right * leak
    sums_ref[2] = left * top
    sums_ref[3] = first + left * last
    sums_ref[4] = right * last
    last_row_ref[0] = last * inverse
    last_row_ref[1] = left
    last_row_ref[2] = right


def local_z_kernel(second_ref, z_plan_ref, z_ends_ref, t_ref, out_ref):
    chunk = rows_of((LANES, NX), 0)
    for y in range(NB):
        plan = get_plan(z_plan_ref, (y,), ZC)
        b, over = fold_sources(plan, split(second_ref[y]))
        b0 = jnp.where(chunk > 0, b[0] + shift(over, 1, 0), 0.0)
        head = separator_solve([z_ends_ref[y, j] for j in range(2 * len(STRIDES) + 1)], b0)
        following = jnp.where(chunk == LANES - 1, 0.0, shift(head, -1, 0))
        x = jnp.concatenate(unfold(plan, b, head, following), axis=0)
        out_ref[y] = block_row(t_ref, y) + x


def last_kernel(local_ref, spikes_ref, last_row_ref, e0_ref, e1_ref, e2_ref, e3_ref, out_hbm, line, ends,
                rows, sems):
    zg = lax.axis_index("zg")
    for j, e_ref in enumerate((e0_ref, e1_ref, e2_ref, e3_ref)):
        line[lax.bitwise_xor(zg, j)] = e_ref[...]
    inverses, sources = [], []
    leak, source = line[0, 0], line[0, 3]
    for d in range(NZG):
        couple = line[d, 2]
        inverse = 1.0 / (leak + couple)
        inverses.append(inverse)
        sources.append(source)
        if d + 1 < NZG:
            passed = couple * inverse
            leak = line[d + 1, 0] + line[d, 1] + passed * leak
            source = line[d + 1, 3] + line[d, 4] + passed * source
    value = jnp.zeros_like(source)
    ends[NZG] = value
    for d in reversed(range(NZG)):
        value = (sources[d] + line[d, 2] * value) * inverses[d]
        ends[d] = value
    own = ends[zg]
    following = last_row_ref[0] + last_row_ref[1] * own + last_row_ref[2] * ends[zg + 1]
    copies = []
    for y in range(NB):
        x = local_ref[y] + spikes_ref[0, y] * own[y:y + 1] + spikes_ref[1, y] * following[y:y + 1]
        for a, part in enumerate(split(x)):
            rows[y, pl.ds(a, LANES, stride=ZC), :] = part
        copies.append(pltpu.make_async_copy(rows.at[y], out_hbm.at[y], sems.at[y]))
        copies[-1].start()
    for copy in copies:
        copy.wait()


def call(kernel, name, outs, args, scratch=(), cost=2000000, granted=0, result=False):
    shapes = [jax.ShapeDtypeStruct(o, jnp.float32) for o in outs]
    vmem = pl.BlockSpec(memory_space=pltpu.VMEM)
    return pl.pallas_call(
        kernel,
        name=name,
        out_shape=shapes,
        in_specs=[pl.BlockSpec(memory_space=pltpu.HBM)] * len(args) if granted else [vmem] * len(args),
        out_specs=[pl.BlockSpec(memory_space=pltpu.HBM) if result else vmem] * len(outs),
        scratch_shapes=scratch,
        cost_estimate=pl.CostEstimate(flops=cost, bytes_accessed=cost, transcendentals=0),
        compiler_params=pltpu.CompilerParams(vmem_limit_bytes=(granted or 24576) * 1024),
    )(*args)


def swapped(x, axis, first):
    pairs = []
    for zg in range(NZG):
        for gy in range(NGY):
            place, count = (zg, NZG) if axis == "zg" else (gy, NGY)
            partner = ((place - first) ^ 1) + first
            if not 0 <= partner < count:
                target = (zg, gy ^ 1) if axis == "zg" else (zg ^ 1, gy)
            else:
                target = (partner, gy) if axis == "zg" else (zg, partner)
            pairs.append((zg * NGY + gy, target[0] * NGY + target[1]))
    return lax.ppermute(x, ("zg", "gy"), pairs)


def crossed(x, axis, by):
    return lax.ppermute(x, axis, [(i, i ^ by) for i in range(lax.axis_size(axis))])


def shards(t, k):
    block = (NB, NZB, NX)
    t, k, across, inside, z_even, z_odd = call(
        load_kernel, "load", [block, block, (2, NZB, NX), (2, NZB, NX), (2, NB, NX), (2, NB, NX)], [t, k],
        scratch=[pltpu.SemaphoreType.DMA((2,))], granted=LOAD_GRANT)
    across = swapped(across, "gy", 1)
    z_odd = swapped(z_odd, "zg", 1)
    z_even = swapped(z_even, "zg", 0)
    inside = swapped(inside, "gy", 0)
    turned = pltpu.VMEM((NB // 2, NX, 2 * NZB), jnp.float32)
    ends = (2 * len(STRIDES) + 1, LANES, NX)
    inner, faces, x_plan, x_ends, z_plan, z_ends, spikes, coeffs = call(
        inner_kernel, "inner",
        [block, (NB - 1, NZB, NX), (NB // 2, XC - 1, 3, LANES, 2 * NZB), (NB // 2,) + ends,
         (NB, ZC - 1, 3, LANES, NX), (NB,) + ends, (2,) + block, (3, NB, NX)], [t, k], scratch=[turned])
    bundle, back, top = call(
        first_kernel, "first", [(NZB * VALUES, NX), (3, NB - 1, NZB, NX), (NB, NX)],
        [t, k, inner, faces, x_plan, x_ends, inside, across, z_even, z_odd], scratch=[turned])
    columns = lax.all_to_all(bundle.reshape(NZB * VALUES, 1, NX), "gy", split_axis=0, concat_axis=0, tiled=True)
    (ends,) = call(column_kernel, "column", [(2 * NGY, NX)], [columns.reshape(NGY * VALUES, NX)])
    ends = lax.all_to_all(ends, "gy", split_axis=0, concat_axis=0, tiled=True)
    second, sums, last_row = call(
        second_kernel, "second", [block, (5, NB, NX), (3, NB, NX)], [ends, back, spikes, coeffs, top])
    sums = [sums] + [crossed(sums, "zg", j) for j in range(1, NZG)]
    (local,) = call(local_z_kernel, "local_z", [block], [second, z_plan, z_ends, t])
    (out,) = call(last_kernel, "last", [block], [local, spikes, last_row] + sums,
                  scratch=[pltpu.VMEM((NZG, 5, NB, NX), jnp.float32), pltpu.VMEM((NZG + 1, NB, NX), jnp.float32),
                           pltpu.VMEM(block, jnp.float32), pltpu.SemaphoreType.DMA((NB,))], result=True)
    return out


def solution(mesh):
    return jax.shard_map(
        shards,
        mesh=mesh,
        in_specs=(P("gy", "zg", None), P("gy", "zg", None)),
        out_specs=P("gy", "zg", None),
        check_vma=False,
    )
```

```python
import jax
import jax.numpy as jnp
from jax import lax
from jax.experimental import pallas as pl
from jax.experimental.pallas import tpu as pltpu
from jax.sharding import PartitionSpec as P

mesh_courant_number = 300.0

NB, NZB, NX = 4, 64, 128
NGY, NZG = 64, 4
LANES = 8
XC, ZC, YC = NX // LANES, NZB // LANES, NGY // LANES
STRIDES = (1, 2, 4)
VALUES = 5

LOAD_GRANT = 54816


def face(k, q):
    return (2.0 * mesh_courant_number) * k * q / (k + q)


def shift(v, by, axis):
    return pltpu.roll(v, by % v.shape[axis], axis)


def rows_of(shape, axis):
    return lax.broadcasted_iota(jnp.int32, shape, axis)


def chunked(load, count):
    return jnp.concatenate([load(pl.ds(a, LANES, stride=count)) for a in range(count)], axis=0)


def split(v):
    return [v[LANES * a:LANES * (a + 1)] for a in range(v.shape[0] // LANES)]


def before(v):
    last = v.shape[0] - LANES
    return jnp.concatenate([shift(v[last:], 1, 0), v[:last]], axis=0)


def after(v):
    return jnp.concatenate([v[LANES:], shift(v[:LANES], -1, 0)], axis=0)


def order(count):
    step = 1
    while step < count:
        for a in range(step, count, 2 * step):
            yield a, step
        step *= 2


def fold(leaks, couples, closed=None):
    leaks, couples, plan, over = list(leaks), list(couples), [], 0.0
    count = len(leaks)
    for a, step in order(count):
        low, high = couples[a - step], couples[a]
        inverse = 1.0 / (leaks[a] + low + high)
        left, right = low * inverse, high * inverse
        if closed is not None and a == count - 1:
            inverse = jnp.where(closed, 0.0, inverse)
            left = jnp.where(closed, 0.0, left)
            right = jnp.where(closed, 1.0, right)
        plan.append((inverse, left, right))
        leaks[a - step] = leaks[a - step] + left * leaks[a]
        if a + step < count:
            leaks[a + step] = leaks[a + step] + right * leaks[a]
        else:
            over = over + right * leaks[a]
        couples[a - step] = low * right
    return plan, leaks[0], over, couples[0]


def fold_sources(plan, sources):
    sources, over = list(sources), 0.0
    count = len(sources)
    for (a, step), (_, left, right) in zip(order(count), plan):
        sources[a - step] = sources[a - step] + left * sources[a]
        if a + step < count:
            sources[a + step] = sources[a + step] + right * sources[a]
        else:
            over = over + right * sources[a]
    return sources, over


def unfold(plan, sources, head, following):
    count = len(plan) + 1
    x = [head] + [None] * (count - 1) + [following]
    for (a, step), (inverse, left, right) in reversed(list(zip(order(count), plan))):
        x[a] = left * x[a - step] + right * x[min(a + step, count)]
        if sources is not None:
            x[a] = x[a] + inverse * sources[a]
    return x[:count]


def put_plan(ref, at, plan):
    for i, entries in enumerate(plan):
        for j, entry in enumerate(entries):
            ref[at + (i, j)] = entry


def get_plan(ref, at, count):
    return [tuple(ref[at + (i, j)] for j in range(3)) for i in range(count - 1)]


def separator_factors(leak, low, high):
    factors = []
    for s in STRIDES:
        inverse = 1.0 / (leak + low + high)
        from_low = low * shift(inverse, s, 0)
        from_high = high * shift(inverse, -s, 0)
        factors += [from_low, from_high]
        leak = leak + from_low * shift(leak, s, 0) + from_high * shift(leak, -s, 0)
        low = from_low * shift(low, s, 0)
        high = from_high * shift(high, -s, 0)
    return factors + [1.0 / (leak + low + high)]


def separator_solve(factors, b):
    for j, s in enumerate(STRIDES):
        b = b + factors[2 * j] * shift(b, s, 0) + factors[2 * j + 1] * shift(b, -s, 0)
    return b * factors[2 * len(STRIDES)]


def load_kernel(t_hbm, k_hbm, t_ref, k_ref, across_ref, inside_ref, z_even_ref, z_odd_ref, sems):
    odd = lax.rem(lax.axis_index("gy"), 2)
    upper = lax.rem(lax.axis_index("zg"), 2) == 1
    copies = [pltpu.make_async_copy(t_hbm, t_ref, sems.at[0]), pltpu.make_async_copy(k_hbm, k_ref, sems.at[1])]
    for copy in copies:
        copy.start()
    for j, (copy, ref) in enumerate(zip(copies, (t_ref, k_ref))):
        copy.wait()
        across_ref[j] = ref[odd * (NB - 1)]
        inside_ref[j] = ref[(1 - odd) * (NB - 1)]
        for y in range(NB):
            first, last = ref[y, :1], ref[y, NZB - 1:]
            z_even_ref[j, y:y + 1] = jnp.where(upper, first, last)
            z_odd_ref[j, y:y + 1] = jnp.where(upper, last, first)


def block_row(ref, *at):
    return chunked(lambda rows: ref[at + (rows, slice(None))], ZC)


def inner_kernel(t_ref, k_ref, inner_ref, faces_ref, x_plan_ref, x_ends_ref, z_plan_ref, z_ends_ref, spikes_ref,
                 coeffs_ref, turned):
    lane = rows_of((NZB, NX), 1)
    row = rows_of((NZB, NX), 0)
    chunk = rows_of((LANES, NX), 0)
    ts = [block_row(t_ref, y) for y in range(NB)]
    ks = [block_row(k_ref, y) for y in range(NB)]
    flux_y = None
    for y in range(NB):
        k, t = ks[y], ts[y]
        low = jnp.where(lane > 0, face(k, shift(k, 1, 1)), 0.0)
        flux = low * (t - shift(t, 1, 1))
        total = shift(flux, -1, 1) - flux
        face_z = jnp.where(row > 0, face(k, before(k)), 0.0)
        flux = face_z * (t - before(t))
        total = total + (after(flux) - flux)
        if y > 0:
            total = total - flux_y
        if y < NB - 1:
            next_face = face(ks[y + 1], k)
            faces_ref[y] = next_face
            flux_y = next_face * (ts[y + 1] - t)
            total = total + flux_y
        inner_ref[y] = total

        ones = [jnp.ones((LANES, NX), jnp.float32)] * ZC
        plan, leak, over, couple = fold(ones, split(after(face_z)), chunk == LANES - 1)
        put_plan(z_plan_ref, (y,), plan)
        over = shift(over, 1, 0)
        leak_end = over[:1]
        leak = leak + jnp.where(chunk > 0, over, 0.0)
        low = shift(couple, 1, 0)
        at_first = jnp.where(chunk == 1, low, 0.0)
        at_last = jnp.where(chunk == LANES - 1, couple, 0.0)
        factors = separator_factors(leak + at_first + at_last, jnp.where(chunk > 1, low, 0.0),
                                    jnp.where((chunk > 0) & (chunk < LANES - 1), couple, 0.0))
        for j, factor in enumerate(factors):
            z_ends_ref[y, j] = factor
        lam = jnp.where(chunk == 0, 1.0, separator_solve(factors, at_first))
        rho = separator_solve(factors, at_last)
        coeffs_ref[0, y:y + 1] = jnp.sum(lam * leak, axis=0, keepdims=True)
        coeffs_ref[1, y:y + 1] = jnp.sum(rho * leak, axis=0, keepdims=True) + leak_end
        coeffs_ref[2, y:y + 1] = couple[LANES - 1:] * lam[LANES - 1:]
        following = jnp.where(chunk == LANES - 1, 0.0, shift(lam, -1, 0))
        spikes_ref[0, y] = jnp.concatenate(unfold(plan, None, lam, following), axis=0)
        following = jnp.where(chunk == LANES - 1, 1.0, shift(rho, -1, 0))
        spikes_ref[1, y] = jnp.concatenate(unfold(plan, None, rho, following), axis=0)

    for h in range(NB // 2):
        turned[h] = jnp.concatenate(ks[2 * h:2 * h + 2], axis=0).T
        k = block_line(turned, h)
        couples = face(k, after(k))
        couples = jnp.where((rows_of(couples.shape, 0) == NX - 1), 0.0, couples)
        ones = [jnp.ones((LANES, 2 * NZB), jnp.float32)] * XC
        plan, leak, over, couple = fold(ones, split(couples))
        put_plan(x_plan_ref, (h,), plan)
        factors = separator_factors(leak + shift(over, 1, 0), shift(couple, 1, 0), couple)
        for j, factor in enumerate(factors):
            x_ends_ref[h, j] = factor


def block_line(ref, h):
    return chunked(lambda rows: ref[h, rows, :], XC)


def first_kernel(t_ref, k_ref, inner_ref, faces_ref, x_plan_ref, x_ends_ref, inside_ref, across_ref, z_even_ref, z_odd_ref,
                 bundle_ref, back_ref, top_ref, turned):
    gy = lax.axis_index("gy")
    zg = lax.axis_index("zg")
    odd = lax.rem(gy, 2) == 1
    across = [block_row(across_ref, j) for j in range(2)]
    inside = [block_row(inside_ref, j) for j in range(2)]
    yp = [jnp.where(odd, b, a) for a, b in zip(across, inside)]
    yn = [jnp.where(odd, a, b) for a, b in zip(across, inside)]
    upper = lax.rem(zg, 2) == 1
    zp = jnp.where(upper, z_even_ref[...], z_odd_ref[...])
    zn = jnp.where(upper, z_odd_ref[...], z_even_ref[...])
    has_south = jnp.where(gy > 0, 1.0, 0.0)
    has_north = jnp.where(gy < NGY - 1, 1.0, 0.0)
    has_below = jnp.where(zg > 0, 1.0, 0.0)
    has_above = jnp.where(zg < NZG - 1, 1.0, 0.0)
    row = rows_of((NZB, NX), 0)
    sources = []
    g4 = None
    for y in range(NB):
        b = inner_ref[y]
        if y == 0:
            b = b + face(block_row(k_ref, y), yp[1] * has_south) * (yp[0] - block_row(t_ref, y))
        if y == NB - 1:
            g4 = face(block_row(k_ref, y), yn[1] * has_north)
            b = b + g4 * (yn[0] - block_row(t_ref, y))
        k_low, k_high = k_ref[y, :1], k_ref[y, NZB - 1:]
        below = face(k_low, zp[1, y:y + 1] * has_below) * (zp[0, y:y + 1] - t_ref[y, :1])
        top = face(k_high, zn[1, y:y + 1] * has_above)
        top_ref[y:y + 1] = top
        above = top * (zn[0, y:y + 1] - t_ref[y, NZB - 1:])
        b = b + jnp.where(row == 0, below, 0.0) + jnp.where(row == NZB - 1, above, 0.0)
        sources.append(b)
    solved = []
    for h in range(NB // 2):
        turned[h] = jnp.concatenate(sources[2 * h:2 * h + 2], axis=0).T
        plan = get_plan(x_plan_ref, (h,), XC)
        b, over = fold_sources(plan, split(block_line(turned, h)))
        head = separator_solve([x_ends_ref[h, j] for j in range(2 * len(STRIDES) + 1)], b[0] + shift(over, 1, 0))
        for a, x in enumerate(unfold(plan, b, head, shift(head, -1, 0))):
            turned[h, pl.ds(a, LANES, stride=XC), :] = x
        b = turned[h].T
        solved += [b[:NZB], b[NZB:]]
    b0, b1, b2, b3 = solved
    g1, g2, g3 = faces_ref[0], faces_ref[1], faces_ref[2]
    i1 = 1.0 / (1.0 + g1 + g2)
    left, right = g1 * i1, g2 * i1
    source = b0 + left * b1
    b2 = b2 + right * b1
    leak = 1.0 + left
    m2 = 1.0 + right
    a2 = g1 * right
    i2 = 1.0 / (m2 + a2 + g3)
    left, right = a2 * i2, g3 * i2
    source = source + left * b2
    b3 = b3 + right * b2
    leak = leak + left * m2
    m3 = 1.0 + right * m2
    a3 = a2 * right
    i3 = 1.0 / (m3 + a3 + g4)
    left, right = a3 * i3, g4 * i3

    def put(v, x):
        for a, part in enumerate(split(x)):
            bundle_ref[pl.ds(VALUES * a + v, LANES, stride=VALUES * ZC), :] = part

    put(0, leak + left * m3)
    put(1, right * m3)
    put(2, a3 * right)
    put(3, source + left * b3)
    put(4, right * b3)
    beta, lam, rho = b3 * i3, left, right
    back_ref[0, 2], back_ref[1, 2], back_ref[2, 2] = beta, lam, rho
    beta, lam, rho = (b2 + g3 * beta) * i2, (a2 + g3 * lam) * i2, g3 * rho * i2
    back_ref[0, 1], back_ref[1, 1], back_ref[2, 1] = beta, lam, rho
    beta, lam, rho = (b1 + g2 * beta) * i1, (g1 + g2 * lam) * i1, g2 * rho * i1
    back_ref[0, 0], back_ref[1, 0], back_ref[2, 0] = beta, lam, rho


def column_kernel(bundle_ref, out_ref):
    get = lambda v: [bundle_ref[pl.ds(VALUES * a + v, LANES, stride=VALUES * YC), :] for a in range(YC)]
    joined = lambda own, pushed: split(jnp.concatenate(own, axis=0) + before(jnp.concatenate(pushed, axis=0)))
    plan, leak, over, couple = fold(joined(get(0), get(1)), get(2))
    b, over_source = fold_sources(plan, joined(get(3), get(4)))
    factors = separator_factors(leak + shift(over, 1, 0), shift(couple, 1, 0), couple)
    head = separator_solve(factors, b[0] + shift(over_source, 1, 0))
    following = shift(head, -1, 0)
    x = unfold(plan, b, head, following) + [following]
    for a in range(YC):
        out_ref[pl.ds(2 * a, LANES, stride=2 * YC), :] = x[a]
        out_ref[pl.ds(2 * a + 1, LANES, stride=2 * YC), :] = x[a + 1]


def second_kernel(ends_ref, back_ref, spikes_ref, coeffs_ref, top_ref, second_ref, sums_ref, last_row_ref):
    get = lambda v: jnp.concatenate(
        [ends_ref[pl.ds(2 * a + v, LANES, stride=2 * ZC), :] for a in range(ZC)], axis=0)
    own, following = get(0), get(1)
    firsts, lasts = [], []
    for y in range(NB):
        if y == 0:
            u = own
        else:
            u = back_ref[0, y - 1] + back_ref[1, y - 1] * own + back_ref[2, y - 1] * following
        second_ref[y] = u
        firsts.append(jnp.sum(spikes_ref[0, y] * u, axis=0, keepdims=True))
        lasts.append(jnp.sum(spikes_ref[1, y] * u, axis=0, keepdims=True))
    first, last = jnp.concatenate(firsts, axis=0), jnp.concatenate(lasts, axis=0)
    leak, couple, top = coeffs_ref[1], coeffs_ref[2], top_ref[...]
    inverse = 1.0 / (leak + couple + top)
    left, right = couple * inverse, top * inverse
    sums_ref[0] = coeffs_ref[0] + left * leak
    sums_ref[1] = right * leak
    sums_ref[2] = left * top
    sums_ref[3] = first + left * last
    sums_ref[4] = right * last
    last_row_ref[0] = last * inverse
    last_row_ref[1] = left
    last_row_ref[2] = right


def local_z_kernel(second_ref, z_plan_ref, z_ends_ref, t_ref, out_ref):
    chunk = rows_of((LANES, NX), 0)
    for y in range(NB):
        plan = get_plan(z_plan_ref, (y,), ZC)
        b, over = fold_sources(plan, split(second_ref[y]))
        b0 = jnp.where(chunk > 0, b[0] + shift(over, 1, 0), 0.0)
        head = separator_solve([z_ends_ref[y, j] for j in range(2 * len(STRIDES) + 1)], b0)
        following = jnp.where(chunk == LANES - 1, 0.0, shift(head, -1, 0))
        x = jnp.concatenate(unfold(plan, b, head, following), axis=0)
        out_ref[y] = block_row(t_ref, y) + x


def last_kernel(local_ref, spikes_ref, last_row_ref, e0_ref, e1_ref, e2_ref, e3_ref, out_ref, line, ends):
    zg = lax.axis_index("zg")
    for j, e_ref in enumerate((e0_ref, e1_ref, e2_ref, e3_ref)):
        line[lax.bitwise_xor(zg, j)] = e_ref[...]
    inverses, sources = [], []
    leak, source = line[0, 0], line[0, 3]
    for d in range(NZG):
        couple = line[d, 2]
        inverse = 1.0 / (leak + couple)
        inverses.append(inverse)
        sources.append(source)
        if d + 1 < NZG:
            passed = couple * inverse
            leak = line[d + 1, 0] + line[d, 1] + passed * leak
            source = line[d + 1, 3] + line[d, 4] + passed * source
    value = jnp.zeros_like(source)
    ends[NZG] = value
    for d in reversed(range(NZG)):
        value = (sources[d] + line[d, 2] * value) * inverses[d]
        ends[d] = value
    own = ends[zg]
    following = last_row_ref[0] + last_row_ref[1] * own + last_row_ref[2] * ends[zg + 1]
    for y in range(NB):
        x = local_ref[y] + spikes_ref[0, y] * own[y:y + 1] + spikes_ref[1, y] * following[y:y + 1]
        for a, part in enumerate(split(x)):
            out_ref[y, pl.ds(a, LANES, stride=ZC), :] = part


def call(kernel, name, outs, args, scratch=(), cost=2000000, granted=0):
    shapes = [jax.ShapeDtypeStruct(o, jnp.float32) for o in outs]
    vmem = pl.BlockSpec(memory_space=pltpu.VMEM)
    return pl.pallas_call(
        kernel,
        name=name,
        out_shape=shapes,
        in_specs=[pl.BlockSpec(memory_space=pltpu.HBM)] * len(args) if granted else [vmem] * len(args),
        out_specs=[vmem] * len(outs),
        scratch_shapes=scratch,
        cost_estimate=pl.CostEstimate(flops=cost, bytes_accessed=cost, transcendentals=0),
        compiler_params=pltpu.CompilerParams(vmem_limit_bytes=(granted or 24576) * 1024),
    )(*args)


def swapped(x, axis, first):
    pairs = []
    for zg in range(NZG):
        for gy in range(NGY):
            place, count = (zg, NZG) if axis == "zg" else (gy, NGY)
            partner = ((place - first) ^ 1) + first
            if not 0 <= partner < count:
                target = (zg, gy ^ 1) if axis == "zg" else (zg ^ 1, gy)
            else:
                target = (partner, gy) if axis == "zg" else (zg, partner)
            pairs.append((zg * NGY + gy, target[0] * NGY + target[1]))
    return lax.ppermute(x, ("zg", "gy"), pairs)


def crossed(x, axis, by):
    return lax.ppermute(x, axis, [(i, i ^ by) for i in range(lax.axis_size(axis))])


def shards(t, k):
    block = (NB, NZB, NX)
    t, k, across, inside, z_even, z_odd = call(
        load_kernel, "load", [block, block, (2, NZB, NX), (2, NZB, NX), (2, NB, NX), (2, NB, NX)], [t, k],
        scratch=[pltpu.SemaphoreType.DMA((2,))], granted=LOAD_GRANT)
    across = swapped(across, "gy", 1)
    z_odd = swapped(z_odd, "zg", 1)
    z_even = swapped(z_even, "zg", 0)
    inside = swapped(inside, "gy", 0)
    turned = pltpu.VMEM((NB // 2, NX, 2 * NZB), jnp.float32)
    ends = (2 * len(STRIDES) + 1, LANES, NX)
    inner, faces, x_plan, x_ends, z_plan, z_ends, spikes, coeffs = call(
        inner_kernel, "inner",
        [block, (NB - 1, NZB, NX), (NB // 2, XC - 1, 3, LANES, 2 * NZB), (NB // 2,) + ends,
         (NB, ZC - 1, 3, LANES, NX), (NB,) + ends, (2,) + block, (3, NB, NX)], [t, k], scratch=[turned])
    bundle, back, top = call(
        first_kernel, "first", [(NZB * VALUES, NX), (3, NB - 1, NZB, NX), (NB, NX)],
        [t, k, inner, faces, x_plan, x_ends, inside, across, z_even, z_odd], scratch=[turned])
    columns = lax.all_to_all(bundle.reshape(NZB * VALUES, 1, NX), "gy", split_axis=0, concat_axis=0, tiled=True)
    (ends,) = call(column_kernel, "column", [(2 * NGY, NX)], [columns.reshape(NGY * VALUES, NX)])
    ends = lax.all_to_all(ends.reshape(2 * NGY, 1, NX), "gy", split_axis=0, concat_axis=0, tiled=True)
    ends = ends.reshape(2 * NZB, NX)
    second, sums, last_row = call(
        second_kernel, "second", [block, (5, NB, NX), (3, NB, NX)], [ends, back, spikes, coeffs, top])
    sums = [sums] + [crossed(sums, "zg", j) for j in range(1, NZG)]
    (local,) = call(local_z_kernel, "local_z", [block], [second, z_plan, z_ends, t])
    (out,) = call(last_kernel, "last", [block], [local, spikes, last_row] + sums,
                  scratch=[pltpu.VMEM((NZG, 5, NB, NX), jnp.float32), pltpu.VMEM((NZG + 1, NB, NX), jnp.float32)])
    return out


def solution(mesh):
    return jax.shard_map(
        shards,
        mesh=mesh,
        in_specs=(P("gy", "zg", None), P("gy", "zg", None)),
        out_specs=P("gy", "zg", None),
        check_vma=False,
    )
```

```python
import jax
import jax.numpy as jnp
from jax import lax
from jax.experimental import pallas as pl
from jax.experimental.pallas import tpu as pltpu
from jax.sharding import PartitionSpec as P

mesh_courant_number = 300.0

NB, NZB, NX = 4, 64, 128
NGY, NZG = 64, 4
LANES = 8
XC, ZC, YC = NX // LANES, NZB // LANES, NGY // LANES
STRIDES = (1, 2, 4)
VALUES = 5

LOAD_GRANT = 54816


def face(k, q):
    return (2.0 * mesh_courant_number) * k * q / (k + q)


def shift(v, by, axis):
    return pltpu.roll(v, by % v.shape[axis], axis)


def rows_of(shape, axis):
    return lax.broadcasted_iota(jnp.int32, shape, axis)


def chunked(load, count):
    return jnp.concatenate([load(pl.ds(a, LANES, stride=count)) for a in range(count)], axis=0)


def split(v):
    return [v[LANES * a:LANES * (a + 1)] for a in range(v.shape[0] // LANES)]


def before(v):
    last = v.shape[0] - LANES
    return jnp.concatenate([shift(v[last:], 1, 0), v[:last]], axis=0)


def after(v):
    return jnp.concatenate([v[LANES:], shift(v[:LANES], -1, 0)], axis=0)


def order(count):
    step = 1
    while step < count:
        for a in range(step, count, 2 * step):
            yield a, step
        step *= 2


def fold(leaks, couples, closed=None):
    leaks, couples, plan, over = list(leaks), list(couples), [], 0.0
    count = len(leaks)
    for a, step in order(count):
        low, high = couples[a - step], couples[a]
        inverse = 1.0 / (leaks[a] + low + high)
        left, right = low * inverse, high * inverse
        if closed is not None and a == count - 1:
            inverse = jnp.where(closed, 0.0, inverse)
            left = jnp.where(closed, 0.0, left)
            right = jnp.where(closed, 1.0, right)
        plan.append((inverse, left, right))
        leaks[a - step] = leaks[a - step] + left * leaks[a]
        if a + step < count:
            leaks[a + step] = leaks[a + step] + right * leaks[a]
        else:
            over = over + right * leaks[a]
        couples[a - step] = low * right
    return plan, leaks[0], over, couples[0]


def fold_sources(plan, sources):
    sources, over = list(sources), 0.0
    count = len(sources)
    for (a, step), (_, left, right) in zip(order(count), plan):
        sources[a - step] = sources[a - step] + left * sources[a]
        if a + step < count:
            sources[a + step] = sources[a + step] + right * sources[a]
        else:
            over = over + right * sources[a]
    return sources, over


def unfold(plan, sources, head, following):
    count = len(plan) + 1
    x = [head] + [None] * (count - 1) + [following]
    for (a, step), (inverse, left, right) in reversed(list(zip(order(count), plan))):
        x[a] = left * x[a - step] + right * x[min(a + step, count)]
        if sources is not None:
            x[a] = x[a] + inverse * sources[a]
    return x[:count]


def put_plan(ref, at, plan):
    for i, entries in enumerate(plan):
        for j, entry in enumerate(entries):
            ref[at + (i, j)] = entry


def get_plan(ref, at, count):
    return [tuple(ref[at + (i, j)] for j in range(3)) for i in range(count - 1)]


def separator_factors(leak, low, high):
    factors = []
    for s in STRIDES:
        inverse = 1.0 / (leak + low + high)
        from_low = low * shift(inverse, s, 0)
        from_high = high * shift(inverse, -s, 0)
        factors += [from_low, from_high]
        leak = leak + from_low * shift(leak, s, 0) + from_high * shift(leak, -s, 0)
        low = from_low * shift(low, s, 0)
        high = from_high * shift(high, -s, 0)
    return factors + [1.0 / (leak + low + high)]


def separator_solve(factors, b):
    for j, s in enumerate(STRIDES):
        b = b + factors[2 * j] * shift(b, s, 0) + factors[2 * j + 1] * shift(b, -s, 0)
    return b * factors[2 * len(STRIDES)]


def load_kernel(t_hbm, k_hbm, t_ref, k_ref, across_ref, inside_ref, z_even_ref, z_odd_ref, sems):
    odd = lax.rem(lax.axis_index("gy"), 2)
    upper = lax.rem(lax.axis_index("zg"), 2) == 1
    copies = [pltpu.make_async_copy(t_hbm, t_ref, sems.at[0]), pltpu.make_async_copy(k_hbm, k_ref, sems.at[1])]
    for copy in copies:
        copy.start()
    for j, (copy, ref) in enumerate(zip(copies, (t_ref, k_ref))):
        copy.wait()
        across_ref[j] = ref[odd * (NB - 1)]
        inside_ref[j] = ref[(1 - odd) * (NB - 1)]
        for y in range(NB):
            first, last = ref[y, :1], ref[y, NZB - 1:]
            z_even_ref[j, y:y + 1] = jnp.where(upper, first, last)
            z_odd_ref[j, y:y + 1] = jnp.where(upper, last, first)


def block_row(ref, *at):
    return chunked(lambda rows: ref[at + (rows, slice(None))], ZC)


def inner_kernel(t_ref, k_ref, inner_ref, faces_ref, x_plan_ref, x_ends_ref, z_plan_ref, z_ends_ref, spikes_ref,
                 coeffs_ref, turned):
    lane = rows_of((NZB, NX), 1)
    row = rows_of((NZB, NX), 0)
    chunk = rows_of((LANES, NX), 0)
    ts = [block_row(t_ref, y) for y in range(NB)]
    ks = [block_row(k_ref, y) for y in range(NB)]
    flux_y = None
    for y in range(NB):
        k, t = ks[y], ts[y]
        low = jnp.where(lane > 0, face(k, shift(k, 1, 1)), 0.0)
        flux = low * (t - shift(t, 1, 1))
        total = shift(flux, -1, 1) - flux
        face_z = jnp.where(row > 0, face(k, before(k)), 0.0)
        flux = face_z * (t - before(t))
        total = total + (after(flux) - flux)
        if y > 0:
            total = total - flux_y
        if y < NB - 1:
            next_face = face(ks[y + 1], k)
            faces_ref[y] = next_face
            flux_y = next_face * (ts[y + 1] - t)
            total = total + flux_y
        inner_ref[y] = total

        ones = [jnp.ones((LANES, NX), jnp.float32)] * ZC
        plan, leak, over, couple = fold(ones, split(after(face_z)), chunk == LANES - 1)
        put_plan(z_plan_ref, (y,), plan)
        over = shift(over, 1, 0)
        leak_end = over[:1]
        leak = leak + jnp.where(chunk > 0, over, 0.0)
        low = shift(couple, 1, 0)
        at_first = jnp.where(chunk == 1, low, 0.0)
        at_last = jnp.where(chunk == LANES - 1, couple, 0.0)
        factors = separator_factors(leak + at_first + at_last, jnp.where(chunk > 1, low, 0.0),
                                    jnp.where((chunk > 0) & (chunk < LANES - 1), couple, 0.0))
        for j, factor in enumerate(factors):
            z_ends_ref[y, j] = factor
        lam = jnp.where(chunk == 0, 1.0, separator_solve(factors, at_first))
        rho = separator_solve(factors, at_last)
        coeffs_ref[0, y:y + 1] = jnp.sum(lam * leak, axis=0, keepdims=True)
        coeffs_ref[1, y:y + 1] = jnp.sum(rho * leak, axis=0, keepdims=True) + leak_end
        coeffs_ref[2, y:y + 1] = couple[LANES - 1:] * lam[LANES - 1:]
        following = jnp.where(chunk == LANES - 1, 0.0, shift(lam, -1, 0))
        spikes_ref[0, y] = jnp.concatenate(unfold(plan, None, lam, following), axis=0)
        following = jnp.where(chunk == LANES - 1, 1.0, shift(rho, -1, 0))
        spikes_ref[1, y] = jnp.concatenate(unfold(plan, None, rho, following), axis=0)

    for h in range(NB // 2):
        turned[h] = jnp.concatenate(ks[2 * h:2 * h + 2], axis=0).T
        k = block_line(turned, h)
        couples = face(k, after(k))
        couples = jnp.where((rows_of(couples.shape, 0) == NX - 1), 0.0, couples)
        ones = [jnp.ones((LANES, 2 * NZB), jnp.float32)] * XC
        plan, leak, over, couple = fold(ones, split(couples))
        put_plan(x_plan_ref, (h,), plan)
        factors = separator_factors(leak + shift(over, 1, 0), shift(couple, 1, 0), couple)
        for j, factor in enumerate(factors):
            x_ends_ref[h, j] = factor


def block_line(ref, h):
    return chunked(lambda rows: ref[h, rows, :], XC)


def first_kernel(t_ref, k_ref, inner_ref, faces_ref, x_plan_ref, x_ends_ref, inside_ref, across_ref, z_odd_ref, z_even_ref,
                 bundle_ref, back_ref, top_ref, turned):
    gy = lax.axis_index("gy")
    zg = lax.axis_index("zg")
    odd = lax.rem(gy, 2) == 1
    across = [block_row(across_ref, j) for j in range(2)]
    inside = [block_row(inside_ref, j) for j in range(2)]
    yp = [jnp.where(odd, b, a) for a, b in zip(across, inside)]
    yn = [jnp.where(odd, a, b) for a, b in zip(across, inside)]
    upper = lax.rem(zg, 2) == 1
    zp = jnp.where(upper, z_even_ref[...], z_odd_ref[...])
    zn = jnp.where(upper, z_odd_ref[...], z_even_ref[...])
    has_south = jnp.where(gy > 0, 1.0, 0.0)
    has_north = jnp.where(gy < NGY - 1, 1.0, 0.0)
    has_below = jnp.where(zg > 0, 1.0, 0.0)
    has_above = jnp.where(zg < NZG - 1, 1.0, 0.0)
    row = rows_of((NZB, NX), 0)
    sources = []
    g4 = None
    for y in range(NB):
        b = inner_ref[y]
        if y == 0:
            b = b + face(block_row(k_ref, y), yp[1] * has_south) * (yp[0] - block_row(t_ref, y))
        if y == NB - 1:
            g4 = face(block_row(k_ref, y), yn[1] * has_north)
            b = b + g4 * (yn[0] - block_row(t_ref, y))
        k_low, k_high = k_ref[y, :1], k_ref[y, NZB - 1:]
        below = face(k_low, zp[1, y:y + 1] * has_below) * (zp[0, y:y + 1] - t_ref[y, :1])
        top = face(k_high, zn[1, y:y + 1] * has_above)
        top_ref[y:y + 1] = top
        above = top * (zn[0, y:y + 1] - t_ref[y, NZB - 1:])
        b = b + jnp.where(row == 0, below, 0.0) + jnp.where(row == NZB - 1, above, 0.0)
        sources.append(b)
    solved = []
    for h in range(NB // 2):
        turned[h] = jnp.concatenate(sources[2 * h:2 * h + 2], axis=0).T
        plan = get_plan(x_plan_ref, (h,), XC)
        b, over = fold_sources(plan, split(block_line(turned, h)))
        head = separator_solve([x_ends_ref[h, j] for j in range(2 * len(STRIDES) + 1)], b[0] + shift(over, 1, 0))
        for a, x in enumerate(unfold(plan, b, head, shift(head, -1, 0))):
            turned[h, pl.ds(a, LANES, stride=XC), :] = x
        b = turned[h].T
        solved += [b[:NZB], b[NZB:]]
    b0, b1, b2, b3 = solved
    g1, g2, g3 = faces_ref[0], faces_ref[1], faces_ref[2]
    i1 = 1.0 / (1.0 + g1 + g2)
    left, right = g1 * i1, g2 * i1
    source = b0 + left * b1
    b2 = b2 + right * b1
    leak = 1.0 + left
    m2 = 1.0 + right
    a2 = g1 * right
    i2 = 1.0 / (m2 + a2 + g3)
    left, right = a2 * i2, g3 * i2
    source = source + left * b2
    b3 = b3 + right * b2
    leak = leak + left * m2
    m3 = 1.0 + right * m2
    a3 = a2 * right
    i3 = 1.0 / (m3 + a3 + g4)
    left, right = a3 * i3, g4 * i3

    def put(v, x):
        for a, part in enumerate(split(x)):
            bundle_ref[pl.ds(VALUES * a + v, LANES, stride=VALUES * ZC), :] = part

    put(0, leak + left * m3)
    put(1, right * m3)
    put(2, a3 * right)
    put(3, source + left * b3)
    put(4, right * b3)
    beta, lam, rho = b3 * i3, left, right
    back_ref[0, 2], back_ref[1, 2], back_ref[2, 2] = beta, lam, rho
    beta, lam, rho = (b2 + g3 * beta) * i2, (a2 + g3 * lam) * i2, g3 * rho * i2
    back_ref[0, 1], back_ref[1, 1], back_ref[2, 1] = beta, lam, rho
    beta, lam, rho = (b1 + g2 * beta) * i1, (g1 + g2 * lam) * i1, g2 * rho * i1
    back_ref[0, 0], back_ref[1, 0], back_ref[2, 0] = beta, lam, rho


def column_kernel(bundle_ref, out_ref):
    get = lambda v: [bundle_ref[pl.ds(VALUES * a + v, LANES, stride=VALUES * YC), :] for a in range(YC)]
    joined = lambda own, pushed: split(jnp.concatenate(own, axis=0) + before(jnp.concatenate(pushed, axis=0)))
    plan, leak, over, couple = fold(joined(get(0), get(1)), get(2))
    b, over_source = fold_sources(plan, joined(get(3), get(4)))
    factors = separator_factors(leak + shift(over, 1, 0), shift(couple, 1, 0), couple)
    head = separator_solve(factors, b[0] + shift(over_source, 1, 0))
    following = shift(head, -1, 0)
    x = unfold(plan, b, head, following) + [following]
    for a in range(YC):
        out_ref[pl.ds(2 * a, LANES, stride=2 * YC), :] = x[a]
        out_ref[pl.ds(2 * a + 1, LANES, stride=2 * YC), :] = x[a + 1]


def second_kernel(ends_ref, back_ref, spikes_ref, coeffs_ref, top_ref, second_ref, sums_ref, last_row_ref):
    get = lambda v: jnp.concatenate(
        [ends_ref[pl.ds(2 * a + v, LANES, stride=2 * ZC), :] for a in range(ZC)], axis=0)
    own, following = get(0), get(1)
    firsts, lasts = [], []
    for y in range(NB):
        if y == 0:
            u = own
        else:
            u = back_ref[0, y - 1] + back_ref[1, y - 1] * own + back_ref[2, y - 1] * following
        second_ref[y] = u
        firsts.append(jnp.sum(spikes_ref[0, y] * u, axis=0, keepdims=True))
        lasts.append(jnp.sum(spikes_ref[1, y] * u, axis=0, keepdims=True))
    first, last = jnp.concatenate(firsts, axis=0), jnp.concatenate(lasts, axis=0)
    leak, couple, top = coeffs_ref[1], coeffs_ref[2], top_ref[...]
    inverse = 1.0 / (leak + couple + top)
    left, right = couple * inverse, top * inverse
    sums_ref[0] = coeffs_ref[0] + left * leak
    sums_ref[1] = right * leak
    sums_ref[2] = left * top
    sums_ref[3] = first + left * last
    sums_ref[4] = right * last
    last_row_ref[0] = last * inverse
    last_row_ref[1] = left
    last_row_ref[2] = right


def local_z_kernel(second_ref, z_plan_ref, z_ends_ref, t_ref, out_ref):
    chunk = rows_of((LANES, NX), 0)
    for y in range(NB):
        plan = get_plan(z_plan_ref, (y,), ZC)
        b, over = fold_sources(plan, split(second_ref[y]))
        b0 = jnp.where(chunk > 0, b[0] + shift(over, 1, 0), 0.0)
        head = separator_solve([z_ends_ref[y, j] for j in range(2 * len(STRIDES) + 1)], b0)
        following = jnp.where(chunk == LANES - 1, 0.0, shift(head, -1, 0))
        x = jnp.concatenate(unfold(plan, b, head, following), axis=0)
        out_ref[y] = block_row(t_ref, y) + x


def last_kernel(local_ref, spikes_ref, last_row_ref, e0_ref, e1_ref, e2_ref, e3_ref, out_ref, line, ends):
    zg = lax.axis_index("zg")
    for j, e_ref in enumerate((e0_ref, e1_ref, e2_ref, e3_ref)):
        line[lax.bitwise_xor(zg, j)] = e_ref[...]
    inverses, sources = [], []
    leak, source = line[0, 0], line[0, 3]
    for d in range(NZG):
        couple = line[d, 2]
        inverse = 1.0 / (leak + couple)
        inverses.append(inverse)
        sources.append(source)
        if d + 1 < NZG:
            passed = couple * inverse
            leak = line[d + 1, 0] + line[d, 1] + passed * leak
            source = line[d + 1, 3] + line[d, 4] + passed * source
    value = jnp.zeros_like(source)
    ends[NZG] = value
    for d in reversed(range(NZG)):
        value = (sources[d] + line[d, 2] * value) * inverses[d]
        ends[d] = value
    own = ends[zg]
    following = last_row_ref[0] + last_row_ref[1] * own + last_row_ref[2] * ends[zg + 1]
    for y in range(NB):
        x = local_ref[y] + spikes_ref[0, y] * own[y:y + 1] + spikes_ref[1, y] * following[y:y + 1]
        for a, part in enumerate(split(x)):
            out_ref[y, pl.ds(a, LANES, stride=ZC), :] = part


def call(kernel, name, outs, args, scratch=(), cost=2000000, granted=0):
    shapes = [jax.ShapeDtypeStruct(o, jnp.float32) for o in outs]
    vmem = pl.BlockSpec(memory_space=pltpu.VMEM)
    return pl.pallas_call(
        kernel,
        name=name,
        out_shape=shapes,
        in_specs=[pl.BlockSpec(memory_space=pltpu.HBM)] * len(args) if granted else [vmem] * len(args),
        out_specs=[vmem] * len(outs),
        scratch_shapes=scratch,
        cost_estimate=pl.CostEstimate(flops=cost, bytes_accessed=cost, transcendentals=0),
        compiler_params=pltpu.CompilerParams(vmem_limit_bytes=(granted or 24576) * 1024),
    )(*args)


def swapped(x, axis, first):
    pairs = []
    for zg in range(NZG):
        for gy in range(NGY):
            place, count = (zg, NZG) if axis == "zg" else (gy, NGY)
            partner = ((place - first) ^ 1) + first
            if not 0 <= partner < count:
                target = (zg, gy ^ 1) if axis == "zg" else (zg ^ 1, gy)
            else:
                target = (partner, gy) if axis == "zg" else (zg, partner)
            pairs.append((zg * NGY + gy, target[0] * NGY + target[1]))
    return lax.ppermute(x, ("zg", "gy"), pairs)


def crossed(x, axis, by):
    return lax.ppermute(x, axis, [(i, i ^ by) for i in range(lax.axis_size(axis))])


def shards(t, k):
    block = (NB, NZB, NX)
    t, k, across, inside, z_even, z_odd = call(
        load_kernel, "load", [block, block, (2, NZB, NX), (2, NZB, NX), (2, NB, NX), (2, NB, NX)], [t, k],
        scratch=[pltpu.SemaphoreType.DMA((2,))], granted=LOAD_GRANT)
    across = swapped(across, "gy", 1)
    z_odd = swapped(z_odd, "zg", 1)
    z_even = swapped(z_even, "zg", 0)
    inside = swapped(inside, "gy", 0)
    turned = pltpu.VMEM((NB // 2, NX, 2 * NZB), jnp.float32)
    ends = (2 * len(STRIDES) + 1, LANES, NX)
    inner, faces, x_plan, x_ends, z_plan, z_ends, spikes, coeffs = call(
        inner_kernel, "inner",
        [block, (NB - 1, NZB, NX), (NB // 2, XC - 1, 3, LANES, 2 * NZB), (NB // 2,) + ends,
         (NB, ZC - 1, 3, LANES, NX), (NB,) + ends, (2,) + block, (3, NB, NX)], [t, k], scratch=[turned])
    bundle, back, top = call(
        first_kernel, "first", [(NZB * VALUES, NX), (3, NB - 1, NZB, NX), (NB, NX)],
        [t, k, inner, faces, x_plan, x_ends, inside, across, z_odd, z_even], scratch=[turned])
    columns = lax.all_to_all(bundle.reshape(NZB * VALUES, 1, NX), "gy", split_axis=0, concat_axis=0, tiled=True)
    (ends,) = call(column_kernel, "column", [(2 * NGY, NX)], [columns.reshape(NGY * VALUES, NX)])
    ends = lax.all_to_all(ends, "gy", split_axis=0, concat_axis=0, tiled=True)
    second, sums, last_row = call(
        second_kernel, "second", [block, (5, NB, NX), (3, NB, NX)], [ends, back, spikes, coeffs, top])
    sums = [sums] + [crossed(sums, "zg", j) for j in range(1, NZG)]
    (local,) = call(local_z_kernel, "local_z", [block], [second, z_plan, z_ends, t])
    (out,) = call(last_kernel, "last", [block], [local, spikes, last_row] + sums,
                  scratch=[pltpu.VMEM((NZG, 5, NB, NX), jnp.float32), pltpu.VMEM((NZG + 1, NB, NX), jnp.float32)])
    return out


def solution(mesh):
    return jax.shard_map(
        shards,
        mesh=mesh,
        in_specs=(P("gy", "zg", None), P("gy", "zg", None)),
        out_specs=P("gy", "zg", None),
        check_vma=False,
    )
```

```python
import jax
import jax.numpy as jnp
from jax import lax
from jax.experimental import pallas as pl
from jax.experimental.pallas import tpu as pltpu
from jax.sharding import PartitionSpec as P

mesh_courant_number = 300.0

NB, NZB, NX = 4, 64, 128
NGY, NZG = 64, 4
LANES = 8
XC, ZC, YC = NX // LANES, NZB // LANES, NGY // LANES
STRIDES = (1, 2, 4)
VALUES = 5

HALO_GRANT, LOAD_GRANT = 55000, 54940


def face(k, q):
    return (2.0 * mesh_courant_number) * k * q / (k + q)


def shift(v, by, axis):
    return pltpu.roll(v, by % v.shape[axis], axis)


def rows_of(shape, axis):
    return lax.broadcasted_iota(jnp.int32, shape, axis)


def chunked(load, count):
    return jnp.concatenate([load(pl.ds(a, LANES, stride=count)) for a in range(count)], axis=0)


def split(v):
    return [v[LANES * a:LANES * (a + 1)] for a in range(v.shape[0] // LANES)]


def before(v):
    last = v.shape[0] - LANES
    return jnp.concatenate([shift(v[last:], 1, 0), v[:last]], axis=0)


def after(v):
    return jnp.concatenate([v[LANES:], shift(v[:LANES], -1, 0)], axis=0)


def order(count):
    step = 1
    while step < count:
        for a in range(step, count, 2 * step):
            yield a, step
        step *= 2


def fold(leaks, couples, closed=None):
    leaks, couples, plan, over = list(leaks), list(couples), [], 0.0
    count = len(leaks)
    for a, step in order(count):
        low, high = couples[a - step], couples[a]
        inverse = 1.0 / (leaks[a] + low + high)
        left, right = low * inverse, high * inverse
        if closed is not None and a == count - 1:
            inverse = jnp.where(closed, 0.0, inverse)
            left = jnp.where(closed, 0.0, left)
            right = jnp.where(closed, 1.0, right)
        plan.append((inverse, left, right))
        leaks[a - step] = leaks[a - step] + left * leaks[a]
        if a + step < count:
            leaks[a + step] = leaks[a + step] + right * leaks[a]
        else:
            over = over + right * leaks[a]
        couples[a - step] = low * right
    return plan, leaks[0], over, couples[0]


def fold_sources(plan, sources):
    sources, over = list(sources), 0.0
    count = len(sources)
    for (a, step), (_, left, right) in zip(order(count), plan):
        sources[a - step] = sources[a - step] + left * sources[a]
        if a + step < count:
            sources[a + step] = sources[a + step] + right * sources[a]
        else:
            over = over + right * sources[a]
    return sources, over


def unfold(plan, sources, head, following):
    count = len(plan) + 1
    x = [head] + [None] * (count - 1) + [following]
    for (a, step), (inverse, left, right) in reversed(list(zip(order(count), plan))):
        x[a] = left * x[a - step] + right * x[min(a + step, count)]
        if sources is not None:
            x[a] = x[a] + inverse * sources[a]
    return x[:count]


def put_plan(ref, at, plan):
    for i, entries in enumerate(plan):
        for j, entry in enumerate(entries):
            ref[at + (i, j)] = entry


def get_plan(ref, at, count):
    return [tuple(ref[at + (i, j)] for j in range(3)) for i in range(count - 1)]


def separator_factors(leak, low, high):
    factors = []
    for s in STRIDES:
        inverse = 1.0 / (leak + low + high)
        from_low = low * shift(inverse, s, 0)
        from_high = high * shift(inverse, -s, 0)
        factors += [from_low, from_high]
        leak = leak + from_low * shift(leak, s, 0) + from_high * shift(leak, -s, 0)
        low = from_low * shift(low, s, 0)
        high = from_high * shift(high, -s, 0)
    return factors + [1.0 / (leak + low + high)]


def separator_solve(factors, b):
    for j, s in enumerate(STRIDES):
        b = b + factors[2 * j] * shift(b, s, 0) + factors[2 * j + 1] * shift(b, -s, 0)
    return b * factors[2 * len(STRIDES)]


def halo_kernel(t_hbm, k_hbm, across_ref, inside_ref, z_even_ref, z_odd_ref, edges, sems):
    odd = lax.rem(lax.axis_index("gy"), 2)
    upper = lax.rem(lax.axis_index("zg"), 2) == 1
    copies = []
    for j, array in enumerate((t_hbm, k_hbm)):
        moves = (
            (array.at[(1 - odd) * (NB - 1)], inside_ref.at[j]),
            (array.at[odd * (NB - 1)], across_ref.at[j]),
            (array.at[:, pl.ds(0, LANES)], edges.at[j, 0]),
            (array.at[:, pl.ds(NZB - LANES, LANES)], edges.at[j, 1]),
        )
        for n, (source, target) in enumerate(moves):
            copies.append(pltpu.make_async_copy(source, target, sems.at[j, n]))
            copies[-1].start()
    for copy in copies:
        copy.wait()
    for j in range(2):
        for y in range(NB):
            first, last = edges[j, 0, y, :1], edges[j, 1, y, LANES - 1:]
            z_even_ref[j, y:y + 1] = jnp.where(upper, first, last)
            z_odd_ref[j, y:y + 1] = jnp.where(upper, last, first)


def load_kernel(t_hbm, k_hbm, t_ref, k_ref, sems):
    copies = [pltpu.make_async_copy(t_hbm, t_ref, sems.at[0]), pltpu.make_async_copy(k_hbm, k_ref, sems.at[1])]
    for copy in copies:
        copy.start()
    for copy in copies:
        copy.wait()


def block_row(ref, *at):
    return chunked(lambda rows: ref[at + (rows, slice(None))], ZC)


def inner_kernel(t_ref, k_ref, inner_ref, faces_ref, x_plan_ref, x_ends_ref, z_plan_ref, z_ends_ref, spikes_ref,
                 coeffs_ref, turned):
    lane = rows_of((NZB, NX), 1)
    row = rows_of((NZB, NX), 0)
    chunk = rows_of((LANES, NX), 0)
    ts = [block_row(t_ref, y) for y in range(NB)]
    ks = [block_row(k_ref, y) for y in range(NB)]
    flux_y = None
    for y in range(NB):
        k, t = ks[y], ts[y]
        low = jnp.where(lane > 0, face(k, shift(k, 1, 1)), 0.0)
        flux = low * (t - shift(t, 1, 1))
        total = shift(flux, -1, 1) - flux
        face_z = jnp.where(row > 0, face(k, before(k)), 0.0)
        flux = face_z * (t - before(t))
        total = total + (after(flux) - flux)
        if y > 0:
            total = total - flux_y
        if y < NB - 1:
            next_face = face(ks[y + 1], k)
            faces_ref[y] = next_face
            flux_y = next_face * (ts[y + 1] - t)
            total = total + flux_y
        inner_ref[y] = total

        ones = [jnp.ones((LANES, NX), jnp.float32)] * ZC
        plan, leak, over, couple = fold(ones, split(after(face_z)), chunk == LANES - 1)
        put_plan(z_plan_ref, (y,), plan)
        over = shift(over, 1, 0)
        leak_end = over[:1]
        leak = leak + jnp.where(chunk > 0, over, 0.0)
        low = shift(couple, 1, 0)
        at_first = jnp.where(chunk == 1, low, 0.0)
        at_last = jnp.where(chunk == LANES - 1, couple, 0.0)
        factors = separator_factors(leak + at_first + at_last, jnp.where(chunk > 1, low, 0.0),
                                    jnp.where((chunk > 0) & (chunk < LANES - 1), couple, 0.0))
        for j, factor in enumerate(factors):
            z_ends_ref[y, j] = factor
        lam = jnp.where(chunk == 0, 1.0, separator_solve(factors, at_first))
        rho = separator_solve(factors, at_last)
        coeffs_ref[0, y:y + 1] = jnp.sum(lam * leak, axis=0, keepdims=True)
        coeffs_ref[1, y:y + 1] = jnp.sum(rho * leak, axis=0, keepdims=True) + leak_end
        coeffs_ref[2, y:y + 1] = couple[LANES - 1:] * lam[LANES - 1:]
        following = jnp.where(chunk == LANES - 1, 0.0, shift(lam, -1, 0))
        spikes_ref[0, y] = jnp.concatenate(unfold(plan, None, lam, following), axis=0)
        following = jnp.where(chunk == LANES - 1, 1.0, shift(rho, -1, 0))
        spikes_ref[1, y] = jnp.concatenate(unfold(plan, None, rho, following), axis=0)

    for h in range(NB // 2):
        turned[h] = jnp.concatenate(ks[2 * h:2 * h + 2], axis=0).T
        k = block_line(turned, h)
        couples = face(k, after(k))
        couples = jnp.where((rows_of(couples.shape, 0) == NX - 1), 0.0, couples)
        ones = [jnp.ones((LANES, 2 * NZB), jnp.float32)] * XC
        plan, leak, over, couple = fold(ones, split(couples))
        put_plan(x_plan_ref, (h,), plan)
        factors = separator_factors(leak + shift(over, 1, 0), shift(couple, 1, 0), couple)
        for j, factor in enumerate(factors):
            x_ends_ref[h, j] = factor


def block_line(ref, h):
    return chunked(lambda rows: ref[h, rows, :], XC)


def first_kernel(t_ref, k_ref, inner_ref, faces_ref, x_plan_ref, x_ends_ref, inside_ref, across_ref, z_even_ref, z_odd_ref,
                 bundle_ref, back_ref, top_ref, turned):
    gy = lax.axis_index("gy")
    zg = lax.axis_index("zg")
    odd = lax.rem(gy, 2) == 1
    across = [block_row(across_ref, j) for j in range(2)]
    inside = [block_row(inside_ref, j) for j in range(2)]
    yp = [jnp.where(odd, b, a) for a, b in zip(across, inside)]
    yn = [jnp.where(odd, a, b) for a, b in zip(across, inside)]
    upper = lax.rem(zg, 2) == 1
    zp = jnp.where(upper, z_even_ref[...], z_odd_ref[...])
    zn = jnp.where(upper, z_odd_ref[...], z_even_ref[...])
    has_south = jnp.where(gy > 0, 1.0, 0.0)
    has_north = jnp.where(gy < NGY - 1, 1.0, 0.0)
    has_below = jnp.where(zg > 0, 1.0, 0.0)
    has_above = jnp.where(zg < NZG - 1, 1.0, 0.0)
    row = rows_of((NZB, NX), 0)
    sources = []
    g4 = None
    for y in range(NB):
        b = inner_ref[y]
        if y == 0:
            b = b + face(block_row(k_ref, y), yp[1] * has_south) * (yp[0] - block_row(t_ref, y))
        if y == NB - 1:
            g4 = face(block_row(k_ref, y), yn[1] * has_north)
            b = b + g4 * (yn[0] - block_row(t_ref, y))
        k_low, k_high = k_ref[y, :1], k_ref[y, NZB - 1:]
        below = face(k_low, zp[1, y:y + 1] * has_below) * (zp[0, y:y + 1] - t_ref[y, :1])
        top = face(k_high, zn[1, y:y + 1] * has_above)
        top_ref[y:y + 1] = top
        above = top * (zn[0, y:y + 1] - t_ref[y, NZB - 1:])
        b = b + jnp.where(row == 0, below, 0.0) + jnp.where(row == NZB - 1, above, 0.0)
        sources.append(b)
    solved = []
    for h in range(NB // 2):
        turned[h] = jnp.concatenate(sources[2 * h:2 * h + 2], axis=0).T
        plan = get_plan(x_plan_ref, (h,), XC)
        b, over = fold_sources(plan, split(block_line(turned, h)))
        head = separator_solve([x_ends_ref[h, j] for j in range(2 * len(STRIDES) + 1)], b[0] + shift(over, 1, 0))
        for a, x in enumerate(unfold(plan, b, head, shift(head, -1, 0))):
            turned[h, pl.ds(a, LANES, stride=XC), :] = x
        b = turned[h].T
        solved += [b[:NZB], b[NZB:]]
    b0, b1, b2, b3 = solved
    g1, g2, g3 = faces_ref[0], faces_ref[1], faces_ref[2]
    i1 = 1.0 / (1.0 + g1 + g2)
    left, right = g1 * i1, g2 * i1
    source = b0 + left * b1
    b2 = b2 + right * b1
    leak = 1.0 + left
    m2 = 1.0 + right
    a2 = g1 * right
    i2 = 1.0 / (m2 + a2 + g3)
    left, right = a2 * i2, g3 * i2
    source = source + left * b2
    b3 = b3 + right * b2
    leak = leak + left * m2
    m3 = 1.0 + right * m2
    a3 = a2 * right
    i3 = 1.0 / (m3 + a3 + g4)
    left, right = a3 * i3, g4 * i3

    def put(v, x):
        for a, part in enumerate(split(x)):
            bundle_ref[pl.ds(VALUES * a + v, LANES, stride=VALUES * ZC), :] = part

    put(0, leak + left * m3)
    put(1, right * m3)
    put(2, a3 * right)
    put(3, source + left * b3)
    put(4, right * b3)
    beta, lam, rho = b3 * i3, left, right
    back_ref[0, 2], back_ref[1, 2], back_ref[2, 2] = beta, lam, rho
    beta, lam, rho = (b2 + g3 * beta) * i2, (a2 + g3 * lam) * i2, g3 * rho * i2
    back_ref[0, 1], back_ref[1, 1], back_ref[2, 1] = beta, lam, rho
    beta, lam, rho = (b1 + g2 * beta) * i1, (g1 + g2 * lam) * i1, g2 * rho * i1
    back_ref[0, 0], back_ref[1, 0], back_ref[2, 0] = beta, lam, rho


def column_kernel(bundle_ref, out_ref):
    get = lambda v: [bundle_ref[pl.ds(VALUES * a + v, LANES, stride=VALUES * YC), :] for a in range(YC)]
    joined = lambda own, pushed: split(jnp.concatenate(own, axis=0) + before(jnp.concatenate(pushed, axis=0)))
    plan, leak, over, couple = fold(joined(get(0), get(1)), get(2))
    b, over_source = fold_sources(plan, joined(get(3), get(4)))
    factors = separator_factors(leak + shift(over, 1, 0), shift(couple, 1, 0), couple)
    head = separator_solve(factors, b[0] + shift(over_source, 1, 0))
    following = shift(head, -1, 0)
    x = unfold(plan, b, head, following) + [following]
    for a in range(YC):
        out_ref[pl.ds(2 * a, LANES, stride=2 * YC), :] = x[a]
        out_ref[pl.ds(2 * a + 1, LANES, stride=2 * YC), :] = x[a + 1]


def second_kernel(ends_ref, back_ref, spikes_ref, coeffs_ref, top_ref, second_ref, sums_ref, last_row_ref):
    get = lambda v: jnp.concatenate(
        [ends_ref[pl.ds(2 * a + v, LANES, stride=2 * ZC), :] for a in range(ZC)], axis=0)
    own, following = get(0), get(1)
    firsts, lasts = [], []
    for y in range(NB):
        if y == 0:
            u = own
        else:
            u = back_ref[0, y - 1] + back_ref[1, y - 1] * own + back_ref[2, y - 1] * following
        second_ref[y] = u
        firsts.append(jnp.sum(spikes_ref[0, y] * u, axis=0, keepdims=True))
        lasts.append(jnp.sum(spikes_ref[1, y] * u, axis=0, keepdims=True))
    first, last = jnp.concatenate(firsts, axis=0), jnp.concatenate(lasts, axis=0)
    leak, couple, top = coeffs_ref[1], coeffs_ref[2], top_ref[...]
    inverse = 1.0 / (leak + couple + top)
    left, right = couple * inverse, top * inverse
    sums_ref[0] = coeffs_ref[0] + left * leak
    sums_ref[1] = right * leak
    sums_ref[2] = left * top
    sums_ref[3] = first + left * last
    sums_ref[4] = right * last
    last_row_ref[0] = last * inverse
    last_row_ref[1] = left
    last_row_ref[2] = right


def local_z_kernel(second_ref, z_plan_ref, z_ends_ref, t_ref, out_ref):
    chunk = rows_of((LANES, NX), 0)
    for y in range(NB):
        plan = get_plan(z_plan_ref, (y,), ZC)
        b, over = fold_sources(plan, split(second_ref[y]))
        b0 = jnp.where(chunk > 0, b[0] + shift(over, 1, 0), 0.0)
        head = separator_solve([z_ends_ref[y, j] for j in range(2 * len(STRIDES) + 1)], b0)
        following = jnp.where(chunk == LANES - 1, 0.0, shift(head, -1, 0))
        x = jnp.concatenate(unfold(plan, b, head, following), axis=0)
        out_ref[y] = block_row(t_ref, y) + x


def last_kernel(local_ref, spikes_ref, last_row_ref, e0_ref, e1_ref, e2_ref, e3_ref, out_ref, line, ends):
    zg = lax.axis_index("zg")
    for j, e_ref in enumerate((e0_ref, e1_ref, e2_ref, e3_ref)):
        line[lax.bitwise_xor(zg, j)] = e_ref[...]
    inverses, sources = [], []
    leak, source = line[0, 0], line[0, 3]
    for d in range(NZG):
        couple = line[d, 2]
        inverse = 1.0 / (leak + couple)
        inverses.append(inverse)
        sources.append(source)
        if d + 1 < NZG:
            passed = couple * inverse
            leak = line[d + 1, 0] + line[d, 1] + passed * leak
            source = line[d + 1, 3] + line[d, 4] + passed * source
    value = jnp.zeros_like(source)
    ends[NZG] = value
    for d in reversed(range(NZG)):
        value = (sources[d] + line[d, 2] * value) * inverses[d]
        ends[d] = value
    own = ends[zg]
    following = last_row_ref[0] + last_row_ref[1] * own + last_row_ref[2] * ends[zg + 1]
    for y in range(NB):
        x = local_ref[y] + spikes_ref[0, y] * own[y:y + 1] + spikes_ref[1, y] * following[y:y + 1]
        for a, part in enumerate(split(x)):
            out_ref[y, pl.ds(a, LANES, stride=ZC), :] = part


def call(kernel, name, outs, args, scratch=(), cost=2000000, granted=0):
    shapes = [jax.ShapeDtypeStruct(o, jnp.float32) for o in outs]
    vmem = pl.BlockSpec(memory_space=pltpu.VMEM)
    return pl.pallas_call(
        kernel,
        name=name,
        out_shape=shapes,
        in_specs=[pl.BlockSpec(memory_space=pltpu.HBM)] * len(args) if granted else [vmem] * len(args),
        out_specs=[vmem] * len(outs),
        scratch_shapes=scratch,
        cost_estimate=pl.CostEstimate(flops=cost, bytes_accessed=cost, transcendentals=0),
        compiler_params=pltpu.CompilerParams(vmem_limit_bytes=(granted or 24576) * 1024),
    )(*args)


def swapped(x, axis, first):
    pairs = []
    for zg in range(NZG):
        for gy in range(NGY):
            place, count = (zg, NZG) if axis == "zg" else (gy, NGY)
            partner = ((place - first) ^ 1) + first
            if not 0 <= partner < count:
                target = (zg, gy ^ 1) if axis == "zg" else (zg ^ 1, gy)
            else:
                target = (partner, gy) if axis == "zg" else (zg, partner)
            pairs.append((zg * NGY + gy, target[0] * NGY + target[1]))
    return lax.ppermute(x, ("zg", "gy"), pairs)


def crossed(x, axis, by):
    return lax.ppermute(x, axis, [(i, i ^ by) for i in range(lax.axis_size(axis))])


def shards(t, k):
    block = (NB, NZB, NX)
    across, inside, z_even, z_odd = call(
        halo_kernel, "halo", [(2, NZB, NX), (2, NZB, NX), (2, NB, NX), (2, NB, NX)], [t, k],
        scratch=[pltpu.VMEM((2, 2, NB, LANES, NX), jnp.float32), pltpu.SemaphoreType.DMA((2, 4))], granted=HALO_GRANT)
    t, k = call(load_kernel, "load", [block, block], [t, k],
                scratch=[pltpu.SemaphoreType.DMA((2,))], granted=LOAD_GRANT)
    across = swapped(across, "gy", 1)
    z_odd = swapped(z_odd, "zg", 1)
    z_even = swapped(z_even, "zg", 0)
    inside = swapped(inside, "gy", 0)
    turned = pltpu.VMEM((NB // 2, NX, 2 * NZB), jnp.float32)
    ends = (2 * len(STRIDES) + 1, LANES, NX)
    inner, faces, x_plan, x_ends, z_plan, z_ends, spikes, coeffs = call(
        inner_kernel, "inner",
        [block, (NB - 1, NZB, NX), (NB // 2, XC - 1, 3, LANES, 2 * NZB), (NB // 2,) + ends,
         (NB, ZC - 1, 3, LANES, NX), (NB,) + ends, (2,) + block, (3, NB, NX)], [t, k], scratch=[turned])
    bundle, back, top = call(
        first_kernel, "first", [(NZB * VALUES, NX), (3, NB - 1, NZB, NX), (NB, NX)],
        [t, k, inner, faces, x_plan, x_ends, inside, across, z_even, z_odd], scratch=[turned])
    columns = lax.all_to_all(bundle.reshape(NZB * VALUES, 1, NX), "gy", split_axis=0, concat_axis=0, tiled=True)
    (ends,) = call(column_kernel, "column", [(2 * NGY, NX)], [columns.reshape(NGY * VALUES, NX)])
    ends = lax.all_to_all(ends, "gy", split_axis=0, concat_axis=0, tiled=True)
    second, sums, last_row = call(
        second_kernel, "second", [block, (5, NB, NX), (3, NB, NX)], [ends, back, spikes, coeffs, top])
    sums = [sums] + [crossed(sums, "zg", j) for j in range(1, NZG)]
    (local,) = call(local_z_kernel, "local_z", [block], [second, z_plan, z_ends, t])
    (out,) = call(last_kernel, "last", [block], [local, spikes, last_row] + sums,
                  scratch=[pltpu.VMEM((NZG, 5, NB, NX), jnp.float32), pltpu.VMEM((NZG + 1, NB, NX), jnp.float32)])
    return out


def solution(mesh):
    return jax.shard_map(
        shards,
        mesh=mesh,
        in_specs=(P("gy", "zg", None), P("gy", "zg", None)),
        out_specs=P("gy", "zg", None),
        check_vma=False,
    )
```

```python
import jax
import jax.numpy as jnp
from jax import lax
from jax.experimental import pallas as pl
from jax.experimental.pallas import tpu as pltpu
from jax.sharding import PartitionSpec as P

mesh_courant_number = 300.0

NB, NZB, NX = 4, 64, 128
NGY, NZG = 64, 4
LANES = 8
XC, ZC, YC = NX // LANES, NZB // LANES, NGY // LANES
STRIDES = (1, 2, 4)
VALUES = 5

HALO_GRANT, LOAD_GRANT = 55000, 54940


def face(k, q):
    return (2.0 * mesh_courant_number) * k * q / (k + q)


def shift(v, by, axis):
    return pltpu.roll(v, by % v.shape[axis], axis)


def rows_of(shape, axis):
    return lax.broadcasted_iota(jnp.int32, shape, axis)


def chunked(load, count):
    return jnp.concatenate([load(pl.ds(a, LANES, stride=count)) for a in range(count)], axis=0)


def split(v):
    return [v[LANES * a:LANES * (a + 1)] for a in range(v.shape[0] // LANES)]


def before(v):
    last = v.shape[0] - LANES
    return jnp.concatenate([shift(v[last:], 1, 0), v[:last]], axis=0)


def after(v):
    return jnp.concatenate([v[LANES:], shift(v[:LANES], -1, 0)], axis=0)


def order(count):
    step = 1
    while step < count:
        for a in range(step, count, 2 * step):
            yield a, step
        step *= 2


def fold(leaks, couples, closed=None):
    leaks, couples, plan, over = list(leaks), list(couples), [], 0.0
    count = len(leaks)
    for a, step in order(count):
        low, high = couples[a - step], couples[a]
        inverse = 1.0 / (leaks[a] + low + high)
        left, right = low * inverse, high * inverse
        if closed is not None and a == count - 1:
            inverse = jnp.where(closed, 0.0, inverse)
            left = jnp.where(closed, 0.0, left)
            right = jnp.where(closed, 1.0, right)
        plan.append((inverse, left, right))
        leaks[a - step] = leaks[a - step] + left * leaks[a]
        if a + step < count:
            leaks[a + step] = leaks[a + step] + right * leaks[a]
        else:
            over = over + right * leaks[a]
        couples[a - step] = low * right
    return plan, leaks[0], over, couples[0]


def fold_sources(plan, sources):
    sources, over = list(sources), 0.0
    count = len(sources)
    for (a, step), (_, left, right) in zip(order(count), plan):
        sources[a - step] = sources[a - step] + left * sources[a]
        if a + step < count:
            sources[a + step] = sources[a + step] + right * sources[a]
        else:
            over = over + right * sources[a]
    return sources, over


def unfold(plan, sources, head, following):
    count = len(plan) + 1
    x = [head] + [None] * (count - 1) + [following]
    for (a, step), (inverse, left, right) in reversed(list(zip(order(count), plan))):
        x[a] = left * x[a - step] + right * x[min(a + step, count)]
        if sources is not None:
            x[a] = x[a] + inverse * sources[a]
    return x[:count]


def put_plan(ref, at, plan):
    for i, entries in enumerate(plan):
        for j, entry in enumerate(entries):
            ref[at + (i, j)] = entry


def get_plan(ref, at, count):
    return [tuple(ref[at + (i, j)] for j in range(3)) for i in range(count - 1)]


def separator_factors(leak, low, high):
    factors = []
    for s in STRIDES:
        inverse = 1.0 / (leak + low + high)
        from_low = low * shift(inverse, s, 0)
        from_high = high * shift(inverse, -s, 0)
        factors += [from_low, from_high]
        leak = leak + from_low * shift(leak, s, 0) + from_high * shift(leak, -s, 0)
        low = from_low * shift(low, s, 0)
        high = from_high * shift(high, -s, 0)
    return factors + [1.0 / (leak + low + high)]


def separator_solve(factors, b):
    for j, s in enumerate(STRIDES):
        b = b + factors[2 * j] * shift(b, s, 0) + factors[2 * j + 1] * shift(b, -s, 0)
    return b * factors[2 * len(STRIDES)]


def halo_kernel(t_hbm, k_hbm, across_ref, inside_ref, z_even_ref, z_odd_ref, edges, sems):
    odd = lax.rem(lax.axis_index("gy"), 2)
    upper = lax.rem(lax.axis_index("zg"), 2) == 1
    copies = []
    for j, array in enumerate((t_hbm, k_hbm)):
        moves = (
            (array.at[(1 - odd) * (NB - 1)], inside_ref.at[j]),
            (array.at[odd * (NB - 1)], across_ref.at[j]),
            (array.at[:, pl.ds(0, LANES)], edges.at[j, 0]),
            (array.at[:, pl.ds(NZB - LANES, LANES)], edges.at[j, 1]),
        )
        for n, (source, target) in enumerate(moves):
            copies.append(pltpu.make_async_copy(source, target, sems.at[j, n]))
            copies[-1].start()
    for copy in copies:
        copy.wait()
    for j in range(2):
        for y in range(NB):
            first, last = edges[j, 0, y, :1], edges[j, 1, y, LANES - 1:]
            z_even_ref[j, y:y + 1] = jnp.where(upper, first, last)
            z_odd_ref[j, y:y + 1] = jnp.where(upper, last, first)


def load_kernel(t_hbm, k_hbm, t_ref, k_ref, sems):
    copies = [pltpu.make_async_copy(t_hbm, t_ref, sems.at[0]), pltpu.make_async_copy(k_hbm, k_ref, sems.at[1])]
    for copy in copies:
        copy.start()
    for copy in copies:
        copy.wait()


def block_row(ref, *at):
    return chunked(lambda rows: ref[at + (rows, slice(None))], ZC)


def inner_kernel(t_ref, k_ref, inner_ref, y_plan_ref, x_plan_ref, x_ends_ref, z_plan_ref, z_ends_ref, spikes_ref,
                 coeffs_ref, turned):
    lane = rows_of((NZB, NX), 1)
    row = rows_of((NZB, NX), 0)
    chunk = rows_of((LANES, NX), 0)
    ts = [block_row(t_ref, y) for y in range(NB)]
    ks = [block_row(k_ref, y) for y in range(NB)]
    faces = []
    flux_y = None
    for y in range(NB):
        k, t = ks[y], ts[y]
        low = jnp.where(lane > 0, face(k, shift(k, 1, 1)), 0.0)
        flux = low * (t - shift(t, 1, 1))
        total = shift(flux, -1, 1) - flux
        face_z = jnp.where(row > 0, face(k, before(k)), 0.0)
        flux = face_z * (t - before(t))
        total = total + (after(flux) - flux)
        if y > 0:
            total = total - flux_y
        if y < NB - 1:
            next_face = face(ks[y + 1], k)
            faces.append(next_face)
            flux_y = next_face * (ts[y + 1] - t)
            total = total + flux_y
        inner_ref[y] = total

        ones = [jnp.ones((LANES, NX), jnp.float32)] * ZC
        plan, leak, over, couple = fold(ones, split(after(face_z)), chunk == LANES - 1)
        put_plan(z_plan_ref, (y,), plan)
        over = shift(over, 1, 0)
        leak_end = over[:1]
        leak = leak + jnp.where(chunk > 0, over, 0.0)
        low = shift(couple, 1, 0)
        at_first = jnp.where(chunk == 1, low, 0.0)
        at_last = jnp.where(chunk == LANES - 1, couple, 0.0)
        factors = separator_factors(leak + at_first + at_last, jnp.where(chunk > 1, low, 0.0),
                                    jnp.where((chunk > 0) & (chunk < LANES - 1), couple, 0.0))
        for j, factor in enumerate(factors):
            z_ends_ref[y, j] = factor
        lam = jnp.where(chunk == 0, 1.0, separator_solve(factors, at_first))
        rho = separator_solve(factors, at_last)
        coeffs_ref[0, y:y + 1] = jnp.sum(lam * leak, axis=0, keepdims=True)
        coeffs_ref[1, y:y + 1] = jnp.sum(rho * leak, axis=0, keepdims=True) + leak_end
        coeffs_ref[2, y:y + 1] = couple[LANES - 1:] * lam[LANES - 1:]
        following = jnp.where(chunk == LANES - 1, 0.0, shift(lam, -1, 0))
        spikes_ref[0, y] = jnp.concatenate(unfold(plan, None, lam, following), axis=0)
        following = jnp.where(chunk == LANES - 1, 1.0, shift(rho, -1, 0))
        spikes_ref[1, y] = jnp.concatenate(unfold(plan, None, rho, following), axis=0)

    g1, g2, g3 = faces
    i1 = 1.0 / (1.0 + g1 + g2)
    left1, right1 = g1 * i1, g2 * i1
    m2 = 1.0 + right1
    a2 = g1 * right1
    i2 = 1.0 / (m2 + a2 + g3)
    left2, right2 = a2 * i2, g3 * i2
    y_plan = (i1, left1, right1, i2, left2, right2, 1.0 + left1 + left2 * m2, 1.0 + right2 * m2, a2 * right2)
    for j, entry in enumerate(y_plan):
        y_plan_ref[j] = entry

    for h in range(NB // 2):
        turned[h] = jnp.concatenate(ks[2 * h:2 * h + 2], axis=0).T
        k = block_line(turned, h)
        couples = face(k, after(k))
        couples = jnp.where((rows_of(couples.shape, 0) == NX - 1), 0.0, couples)
        ones = [jnp.ones((LANES, 2 * NZB), jnp.float32)] * XC
        plan, leak, over, couple = fold(ones, split(couples))
        put_plan(x_plan_ref, (h,), plan)
        factors = separator_factors(leak + shift(over, 1, 0), shift(couple, 1, 0), couple)
        for j, factor in enumerate(factors):
            x_ends_ref[h, j] = factor


def block_line(ref, h):
    return chunked(lambda rows: ref[h, rows, :], XC)


def first_kernel(t_ref, k_ref, inner_ref, y_plan_ref, x_plan_ref, x_ends_ref, inside_ref, across_ref, z_even_ref, z_odd_ref,
                 bundle_ref, back_ref, top_ref, turned):
    gy = lax.axis_index("gy")
    zg = lax.axis_index("zg")
    odd = lax.rem(gy, 2) == 1
    across = [block_row(across_ref, j) for j in range(2)]
    inside = [block_row(inside_ref, j) for j in range(2)]
    yp = [jnp.where(odd, b, a) for a, b in zip(across, inside)]
    yn = [jnp.where(odd, a, b) for a, b in zip(across, inside)]
    upper = lax.rem(zg, 2) == 1
    zp = jnp.where(upper, z_even_ref[...], z_odd_ref[...])
    zn = jnp.where(upper, z_odd_ref[...], z_even_ref[...])
    has_south = jnp.where(gy > 0, 1.0, 0.0)
    has_north = jnp.where(gy < NGY - 1, 1.0, 0.0)
    has_below = jnp.where(zg > 0, 1.0, 0.0)
    has_above = jnp.where(zg < NZG - 1, 1.0, 0.0)
    row = rows_of((NZB, NX), 0)
    sources = []
    g4 = None
    for y in range(NB):
        b = inner_ref[y]
        if y == 0:
            b = b + face(block_row(k_ref, y), yp[1] * has_south) * (yp[0] - block_row(t_ref, y))
        if y == NB - 1:
            g4 = face(block_row(k_ref, y), yn[1] * has_north)
            b = b + g4 * (yn[0] - block_row(t_ref, y))
        k_low, k_high = k_ref[y, :1], k_ref[y, NZB - 1:]
        below = face(k_low, zp[1, y:y + 1] * has_below) * (zp[0, y:y + 1] - t_ref[y, :1])
        top = face(k_high, zn[1, y:y + 1] * has_above)
        top_ref[y:y + 1] = top
        above = top * (zn[0, y:y + 1] - t_ref[y, NZB - 1:])
        b = b + jnp.where(row == 0, below, 0.0) + jnp.where(row == NZB - 1, above, 0.0)
        sources.append(b)
    solved = []
    for h in range(NB // 2):
        turned[h] = jnp.concatenate(sources[2 * h:2 * h + 2], axis=0).T
        plan = get_plan(x_plan_ref, (h,), XC)
        b, over = fold_sources(plan, split(block_line(turned, h)))
        head = separator_solve([x_ends_ref[h, j] for j in range(2 * len(STRIDES) + 1)], b[0] + shift(over, 1, 0))
        for a, x in enumerate(unfold(plan, b, head, shift(head, -1, 0))):
            turned[h, pl.ds(a, LANES, stride=XC), :] = x
        b = turned[h].T
        solved += [b[:NZB], b[NZB:]]
    b0, b1, b2, b3 = solved
    i1, left1, right1, i2, left2, right2, leak, m3, a3 = [y_plan_ref[j] for j in range(9)]
    source = b0 + left1 * b1
    b2 = b2 + right1 * b1
    source = source + left2 * b2
    b3 = b3 + right2 * b2
    i3 = 1.0 / (m3 + a3 + g4)
    left, right = a3 * i3, g4 * i3

    def put(v, x):
        for a, part in enumerate(split(x)):
            bundle_ref[pl.ds(VALUES * a + v, LANES, stride=VALUES * ZC), :] = part

    put(0, leak + left * m3)
    put(1, right * m3)
    put(2, a3 * right)
    put(3, source + left * b3)
    put(4, right * b3)
    beta, lam, rho = b3 * i3, left, right
    back_ref[0, 2], back_ref[1, 2], back_ref[2, 2] = beta, lam, rho
    beta, lam, rho = b2 * i2 + right2 * beta, left2 + right2 * lam, right2 * rho
    back_ref[0, 1], back_ref[1, 1], back_ref[2, 1] = beta, lam, rho
    beta, lam, rho = b1 * i1 + right1 * beta, left1 + right1 * lam, right1 * rho
    back_ref[0, 0], back_ref[1, 0], back_ref[2, 0] = beta, lam, rho


def column_kernel(bundle_ref, out_ref):
    get = lambda v: [bundle_ref[pl.ds(VALUES * a + v, LANES, stride=VALUES * YC), :] for a in range(YC)]
    joined = lambda own, pushed: split(jnp.concatenate(own, axis=0) + before(jnp.concatenate(pushed, axis=0)))
    plan, leak, over, couple = fold(joined(get(0), get(1)), get(2))
    b, over_source = fold_sources(plan, joined(get(3), get(4)))
    factors = separator_factors(leak + shift(over, 1, 0), shift(couple, 1, 0), couple)
    head = separator_solve(factors, b[0] + shift(over_source, 1, 0))
    following = shift(head, -1, 0)
    x = unfold(plan, b, head, following) + [following]
    for a in range(YC):
        out_ref[pl.ds(2 * a, LANES, stride=2 * YC), :] = x[a]
        out_ref[pl.ds(2 * a + 1, LANES, stride=2 * YC), :] = x[a + 1]


def second_kernel(ends_ref, back_ref, spikes_ref, coeffs_ref, top_ref, second_ref, sums_ref, last_row_ref):
    get = lambda v: jnp.concatenate(
        [ends_ref[pl.ds(2 * a + v, LANES, stride=2 * ZC), :] for a in range(ZC)], axis=0)
    own, following = get(0), get(1)
    firsts, lasts = [], []
    for y in range(NB):
        if y == 0:
            u = own
        else:
            u = back_ref[0, y - 1] + back_ref[1, y - 1] * own + back_ref[2, y - 1] * following
        second_ref[y] = u
        firsts.append(jnp.sum(spikes_ref[0, y] * u, axis=0, keepdims=True))
        lasts.append(jnp.sum(spikes_ref[1, y] * u, axis=0, keepdims=True))
    first, last = jnp.concatenate(firsts, axis=0), jnp.concatenate(lasts, axis=0)
    leak, couple, top = coeffs_ref[1], coeffs_ref[2], top_ref[...]
    inverse = 1.0 / (leak + couple + top)
    left, right = couple * inverse, top * inverse
    sums_ref[0] = coeffs_ref[0] + left * leak
    sums_ref[1] = right * leak
    sums_ref[2] = left * top
    sums_ref[3] = first + left * last
    sums_ref[4] = right * last
    last_row_ref[0] = last * inverse
    last_row_ref[1] = left
    last_row_ref[2] = right


def local_z_kernel(second_ref, z_plan_ref, z_ends_ref, t_ref, out_ref):
    chunk = rows_of((LANES, NX), 0)
    for y in range(NB):
        plan = get_plan(z_plan_ref, (y,), ZC)
        b, over = fold_sources(plan, split(second_ref[y]))
        b0 = jnp.where(chunk > 0, b[0] + shift(over, 1, 0), 0.0)
        head = separator_solve([z_ends_ref[y, j] for j in range(2 * len(STRIDES) + 1)], b0)
        following = jnp.where(chunk == LANES - 1, 0.0, shift(head, -1, 0))
        x = jnp.concatenate(unfold(plan, b, head, following), axis=0)
        out_ref[y] = block_row(t_ref, y) + x


def last_kernel(local_ref, spikes_ref, last_row_ref, e0_ref, e1_ref, e2_ref, e3_ref, out_ref, line, ends):
    zg = lax.axis_index("zg")
    for j, e_ref in enumerate((e0_ref, e1_ref, e2_ref, e3_ref)):
        line[lax.bitwise_xor(zg, j)] = e_ref[...]
    inverses, sources = [], []
    leak, source = line[0, 0], line[0, 3]
    for d in range(NZG):
        couple = line[d, 2]
        inverse = 1.0 / (leak + couple)
        inverses.append(inverse)
        sources.append(source)
        if d + 1 < NZG:
            passed = couple * inverse
            leak = line[d + 1, 0] + line[d, 1] + passed * leak
            source = line[d + 1, 3] + line[d, 4] + passed * source
    value = jnp.zeros_like(source)
    ends[NZG] = value
    for d in reversed(range(NZG)):
        value = (sources[d] + line[d, 2] * value) * inverses[d]
        ends[d] = value
    own = ends[zg]
    following = last_row_ref[0] + last_row_ref[1] * own + last_row_ref[2] * ends[zg + 1]
    for y in range(NB):
        x = local_ref[y] + spikes_ref[0, y] * own[y:y + 1] + spikes_ref[1, y] * following[y:y + 1]
        for a, part in enumerate(split(x)):
            out_ref[y, pl.ds(a, LANES, stride=ZC), :] = part


def call(kernel, name, outs, args, scratch=(), cost=2000000, granted=0):
    shapes = [jax.ShapeDtypeStruct(o, jnp.float32) for o in outs]
    vmem = pl.BlockSpec(memory_space=pltpu.VMEM)
    return pl.pallas_call(
        kernel,
        name=name,
        out_shape=shapes,
        in_specs=[pl.BlockSpec(memory_space=pltpu.HBM)] * len(args) if granted else [vmem] * len(args),
        out_specs=[vmem] * len(outs),
        scratch_shapes=scratch,
        cost_estimate=pl.CostEstimate(flops=cost, bytes_accessed=cost, transcendentals=0),
        compiler_params=pltpu.CompilerParams(vmem_limit_bytes=(granted or 24576) * 1024),
    )(*args)


def swapped(x, axis, first):
    pairs = []
    for zg in range(NZG):
        for gy in range(NGY):
            place, count = (zg, NZG) if axis == "zg" else (gy, NGY)
            partner = ((place - first) ^ 1) + first
            if not 0 <= partner < count:
                target = (zg, gy ^ 1) if axis == "zg" else (zg ^ 1, gy)
            else:
                target = (partner, gy) if axis == "zg" else (zg, partner)
            pairs.append((zg * NGY + gy, target[0] * NGY + target[1]))
    return lax.ppermute(x, ("zg", "gy"), pairs)


def crossed(x, axis, by):
    return lax.ppermute(x, axis, [(i, i ^ by) for i in range(lax.axis_size(axis))])


def shards(t, k):
    block = (NB, NZB, NX)
    across, inside, z_even, z_odd = call(
        halo_kernel, "halo", [(2, NZB, NX), (2, NZB, NX), (2, NB, NX), (2, NB, NX)], [t, k],
        scratch=[pltpu.VMEM((2, 2, NB, LANES, NX), jnp.float32), pltpu.SemaphoreType.DMA((2, 4))], granted=HALO_GRANT)
    t, k = call(load_kernel, "load", [block, block], [t, k],
                scratch=[pltpu.SemaphoreType.DMA((2,))], granted=LOAD_GRANT)
    across = swapped(across, "gy", 1)
    z_odd = swapped(z_odd, "zg", 1)
    z_even = swapped(z_even, "zg", 0)
    inside = swapped(inside, "gy", 0)
    turned = pltpu.VMEM((NB // 2, NX, 2 * NZB), jnp.float32)
    ends = (2 * len(STRIDES) + 1, LANES, NX)
    inner, y_plan, x_plan, x_ends, z_plan, z_ends, spikes, coeffs = call(
        inner_kernel, "inner",
        [block, (9, NZB, NX), (NB // 2, XC - 1, 3, LANES, 2 * NZB), (NB // 2,) + ends,
         (NB, ZC - 1, 3, LANES, NX), (NB,) + ends, (2,) + block, (3, NB, NX)], [t, k], scratch=[turned])
    bundle, back, top = call(
        first_kernel, "first", [(NZB * VALUES, NX), (3, NB - 1, NZB, NX), (NB, NX)],
        [t, k, inner, y_plan, x_plan, x_ends, inside, across, z_even, z_odd], scratch=[turned])
    columns = lax.all_to_all(bundle.reshape(NZB * VALUES, 1, NX), "gy", split_axis=0, concat_axis=0, tiled=True)
    (ends,) = call(column_kernel, "column", [(2 * NGY, NX)], [columns.reshape(NGY * VALUES, NX)])
    ends = lax.all_to_all(ends, "gy", split_axis=0, concat_axis=0, tiled=True)
    second, sums, last_row = call(
        second_kernel, "second", [block, (5, NB, NX), (3, NB, NX)], [ends, back, spikes, coeffs, top])
    sums = [sums] + [crossed(sums, "zg", j) for j in range(1, NZG)]
    (local,) = call(local_z_kernel, "local_z", [block], [second, z_plan, z_ends, t])
    (out,) = call(last_kernel, "last", [block], [local, spikes, last_row] + sums,
                  scratch=[pltpu.VMEM((NZG, 5, NB, NX), jnp.float32), pltpu.VMEM((NZG + 1, NB, NX), jnp.float32)])
    return out


def solution(mesh):
    return jax.shard_map(
        shards,
        mesh=mesh,
        in_specs=(P("gy", "zg", None), P("gy", "zg", None)),
        out_specs=P("gy", "zg", None),
        check_vma=False,
    )
```
